32 devices in a mesh: dp: 8 (over z, y), fsdp: 4 (over x, core).
Axes of the slice: x: 2, y: 2, z: 4, core: 2. Of those that a mesh axis runs over, the one named last changes fastest.
Arguments:
- tokens: bfloat16 [4, 32, 1024, 512], P('fsdp', 'dp'), may hold values from -6 to 6
- segment_ids: int32 [4, 32, 1024], P('fsdp', 'dp'), may hold values from 0 to 3, never falling along the last dimension, each value on 1 to 512 neighbouring positions
- pad_tokens: int32 [4, 32], P('fsdp'), may hold values from 0 to 256, as said below
- cotangent: bfloat16 [4, 32, 1024, 512], P('fsdp', 'dp'), may hold values from -6 to 6
- project_in: bfloat16 [512, 1536], P(('dp', 'fsdp')), may hold values from -0.25 to 0.25
- project_out: bfloat16 [512, 512], P(('dp', 'fsdp')), may hold values from -2 to 2
- router_weight: bfloat16 [512, 4], P(('dp', 'fsdp')), may hold values from -0.125 to 0.125
- expert_in: bfloat16 [4, 512, 2048], P('fsdp', None, 'dp'), may hold values from -0.5 to 0.5
- expert_out: bfloat16 [4, 2048, 512], P('fsdp', 'dp'), may hold values from -0.125 to 0.125
- first_gain: bfloat16 [512], P(('dp', 'fsdp')), may hold values from 0.099609375 to 1.8984375
- first_bias: bfloat16 [512], P(('dp', 'fsdp')), may hold values from -0.5 to 0.5
- second_gain: bfloat16 [512], P(('dp', 'fsdp')), may hold values from 0.099609375 to 1.8984375
- second_bias: bfloat16 [512], P(('dp', 'fsdp')), may hold values from -0.5 to 0.5
Outputs:
- layer_output: bfloat16 [4, 32, 1024, 512], P('fsdp', 'dp')
- tokens_grad: float32 [4, 32, 1024, 512], P('fsdp', 'dp')
- project_in_grad: float32 [512, 1536], P(('dp', 'fsdp'))
- project_out_grad: float32 [512, 512], P(('dp', 'fsdp'))
- router_grad: float32 [512, 4], P(('dp', 'fsdp'))
- expert_in_grad: float32 [4, 512, 2048], P('fsdp', None, 'dp')
- expert_out_grad: float32 [4, 2048, 512], P('fsdp', 'dp')
- first_gain_grad: float32 [512], P(('dp', 'fsdp'))
- first_bias_grad: float32 [512], P(('dp', 'fsdp'))
- second_gain_grad: float32 [512], P(('dp', 'fsdp'))
- second_bias_grad: float32 [512], P(('dp', 'fsdp'))
The draws below stay inside these ranges and needn't reach their ends.
Inputs may be any that keep to these rules, and one draw needn't show every extreme that they name: `pad_tokens`: in each of the 4 blocks some row of the group has no padding.
All inputs are finite; a program needn't handle non-finite values.
Results may differ from the reference program's by a relative error of at most 0.018.
Values may be sent and summed in bfloat16 or wider, within the bound.
No kernel may reach another device: no remote copies, remote signals or barrier semaphores. Data moves between devices by JAX's collectives and lax.ppermute only.
A program may use at most 256 MiB of HBM per device.

```python
import math
import jax
import jax.numpy as jnp
import numpy as np
from jax import lax

D = 512
HEAD_DIM = 64
FFX = 2048
GROUP = 32
LEN = 1024
DOCS = 4
EXPERTS = 4
BLOCKS = 4


def draw_pad_tokens(key, part):
    key = jax.random.fold_in(key, 7)
    key_counts, key_orders = jax.random.split(key)
    counts = jax.random.randint(key_counts, (BLOCKS, GROUP), 0, LEN // 4 + 1)
    orders = jax.vmap(lambda subkey: jax.random.permutation(subkey, GROUP))(jax.random.split(key_orders, BLOCKS))
    counts = jnp.where(orders == 0, 0, counts)
    counts = jnp.where(orders == 1, LEN // 4, counts)
    return counts.astype(jnp.int32)


def level_of(key, extent, cuts, least, largest):
    factor_of = 1.0
    for dim, blocks in cuts:
        steps = jax.random.uniform(jax.random.fold_in(jax.random.fold_in(key, 6), dim), (blocks,), jnp.float32, least / len(cuts), largest / len(cuts))
        factor_of = factor_of * jnp.repeat(jnp.exp(steps), extent[dim] // blocks).reshape((-1,) + (1,) * (len(extent) - 1 - dim))
    return factor_of


def split_up(amount, total, most, slope):
    loads = [(1 << 20) // math.isqrt(grade ** slope) + 1 for grade in range(2, amount + 1)]
    rest, given = total - most - (amount - 1), [1] * (amount - 1)
    while rest > 0:
        free = [i for i in range(amount - 1) if given[i] < most]
        mass, remaining = sum([loads[i] for i in free]), rest
        for i in free:
            addition = min(most - given[i], max(1, remaining * loads[i] // mass), rest)
            given[i] = given[i] + addition
            rest = rest - addition
    return np.array([most] + given)


def uneven(key, number_of, total, bound, lean):
    if number_of == 2:
        one = jax.random.randint(key, (), max(1, total - bound), min(bound, total - 1) + 1)
        return jnp.stack([one, total - one])
    sizes = jnp.asarray(split_up(number_of, total, bound, lean), jnp.int32)
    twos = (number_of - 1) // 2
    donor, receiver = sizes[1:1 + 2 * twos:2], sizes[2:2 + 2 * twos:2]
    slack = jnp.minimum(donor - 1, bound - receiver)
    shifted = jax.random.randint(jax.random.fold_in(key, 1), (twos,), 0, 1 << 20) % (slack + 1)
    sizes = sizes.at[1:1 + 2 * twos:2].set(donor - shifted).at[2:2 + 2 * twos:2].set(receiver + shifted)
    return sizes[jax.random.permutation(jax.random.fold_in(key, 2), number_of)]


def noise(key, extent, scale, reach, shards=(), dtype=jnp.bfloat16):
    level = level_of(key, extent, shards, -0.22, 0.18) if shards else 1.0
    values = jax.random.normal(key, extent, jnp.float32) * scale * level
    return jnp.minimum(jnp.maximum(values, -reach), reach).astype(dtype)


def setup_inputs(seed: int = 0) -> dict:
    key_list = jax.random.split(jax.random.key(seed), 14)
    return {
        "tokens": noise(key_list[0], (BLOCKS, GROUP, LEN, D), 1.0, 6.0, ((0, 4), (1, 8))),
        "segment_ids": jax.vmap(lambda own: jnp.searchsorted(jnp.cumsum(uneven(own, DOCS, LEN, LEN // 2, 2)), jnp.arange(LEN), side="right"))(jax.random.split(key_list[1], BLOCKS * GROUP)).reshape((BLOCKS, GROUP, LEN)).astype(jnp.int32),
        "pad_tokens": draw_pad_tokens(jax.random.fold_in(key_list[13], 71), 0),
        "cotangent": noise(key_list[3], (BLOCKS, GROUP, LEN, D), 1.0, 6.0, ((0, 4), (1, 8))),
        "project_in": noise(key_list[4], (D, 3 * D), D ** -0.5, 0.25, ((0, 32),)),
        "project_out": noise(key_list[5], (D, D), (D * DOCS * 4 // LEN) ** -0.5, 2.0, ((0, 32),)),
        "router_weight": noise(key_list[6], (D, EXPERTS), (4 * D) ** -0.5, 0.125, ((0, 32),)),
        "expert_in": noise(key_list[7], (EXPERTS, D, FFX), (D // 4) ** -0.5, 0.5, ((0, 4), (2, 8))),
        "expert_out": noise(key_list[8], (EXPERTS, FFX, D), FFX ** -0.5, 0.125, ((0, 4), (1, 8))),
        "first_gain": jnp.clip(1.0 + 0.18 * jax.random.normal(key_list[9], (D,), jnp.float32), 0.099609375, 1.8984375).astype(jnp.bfloat16),
        "first_bias": noise(key_list[10], (D,), 0.1, 0.5, ((0, 32),)),
        "second_gain": jnp.clip(1.0 + 0.18 * jax.random.normal(key_list[11], (D,), jnp.float32), 0.099609375, 1.8984375).astype(jnp.bfloat16),
        "second_bias": noise(key_list[12], (D,), 0.1, 0.5, ((0, 32),)),
    }


HIGHEST = lax.Precision.HIGHEST
NEGATIVE = -1e+30

@jax.custom_vjp
def low(v):
    return lax.optimization_barrier(v.astype(jnp.bfloat16)).astype(jnp.float32)

@jax.custom_vjp
def low_back(v):
    return v

def low_keep(v):
    return (low(v), None)

def low_pass(kept, grad):
    return (grad,)

def back_keep(v):
    return (v, None)

def back_low(kept, grad):
    return (low(grad),)
low.defvjp(low_keep, low_pass)
low_back.defvjp(back_keep, back_low)

def layer_norm(values, gain_vec, shift_vec):
    centred = values - lax.optimization_barrier(jnp.mean(values, axis=-1, keepdims=True))
    spread = lax.optimization_barrier(jnp.mean(centred * centred, axis=-1, keepdims=True))
    return centred * lax.rsqrt(spread + 1e-05) * gain_vec + shift_vec

def activate(values):
    return jax.nn.gelu(values, approximate=True)

def allowed_pairs(seg_row, valid_row):
    places = jnp.arange(seg_row.shape[0])
    same_doc = seg_row[:, None] == seg_row[None, :]
    earlier = places[None, :] <= places[:, None]
    return same_doc & earlier & valid_row[None, :] | (places[None, :] == places[:, None])

def attend_row(query_row, key_row, value_row, seg_row, valid_row):
    length = query_row.shape[0]
    head_count = query_row.shape[1] // HEAD_DIM
    query_heads = query_row.reshape(length, head_count, HEAD_DIM)
    key_heads = key_row.reshape(length, head_count, HEAD_DIM)
    value_heads = value_row.reshape(length, head_count, HEAD_DIM)
    scores = low_back(jnp.einsum('qhd,khd->hqk', query_heads, key_heads, precision=HIGHEST) * (1.0 / math.sqrt(HEAD_DIM)))
    scores = jnp.where(allowed_pairs(seg_row, valid_row)[None], scores, NEGATIVE)
    highest = lax.optimization_barrier(jnp.max(scores, axis=-1, keepdims=True))
    raised = jnp.exp(scores - highest)
    attn_prob = low(raised / lax.optimization_barrier(jnp.sum(raised, axis=-1, keepdims=True)))
    return jnp.einsum('hqk,khd->qhd', attn_prob, value_heads, precision=HIGHEST).reshape(length, head_count * HEAD_DIM)

def block_forward(inputs, segments, padded, project_in, project_out, router_weight, expert_in, expert_out, first_gain, first_bias, second_gain, second_bias):
    length = inputs.shape[1]
    valid = jnp.arange(length)[None, :] < (length - padded)[:, None]
    normed = low(layer_norm(inputs, first_gain, first_bias))
    joined = jnp.einsum('gld,de->gle', normed, project_in, precision=HIGHEST)
    query_all = low(low_back(joined[..., :D]))
    key_all = low(low_back(joined[..., D:2 * D]))
    value_all = low(low_back(joined[..., 2 * D:]))
    attend = jax.checkpoint(attend_row)
    attended = lax.map(lambda packed: attend(*packed), (query_all, key_all, value_all, segments, valid))
    attended = low(low_back(attended))
    branch = low_back(jnp.einsum('gld,de->gle', attended, project_out, precision=HIGHEST))
    hidden = inputs + branch
    mixed_in = low(low_back(layer_norm(hidden, second_gain, second_bias)))
    logits = low_back(jnp.einsum('gld,de->gle', mixed_in, router_weight, precision=HIGHEST))
    keep_mask = valid[..., None]
    highest = lax.optimization_barrier(jnp.max(jnp.where(keep_mask, logits, NEGATIVE), axis=0, keepdims=True))
    raised = jnp.exp(jnp.where(keep_mask, logits - highest, NEGATIVE))
    gate_low = low(low_back(raised / lax.optimization_barrier(jnp.sum(raised, axis=0, keepdims=True))))
    pooled = low(low_back(jnp.einsum('gle,gld->led', gate_low, mixed_in, precision=HIGHEST)))
    pre_act = low_back(jnp.einsum('led,edf->lef', pooled, expert_in, precision=HIGHEST))
    act_low = low(activate(pre_act))
    result = low(low_back(jnp.einsum('lef,efd->led', act_low, expert_out, precision=HIGHEST)))
    spread = low(GROUP * jnp.einsum('gle,led->gld', gate_low, result, precision=HIGHEST))
    return hidden + spread

def reference(tokens, segment_ids, pad_tokens, cotangent, project_in, project_out, router_weight, expert_in, expert_out, first_gain, first_bias, second_gain, second_bias):
    params = tuple((weight.astype(jnp.float32) for weight in (project_in, project_out, router_weight, expert_in, expert_out, first_gain, first_bias, second_gain, second_bias)))

    def one_block(running, packed):
        inputs, segments, padded, cot_block = packed

        def forward(inputs32, *weights):
            return block_forward(inputs32, segments, padded, *weights)
        output, pullback = jax.vjp(forward, inputs.astype(jnp.float32), *params)
        gradients = pullback(cot_block.astype(jnp.float32))
        running = tuple((total + grad for total, grad in zip(running, gradients[1:])))
        return (running, (output.astype(jnp.bfloat16), gradients[0]))
    initial = tuple((jnp.zeros(weight.shape, jnp.float32) for weight in params))
    totals, (layer_output, tokens_grad) = lax.scan(one_block, initial, (tokens, segment_ids, pad_tokens, cotangent))
    return (layer_output, tokens_grad, totals[0], totals[1], totals[2], totals[3], totals[4], totals[5], totals[6], totals[7], totals[8])
```

```python
import functools, math
import jax, jax.numpy as jnp
from jax import lax
from jax.experimental import pallas as pl
from jax.experimental.pallas import tpu as pltpu
from jax.sharding import PartitionSpec as P

NEGATIVE = -1e30
QB = 128
F32 = jnp.float32
BF16 = jnp.bfloat16
NT = (((1,), (1,)), ((), ()))
TN = (((0,), (0,)), ((), ()))


def dot(a, b):
    return jnp.dot(a, b, preferred_element_type=F32)


def dot_nt(a, b):
    return lax.dot_general(a, b, NT, preferred_element_type=F32)


def dot_tn(a, b):
    return lax.dot_general(a, b, TN, preferred_element_type=F32)


def iota(shape, axis):
    return lax.broadcasted_iota(jnp.int32, shape, axis)


def split_heads(x):
    low = iota(x.shape, 1) < 64
    zero = jnp.zeros_like(x)
    return jnp.concatenate([jnp.where(low, x, zero), jnp.where(low, zero, x)], axis=0)


def join_heads(x):
    half = x.shape[0] // 2
    low = iota((half, x.shape[1]), 1) < 64
    return jnp.where(low, x[:half], x[half:])


def attn_fwd_kernel(width, begin, count, lo_ref, vlen_ref, start_ref, joined_ref, out_ref, bias_ref):
    row = pl.program_id(0)
    vlen = vlen_ref[row]

    def block(step, _):
        qb = step + begin
        lo = lo_ref[row, qb]
        base = pl.multiple_of(qb * QB, QB)
        first = pl.multiple_of(lo * QB, QB)
        own = pl.ds(base, QB)
        target = pl.ds(pl.multiple_of(step * QB, QB), QB)

        def variant(blocks):
            span = blocks * QB
            keys = pl.ds(first, span)
            begins = jnp.broadcast_to(start_ref[0, pl.ds(qb, 1), :], (QB, QB)).T
            i = base + iota((QB, QB), 0)
            for b in range(blocks):
                j = first + b * QB + iota((QB, QB), 1)
                ok = ((j >= begins) & (j <= i) & (j < vlen)) | (j == i)
                bias_ref[:, b * QB:(b + 1) * QB] = jnp.where(ok, 0.0, NEGATIVE)
            bias = bias_ref[:, :span]
            bias = jnp.concatenate([bias, bias], axis=0)
            at = [pl.ds(lane, 128) for lane in range(0, width, 128)]
            key_at = [pl.ds(width + lane, 128) for lane in range(0, width, 128)]
            value_at = [pl.ds(2 * width + lane, 128) for lane in range(0, width, 128)]
            query = [split_heads(joined_ref[0, own, lanes] * jnp.asarray(0.125, BF16)) for lanes in at]
            scores = [dot_nt(q, joined_ref[0, keys, lanes]) for q, lanes in zip(query, key_at)]
            scores = [s + bias for s in scores]
            tops = [jnp.max(s, axis=1, keepdims=True) for s in scores]
            raised = [jnp.exp(s - top) for s, top in zip(scores, tops)]
            totals = [jnp.sum(p, axis=1, keepdims=True) for p in raised]
            out = [dot(p.astype(BF16), joined_ref[0, keys, lanes]) for p, lanes in zip(raised, value_at)]
            for o, total, lanes in zip(out, totals, at):
                out_ref[0, target, lanes] = join_heads(o * (1.0 / total)).astype(BF16)

        for blocks in range(1, 6):
            pl.when(qb - lo + 1 == blocks)(functools.partial(variant, blocks))
        return 0

    lax.fori_loop(0, count, block, 0)


def attn_fwd(joined, starts, lows, vlens, begin, count):
    rows, length, triple = joined.shape
    width = triple // 3
    spec = pltpu.PrefetchScalarGridSpec(
        num_scalar_prefetch=2,
        grid=(rows,),
        in_specs=[
            pl.BlockSpec((1, length // QB, QB), lambda r, *_: (r, 0, 0)),
            pl.BlockSpec((1, length, triple), lambda r, *_: (r, 0, 0)),
        ],
        out_specs=pl.BlockSpec((1, count * QB, width), lambda r, *_: (r, 0, 0)),
        scratch_shapes=[pltpu.VMEM((QB, 5 * QB), F32)],
    )
    return pl.pallas_call(
        functools.partial(attn_fwd_kernel, width, begin, count),
        grid_spec=spec,
        out_shape=jax.ShapeDtypeStruct((rows, count * QB, width), BF16),
        compiler_params=pltpu.CompilerParams(vmem_limit_bytes=48 << 20),
        cost_estimate=pl.CostEstimate(flops=rows * count * QB * 400 * 8 * 256 * 4, bytes_accessed=rows * length * triple * 2, transcendentals=0),
        name="attend",
    )(lows, vlens, starts, joined)


def attn_bwd_kernel(width, length, begin, count, resume, lo_ref, vlen_ref, start_ref, joined_ref, grad_ref, *rest):
    if resume:
        dk_in, dv_in, *rest = rest
    dq_ref, dk_ref, dv_ref, bias_ref = rest
    row = pl.program_id(0)
    vlen = vlen_ref[row]
    dk_ref[...] = jnp.zeros_like(dk_ref)
    dv_ref[...] = jnp.zeros_like(dv_ref)
    if resume:
        n = dk_in.shape[1]
        dk_ref[0, :n] = dk_in[0]
        dv_ref[0, :n] = dv_in[0]

    def block(step, _):
        qb = step + begin
        lo = lo_ref[row, qb]
        base = pl.multiple_of(qb * QB, QB)
        first = pl.multiple_of(lo * QB, QB)
        own = pl.ds(base, QB)
        target = pl.ds(pl.multiple_of(step * QB, QB), QB)

        def variant(blocks):
            span = blocks * QB
            keys = pl.ds(first, span)
            begins = start_ref[0, pl.ds(qb, 1), :]
            i = base + iota((QB, QB), 1)
            for b in range(blocks):
                j = first + b * QB + iota((QB, QB), 0)
                ok = ((j >= begins) & (j <= i) & (j < vlen)) | (j == i)
                bias_ref[b * QB:(b + 1) * QB, :] = jnp.where(ok, 0.0, NEGATIVE)
            bias = bias_ref[:span, :]
            bias = jnp.concatenate([bias, bias], axis=1)
            at = [pl.ds(lane, 128) for lane in range(0, width, 128)]
            key_at = [pl.ds(width + lane, 128) for lane in range(0, width, 128)]
            value_at = [pl.ds(2 * width + lane, 128) for lane in range(0, width, 128)]
            query = [split_heads(joined_ref[0, own, lanes] * jnp.asarray(0.125, BF16)) for lanes in at]
            grads = [split_heads(grad_ref[0, target, lanes]) for lanes in at]
            scores = [dot_nt(joined_ref[0, keys, lanes], q) for q, lanes in zip(query, key_at)]
            change = [dot_nt(joined_ref[0, keys, lanes], g) for g, lanes in zip(grads, value_at)]
            scores = [s + bias for s in scores]
            tops = [jnp.max(s, axis=0, keepdims=True) for s in scores]
            prob = [jnp.exp(s - top) for s, top in zip(scores, tops)]
            totals = [1.0 / jnp.sum(p, axis=0, keepdims=True) for p in prob]
            prob = [p * total for p, total in zip(prob, totals)]
            scaled = [p * c for p, c in zip(prob, change)]
            sums = [jnp.sum(t, axis=0, keepdims=True) for t in scaled]
            moved = [(t - p * total).astype(BF16) for t, p, total in zip(scaled, prob, sums)]
            for p, g, lanes in zip(prob, grads, at):
                dv_ref[0, keys, lanes] += dot(p.astype(BF16), g)
            for m, q, lanes in zip(moved, query, at):
                dk_ref[0, keys, lanes] += dot(m, q)
            back = [dot_tn(m, joined_ref[0, keys, lanes]) for m, lanes in zip(moved, key_at)]
            for b, lanes in zip(back, at):
                dq_ref[0, target, lanes] = (join_heads(b) * 0.125).astype(BF16)

        for blocks in range(1, 6):
            pl.when(qb - lo + 1 == blocks)(functools.partial(variant, blocks))
        return 0

    lax.fori_loop(0, count, block, 0)


def attn_bwd(joined, grads, starts, lows, vlens, begin, count, carry=None):
    rows, length, triple = joined.shape
    width = triple // 3
    full = pl.BlockSpec((1, length, width), lambda r, *_: (r, 0, 0))
    part = pl.BlockSpec((1, count * QB, width), lambda r, *_: (r, 0, 0))
    ins = [
        pl.BlockSpec((1, length // QB, QB), lambda r, *_: (r, 0, 0)),
        pl.BlockSpec((1, length, triple), lambda r, *_: (r, 0, 0)),
        part,
    ]
    args = [lows, vlens, starts, joined, grads]
    reach = begin * QB + count * QB
    if carry is not None:
        ins += [pl.BlockSpec((1, carry[0].shape[1], width), lambda r, *_: (r, 0, 0))] * 2
        args += list(carry)
    outk = pl.BlockSpec((1, reach, width), lambda r, *_: (r, 0, 0))
    spec = pltpu.PrefetchScalarGridSpec(
        num_scalar_prefetch=2,
        grid=(rows,),
        in_specs=ins,
        out_specs=[part, outk, outk],
        scratch_shapes=[pltpu.VMEM((5 * QB, QB), F32)],
    )
    return pl.pallas_call(
        functools.partial(attn_bwd_kernel, width, length, begin, count, carry is not None),
        grid_spec=spec,
        out_shape=[
            jax.ShapeDtypeStruct((rows, count * QB, width), BF16),
            jax.ShapeDtypeStruct((rows, reach, width), F32),
            jax.ShapeDtypeStruct((rows, reach, width), F32),
        ],
        compiler_params=pltpu.CompilerParams(vmem_limit_bytes=56 << 20),
        cost_estimate=pl.CostEstimate(flops=rows * count * QB * 400 * 8 * 256 * 10, bytes_accessed=rows * length * triple * 4, transcendentals=0),
        name="attend_back",
    )(*args)


def normalise(values):
    centred = values - jnp.mean(values, axis=-1, keepdims=True)
    inverse = lax.rsqrt(jnp.mean(centred * centred, axis=-1, keepdims=True) + 1e-05)
    return centred * inverse, inverse


def pull_norm(scaled, hat, inverse):
    return inverse * (
        scaled
        - jnp.mean(scaled, axis=-1, keepdims=True)
        - hat * jnp.mean(scaled * hat, axis=-1, keepdims=True)
    )


def constant_spec(shape, *where):
    where = where or (0,) * len(shape)
    return pl.BlockSpec(shape, lambda *_: where)


def join_kernel(tokens_ref, gains_ref, weight_ref, joined_ref):
    hat, _ = normalise(tokens_ref[0].astype(F32))
    normed = (hat * gains_ref[0:1] + gains_ref[1:2]).astype(BF16)
    joined_ref[0] = dot(normed, weight_ref[...]).astype(BF16)


def join_tokens(tokens, gains, packed, tile=512):
    rows, length, width = tokens.shape
    return pl.pallas_call(
        join_kernel,
        grid=(rows, length // tile),
        in_specs=[
            pl.BlockSpec((1, tile, width), lambda r, t: (r, t, 0)),
            constant_spec(gains.shape),
            constant_spec((width, 3 * width)),
        ],
        out_specs=pl.BlockSpec((1, tile, 3 * width), lambda r, t: (r, t, 0)),
        out_shape=jax.ShapeDtypeStruct((rows, length, 3 * width), BF16),
        compiler_params=pltpu.CompilerParams(vmem_limit_bytes=40 << 20),
        cost_estimate=pl.CostEstimate(
            flops=rows * length * width * width * 6, bytes_accessed=rows * length * width * 8, transcendentals=0
        ),
        name="join",
    )(tokens, gains, packed)


def mixed_kernel(attended_ref, tokens_ref, gains_ref, weight_ref, router_ref, hidden_ref, mixed_ref, logits_ref):
    hidden = tokens_ref[0].astype(F32) + dot(attended_ref[0], weight_ref[...])
    hidden_ref[0] = hidden
    hat, _ = normalise(hidden)
    mixed = (hat * gains_ref[2:3] + gains_ref[3:4]).astype(BF16)
    mixed_ref[0] = mixed
    logits_ref[0] = dot_nt(router_ref[...], mixed)


def mix_tokens(attended, tokens, gains, packed, router, offset, tile=512):
    rows, span, width = attended.shape
    block = pl.BlockSpec((1, tile, width), lambda r, t: (r, t, 0))
    return pl.pallas_call(
        mixed_kernel,
        grid=(rows, span // tile),
        in_specs=[
            block,
            pl.BlockSpec((1, tile, width), lambda r, t: (r, t + offset // tile, 0)),
            constant_spec(gains.shape),
            constant_spec((width, width), 0, 3),
            constant_spec(router.shape),
        ],
        out_specs=[block, block, pl.BlockSpec((1, router.shape[0], tile), lambda r, t: (r, 0, t))],
        out_shape=[
            jax.ShapeDtypeStruct((rows, span, width), F32),
            jax.ShapeDtypeStruct((rows, span, width), BF16),
            jax.ShapeDtypeStruct((rows, router.shape[0], span), F32),
        ],
        compiler_params=pltpu.CompilerParams(vmem_limit_bytes=40 << 20),
        cost_estimate=pl.CostEstimate(
            flops=rows * span * width * width * 2, bytes_accessed=rows * span * width * 10, transcendentals=0
        ),
        name="mix",
    )(attended, tokens, gains, packed, router)


def pool_kernel(experts, scale, gates_ref, values_ref, out_ref):
    rows, places = values_ref.shape[0], values_ref.shape[1]
    sub = 16

    def step(s, _):
        here = pl.ds(pl.multiple_of(s * sub, sub), sub)
        gates = gates_ref[here, :].astype(BF16).astype(F32)
        values = [values_ref[r, here, :].astype(F32) for r in range(rows)]
        for e in range(experts):
            total = sum(gates[:, r * experts + e: r * experts + e + 1] * values[r] for r in range(rows))
            out_ref[0, e, here, :] = (scale * total).astype(BF16)
        return 0

    lax.fori_loop(0, places // sub, step, 0, unroll=2)


def pool_tokens(gates, values, owners, experts, scale):
    rows, span, width = values.shape
    places = span // owners
    return pl.pallas_call(
        functools.partial(pool_kernel, experts, scale),
        grid=(owners,),
        in_specs=[
            pl.BlockSpec((places, gates.shape[1]), lambda i: (i, 0)),
            pl.BlockSpec((rows, places, width), lambda i: (0, i, 0)),
        ],
        out_specs=pl.BlockSpec((1, experts, places, width), lambda i: (i, 0, 0, 0)),
        out_shape=jax.ShapeDtypeStruct((owners, experts, places, width), BF16),
        compiler_params=pltpu.CompilerParams(vmem_limit_bytes=40 << 20),
        cost_estimate=pl.CostEstimate(
            flops=rows * span * width * 200, bytes_accessed=rows * span * width * 8, transcendentals=0
        ),
        name="pool",
    )(gates, values)


CUBIC = 0.044715
SLOPE = math.sqrt(2.0 / math.pi)


def expert_kernel(steps, pooled_ref, weights_ref, result_ref, act_ref, slope_ref, total_ref):
    step = pl.program_id(0)
    blocks, places, width = pooled_ref.shape
    pooled = pooled_ref[...].reshape(blocks * places, width)
    pre = dot(pooled, weights_ref[0, 0])
    square = pre * pre
    bent = jnp.tanh(SLOPE * pre * (1.0 + CUBIC * square))
    half = 0.5 * (1.0 + bent)
    act = (pre * half).astype(BF16)
    act_ref[0] = act
    slope_ref[0] = half + 0.5 * pre * (1.0 - bent * bent) * (SLOPE * (1.0 + 3.0 * CUBIC * square))
    result = dot_nt(act, weights_ref[0, 1])

    @pl.when(step == 0)
    def _():
        total_ref[...] = result

    @pl.when(step > 0)
    def _():
        total_ref[...] += result

    @pl.when(step == steps - 1)
    def _():
        result_ref[...] = total_ref[...].astype(BF16).reshape(blocks, places, width)


def run_experts(pooled, weights):
    blocks, places, width = pooled.shape
    steps, _, _, tile = weights.shape
    count = blocks * places
    return pl.pallas_call(
        functools.partial(expert_kernel, steps),
        grid=(steps,),
        in_specs=[constant_spec(pooled.shape), pl.BlockSpec((1, 2, width, tile), lambda i: (i, 0, 0, 0))],
        out_specs=[
            constant_spec(pooled.shape),
            pl.BlockSpec((1, count, tile), lambda i: (i, 0, 0)),
            pl.BlockSpec((1, count, tile), lambda i: (i, 0, 0)),
        ],
        out_shape=[
            jax.ShapeDtypeStruct(pooled.shape, BF16),
            jax.ShapeDtypeStruct((steps, count, tile), BF16),
            jax.ShapeDtypeStruct((steps, count, tile), F32),
        ],
        scratch_shapes=[pltpu.VMEM((count, width), F32)],
        compiler_params=pltpu.CompilerParams(vmem_limit_bytes=40 << 20),
        cost_estimate=pl.CostEstimate(
            flops=count * width * tile * steps * 8, bytes_accessed=width * tile * steps * 8, transcendentals=0
        ),
        name="experts",
    )(pooled, weights)


def expert_back_kernel(steps, pooled_ref, grads_ref, result_ref, act_ref, slope_ref, weights_ref, back_ref, grad_ref, total_ref):
    step = pl.program_id(0)
    blocks, places, width = pooled_ref.shape
    count = blocks * places
    pooled = pooled_ref[...].reshape(count, width)
    grads = grads_ref[...].reshape(count, width)
    act = act_ref[0]
    grad_pre = (dot(grads, weights_ref[0, 1]) * slope_ref[0]).astype(BF16)
    grad_ref[0, 0] = dot_tn(pooled, grad_pre).astype(BF16)
    grad_ref[0, 1] = dot_tn(grads, act).astype(BF16)
    part = dot_nt(grad_pre, weights_ref[0, 0])

    @pl.when(step == 0)
    def _():
        total_ref[...] = part

    @pl.when(step > 0)
    def _():
        total_ref[...] += part

    @pl.when(step == steps - 1)
    def _():
        grad_pooled = total_ref[...].astype(BF16)
        back_ref[:, :places] = grad_pooled.reshape(blocks, places, width)
        result = result_ref[...].reshape(count, width)
        product = result.astype(F32) * grads.astype(F32) + grad_pooled.astype(F32) * pooled.astype(F32)
        high = product.astype(BF16)
        rest = (product - high.astype(F32)).astype(BF16)
        ones = jnp.ones((16, width), BF16)
        sums = dot_nt(ones, high) + dot_nt(ones, rest)
        top = sums.astype(BF16)
        low = (sums - top.astype(F32)).astype(BF16)
        for b in range(blocks):
            here = slice(b * places, b * places + places)
            fill = jnp.zeros((16, width - 2 * places), BF16)
            back_ref[b, places:] = jnp.concatenate([top[:, here], low[:, here], fill], axis=1)


def pull_experts(pooled, grads, result, act, slope, weights):
    blocks, places, width = pooled.shape
    steps, _, _, tile = weights.shape
    count = blocks * places
    return pl.pallas_call(
        functools.partial(expert_back_kernel, steps),
        grid=(steps,),
        in_specs=[constant_spec(pooled.shape)] * 3
        + [pl.BlockSpec((1, count, tile), lambda i: (i, 0, 0))] * 2
        + [pl.BlockSpec((1, 2, width, tile), lambda i: (i, 0, 0, 0))],
        out_specs=[
            constant_spec((blocks, places + 16, width)),
            pl.BlockSpec((1, 2, width, tile), lambda i: (i, 0, 0, 0)),
        ],
        out_shape=[
            jax.ShapeDtypeStruct((blocks, places + 16, width), BF16),
            jax.ShapeDtypeStruct(weights.shape, BF16),
        ],
        scratch_shapes=[pltpu.VMEM((count, width), F32)],
        compiler_params=pltpu.CompilerParams(vmem_limit_bytes=40 << 20),
        cost_estimate=pl.CostEstimate(
            flops=count * width * tile * steps * 12, bytes_accessed=width * tile * steps * 8, transcendentals=0
        ),
        name="pull_experts",
    )(pooled, grads, result, act, slope, weights)


def spread_kernel(experts, group, gates_ref, result_ref, grads_ref, hidden_ref, out_ref, change_ref):
    rows, places = grads_ref.shape[0], grads_ref.shape[1]
    sub = 16
    slots = gates_ref.shape[1]

    def step(s, _):
        here = pl.ds(pl.multiple_of(s * sub, sub), sub)
        results = [result_ref[0, e, here, :].astype(F32) * group for e in range(experts)]
        gates = gates_ref[here, :].astype(BF16).astype(F32)
        lane = iota((sub, slots), 1)
        changes = jnp.zeros((sub, slots), F32)
        for r in range(rows):
            grads = grads_ref[r, here, :].astype(F32)
            for e in range(experts):
                both = jnp.sum(grads * results[e], axis=1, keepdims=True)
                changes = jnp.where(lane == r * experts + e, both, changes)
            total = sum(gates[:, r * experts + e: r * experts + e + 1] * results[e] for e in range(experts))
            out_ref[r, here, :] = (hidden_ref[r, here, :] + total.astype(BF16).astype(F32)).astype(BF16)
        change_ref[here, :] = changes
        return 0

    lax.fori_loop(0, places // sub, step, 0, unroll=2)


def spread_tokens(gates, result, cotangent, hidden, group):
    rows, span, width = hidden.shape
    owners, experts, places, _ = result.shape
    block = pl.BlockSpec((rows, places, width), lambda i: (0, i, 0))
    slots = pl.BlockSpec((places, gates.shape[1]), lambda i: (i, 0))
    return pl.pallas_call(
        functools.partial(spread_kernel, experts, group),
        grid=(owners,),
        in_specs=[slots, pl.BlockSpec((1, experts, places, width), lambda i: (i, 0, 0, 0)), block, block],
        out_specs=[block, slots],
        out_shape=[jax.ShapeDtypeStruct((rows, span, width), BF16), jax.ShapeDtypeStruct(gates.shape, F32)],
        compiler_params=pltpu.CompilerParams(vmem_limit_bytes=40 << 20),
        cost_estimate=pl.CostEstimate(
            flops=rows * span * width * 200, bytes_accessed=rows * span * width * 10, transcendentals=0
        ),
        name="spread",
    )(gates, result, cotangent, hidden)


def router_kernel(experts, gates_ref, inner_ref, change_ref, pooled_ref, mixed_ref, router_ref, grad_ref, router_grad_ref, logits_ref, routed_ref):
    rows, places = mixed_ref.shape[0], mixed_ref.shape[1]
    sub = 16
    slots = gates_ref.shape[1]

    @pl.when(pl.program_id(0) == 0)
    def _():
        router_grad_ref[...] = jnp.zeros_like(router_grad_ref)

    def change(s, _):
        here = pl.ds(pl.multiple_of(s * sub, sub), sub)
        pooled = [pooled_ref[0, e, here, :].astype(F32) for e in range(experts)]
        lane = iota((sub, slots), 1)
        changes = jnp.zeros((sub, slots), F32)
        for r in range(rows):
            mixed = mixed_ref[r, here, :].astype(F32)
            for e in range(experts):
                both = jnp.sum(pooled[e] * mixed, axis=1, keepdims=True)
                changes = jnp.where(lane == r * experts + e, both, changes)
        changes = (changes + change_ref[here, :]).astype(BF16).astype(F32)
        logits_ref[here, :] = (gates_ref[here, :] * (changes - inner_ref[here, :])).astype(BF16)
        return 0

    lax.fori_loop(0, places // sub, change, 0, unroll=2)
    low = logits_ref[...]
    for r in range(rows):
        routed_ref[r] = dot(low, router_ref[r])
        router_grad_ref[...] += dot_tn(low, mixed_ref[r])[r * experts: r * experts + experts]

    def spread(s, _):
        here = pl.ds(pl.multiple_of(s * sub, sub), sub)
        pooled = [pooled_ref[0, e, here, :].astype(F32) for e in range(experts)]
        gates = gates_ref[here, :].astype(BF16).astype(F32)
        for r in range(rows):
            total = sum(
                (gates[:, r * experts + e: r * experts + e + 1] * pooled[e] for e in range(experts)),
                routed_ref[r, here, :],
            )
            grad_ref[r, here, :] = total.astype(BF16)
        return 0

    lax.fori_loop(0, places // sub, spread, 0, unroll=2)


def pull_gates(gates, inner, change, pooled, mixed, router):
    rows, span, width = mixed.shape
    owners, experts, depth, _ = pooled.shape
    places = span // owners
    block = pl.BlockSpec((rows, places, width), lambda i: (0, i, 0))
    slots = pl.BlockSpec((places, gates.shape[1]), lambda i: (i, 0))
    return pl.pallas_call(
        functools.partial(router_kernel, experts),
        grid=(owners,),
        in_specs=[
            slots,
            slots,
            slots,
            pl.BlockSpec((1, experts, depth, width), lambda i: (i, 0, 0, 0)),
            block,
            constant_spec(router.shape),
        ],
        out_specs=[block, constant_spec((experts, width))],
        out_shape=[
            jax.ShapeDtypeStruct((rows, span, width), BF16),
            jax.ShapeDtypeStruct((experts, width), F32),
        ],
        scratch_shapes=[pltpu.VMEM((places, gates.shape[1]), BF16), pltpu.VMEM((rows, places, width), F32)],
        compiler_params=pltpu.CompilerParams(vmem_limit_bytes=40 << 20),
        cost_estimate=pl.CostEstimate(
            flops=rows * span * width * 200, bytes_accessed=rows * span * width * 10, transcendentals=0
        ),
        name="pull_gates",
    )(gates, inner, change, pooled, mixed, router)


def hidden_kernel(grad_ref, hidden_ref, cotangent_ref, attended_ref, gains_ref, weight_ref, out_ref, low_ref, project_ref, sums_ref):
    @pl.when((pl.program_id(0) == 0) & (pl.program_id(1) == 0))
    def _():
        project_ref[...] = jnp.zeros_like(project_ref)
        sums_ref[...] = jnp.zeros_like(sums_ref)

    grads = grad_ref[0].astype(F32)
    hat, inverse = normalise(hidden_ref[0])
    sums_ref[0:1] += jnp.sum(grads * hat, axis=0, keepdims=True)
    sums_ref[1:2] += jnp.sum(grads, axis=0, keepdims=True)
    total = cotangent_ref[0].astype(F32) + pull_norm(grads * gains_ref[2:3], hat, inverse)
    out_ref[0] = total
    low = total.astype(BF16)
    project_ref[...] += dot_tn(attended_ref[0], low)
    low_ref[0] = dot_nt(low, weight_ref[...]).astype(BF16)


def pull_hidden(grad_mixed, hidden, cotangent, attended, gains, packed, offset, tile=512):
    rows, span, width = hidden.shape
    block = pl.BlockSpec((1, tile, width), lambda r, t: (r, t, 0))
    return pl.pallas_call(
        hidden_kernel,
        grid=(rows, span // tile),
        in_specs=[
            block,
            block,
            pl.BlockSpec((1, tile, width), lambda r, t: (r, t + offset // tile, 0)),
            block,
            constant_spec(gains.shape),
            constant_spec((width, width), 0, 3),
        ],
        out_specs=[block, block, constant_spec((width, width)), constant_spec((8, width))],
        out_shape=[
            jax.ShapeDtypeStruct((rows, span, width), F32),
            jax.ShapeDtypeStruct((rows, span, width), BF16),
            jax.ShapeDtypeStruct((width, width), F32),
            jax.ShapeDtypeStruct((8, width), F32),
        ],
        compiler_params=pltpu.CompilerParams(vmem_limit_bytes=48 << 20),
        cost_estimate=pl.CostEstimate(
            flops=rows * span * width * width * 4, bytes_accessed=rows * span * width * 16, transcendentals=0
        ),
        name="pull_hidden",
    )(grad_mixed, hidden, cotangent, attended, gains, packed)


def tokens_kernel(query_ref, keys_ref, values_ref, tokens_ref, hidden_ref, gains_ref, weight_ref, out_ref, project_ref, sums_ref):
    @pl.when((pl.program_id(0) == 0) & (pl.program_id(1) == 0))
    def _():
        project_ref[...] = jnp.zeros_like(project_ref)
        sums_ref[...] = jnp.zeros_like(sums_ref)

    width = tokens_ref.shape[2]
    hat, inverse = normalise(tokens_ref[0].astype(F32))
    normed = (hat * gains_ref[0:1] + gains_ref[1:2]).astype(BF16)
    parts = [query_ref[0], keys_ref[0].astype(BF16), values_ref[0].astype(BF16)]
    grads = jnp.zeros((normed.shape[0], width), F32)
    for i, part in enumerate(parts):
        lanes = slice(i * width, i * width + width)
        project_ref[:, lanes] += dot_tn(normed, part)
        grads += dot_nt(part, weight_ref[:, lanes])
    sums_ref[0:1] += jnp.sum(grads * hat, axis=0, keepdims=True)
    sums_ref[1:2] += jnp.sum(grads, axis=0, keepdims=True)
    out_ref[0] = hidden_ref[0] + pull_norm(grads * gains_ref[0:1], hat, inverse)


def pull_tokens(query, keys, values, tokens, hidden, gains, packed, tile=512):
    rows, length, width = tokens.shape
    block = pl.BlockSpec((1, tile, width), lambda r, t: (r, t, 0))
    return pl.pallas_call(
        tokens_kernel,
        grid=(rows, length // tile),
        in_specs=[block] * 5 + [constant_spec(gains.shape), constant_spec((width, 3 * width))],
        out_specs=[block, constant_spec((width, 3 * width)), constant_spec((8, width))],
        out_shape=[
            jax.ShapeDtypeStruct((rows, length, width), F32),
            jax.ShapeDtypeStruct((width, 3 * width), F32),
            jax.ShapeDtypeStruct((8, width), F32),
        ],
        compiler_params=pltpu.CompilerParams(vmem_limit_bytes=48 << 20),
        cost_estimate=pl.CostEstimate(
            flops=rows * length * width * width * 12, bytes_accessed=rows * length * width * 20, transcendentals=0
        ),
        name="pull_tokens",
    )(query, keys, values, tokens, hidden, gains, packed)


def ring_order(size):
    inner = 2 if size % 2 == 0 and size > 2 else 1
    outer = size // inner
    up = [z * inner for z in range(outer)]
    if inner == 1:
        return up
    return up + [z * inner + 1 for z in reversed(range(outer))]


def shift(value, order, step):
    count = len(order)
    return lax.ppermute(value, "dp", [(order[i], order[(i + step) % count]) for i in range(count)])


def flip(value, bit, axis="fsdp"):
    count = lax.axis_size(axis)
    return lax.ppermute(value, axis, [(i, i ^ bit) for i in range(count)])


def turn(value, step, axis="dp"):
    count = lax.axis_size(axis)
    return lax.ppermute(value, axis, [(i, (i + step) % count) for i in range(count)])


def take(values, index):
    return lax.dynamic_index_in_dim(values, index, 0, keepdims=False)


def put(values, value, index):
    return lax.dynamic_update_index_in_dim(values, value, index, 0)


def add(a, b):
    return (a.astype(F32) + b.astype(F32)).astype(BF16)


def place_of(order):
    places = [order.index(i) for i in range(len(order))]
    return jnp.array(places)[lax.axis_index("dp")], jnp.array(order)


def scatter_ring(values, order):
    count = len(order)
    here, table = place_of(order)
    half = values.shape[1] // 2
    parts = [(values[:, :half], 1), (values[:, half:], -1)]
    held = [take(part, table[(here - way) % count]) for part, way in parts]
    for step in range(count - 1):
        came = [shift(value, order, way) for value, (_, way) in zip(held, parts)]
        held = [
            add(value, take(part, table[(here - way * (2 + step)) % count])) for value, (part, way) in zip(came, parts)
        ]
    return jnp.concatenate(held, axis=0)


def gather_ring(value, order):
    count = len(order)
    here, table = place_of(order)
    whole = jnp.zeros((count,) + value.shape, value.dtype)
    whole = put(whole, value, table[here])
    ahead = behind = value
    for step in range(1, count // 2 + 1):
        ahead = shift(ahead, order, 1)
        whole = put(whole, ahead, table[(here - step) % count])
        if 2 * step < count:
            behind = shift(behind, order, -1)
            whole = put(whole, behind, table[(here + step) % count])
    return whole


def gather_all(value, order):
    whole = gather_ring(value, order)
    size = lax.axis_size("fsdp")
    here = lax.axis_index("fsdp")
    whole = whole[:, None]
    bit = size // 2
    while bit:
        other = flip(whole, bit)
        first = jnp.concatenate([whole, other], axis=1)
        second = jnp.concatenate([other, whole], axis=1)
        whole = jnp.where((here & bit) == 0, first, second)
        bit //= 2
    bits = size.bit_length() - 1
    shape = whole.shape
    whole = whole.reshape((shape[0],) + (2,) * bits + shape[2:])
    whole = whole.transpose((0,) + tuple(range(bits, 0, -1)) + tuple(range(bits + 1, bits + 1 + len(shape) - 2)))
    return whole.reshape((-1,) + shape[3:])


def scatter_all(values):
    owners, size = lax.axis_size("dp"), lax.axis_size("fsdp")
    bits = size.bit_length() - 1
    here = lax.axis_index("fsdp")
    width = values.shape[1]
    held = values.reshape((owners,) + (2,) * bits + (-1, width))
    for level in range(bits):
        axis = bits - level
        mine = (here >> level) & 1
        keep = lax.dynamic_index_in_dim(held, mine, axis, keepdims=False)
        give = lax.dynamic_index_in_dim(held, 1 - mine, axis, keepdims=False)
        held = add(keep, flip(give, 1 << level))
    data = lax.axis_index("dp")
    total = take(held, data).astype(F32)
    for step in range(1, owners):
        total += turn(take(held, (data + step) % owners), step).astype(F32)
    return total


def exchange(values):
    size = lax.axis_size("fsdp")
    here = lax.axis_index("fsdp")
    whole = values
    for bits in range(1, size):
        whole = put(whole, flip(take(values, here ^ bits), bits), here ^ bits)
    return whole


def per_device(
    tokens,
    segment_ids,
    pad_tokens,
    cotangent,
    project_in,
    project_out,
    router_weight,
    expert_in,
    expert_out,
    first_gain,
    first_bias,
    second_gain,
    second_bias,
):
    blocks_here, rows, length, width = tokens.shape
    tokens = tokens.reshape(rows, length, width)
    cotangent = cotangent.reshape(rows, length, width)
    segments = segment_ids.reshape(rows, length)
    group = pad_tokens.shape[1]
    owners = lax.axis_size("dp")
    experts = router_weight.shape[1]
    order = ring_order(owners)
    data_index = lax.axis_index("dp")
    places = length // owners

    vectors = jnp.stack([first_gain, first_bias, second_gain, second_bias], axis=1)
    small = jnp.concatenate([router_weight, vectors], axis=1)
    small = jnp.pad(small, ((0, 0), (0, 128 - small.shape[1])))
    packed = jnp.concatenate([project_in, project_out, small], axis=1)
    packed = gather_all(packed, order)
    weights = jnp.stack([expert_in[0], expert_out[0].T])
    packed, weights = lax.optimization_barrier((packed, weights))
    weights = gather_ring(weights, order)
    small = packed[:, 4 * width:].T
    router = jnp.pad(small[:experts], ((0, 16 - experts), (0, 0)))
    gains = jnp.pad(small[experts: experts + 4].astype(F32), ((0, 4), (0, 0)))

    own_pads = lax.dynamic_slice_in_dim(pad_tokens[0], data_index * rows, rows, 0)
    vlens = (length - own_pads).astype(jnp.int32)
    starts = jnp.zeros_like(segments)
    for doc in range(1, 4):
        before = jnp.sum((segments < doc).astype(jnp.int32), axis=1, keepdims=True)
        starts = jnp.where(segments == doc, before, starts)
    starts = starts.reshape(rows, length // QB, QB)
    lows = starts[:, :, 0] // QB

    joined = join_tokens(tokens, gains, packed)
    attended = attn_fwd(joined, starts, lows, vlens, 0, length // QB)
    hidden, mixed, logits = mix_tokens(attended, tokens, gains, packed, router, 0)

    logits = logits[:, :experts]
    valid = (jnp.arange(length)[None, :] < vlens[:, None])[:, None, :]
    highest = jnp.max(jnp.where(valid, logits, NEGATIVE), axis=0)
    total = jnp.sum(jnp.where(valid, jnp.exp(logits - highest), 0.0), axis=0)
    stats = jnp.stack([highest, total])
    stats = jnp.stack([stats] + [turn(stats, step) for step in range(1, owners)])
    tops = jnp.max(stats[:, 0], axis=0)
    total = jnp.sum(stats[:, 1] * jnp.exp(stats[:, 0] - tops), axis=0)
    gates = jnp.where(valid, jnp.exp(jnp.where(valid, logits - tops, NEGATIVE)) / total, 0.0)
    gates = gates.reshape(rows * experts, length).T

    pooled = exchange(scatter_ring(pool_tokens(gates, mixed, owners, experts, 1.0), order))
    result, act, slope = run_experts(pooled, weights)
    grad_result = exchange(scatter_ring(pool_tokens(gates, cotangent, owners, experts, float(group)), order))
    grad_pooled, grad_weights = pull_experts(pooled, grad_result, result, act, slope, weights)
    result = gather_ring(exchange(result), order)
    grad_pooled = gather_ring(exchange(grad_pooled), order)
    layer_out, change = spread_tokens(gates, result, cotangent, hidden, group)

    grad_pooled, grad_weights = lax.optimization_barrier((grad_pooled, grad_weights))
    grad_weights = lax.all_to_all(grad_weights, "dp", split_axis=0, concat_axis=0, tiled=True)
    grad_weights = jnp.sum(grad_weights.astype(F32), axis=0)
    inner = grad_pooled[:, :, places].astype(F32)
    inner = inner[..., :places] + inner[..., places: 2 * places]
    inner = inner.transpose(0, 2, 1).reshape(length, 1, experts)
    inner = jnp.broadcast_to(inner, (length, rows, experts)).reshape(length, rows * experts)
    spots = jnp.stack(
        [jnp.pad(router[:experts], ((r * experts, (rows - 1 - r) * experts), (0, 0))) for r in range(rows)]
    )
    grad_mixed, router_grad = pull_gates(gates, inner, change, grad_pooled, mixed, spots)
    grad_hidden, grad_attended, grad_proj_out, sums_two = pull_hidden(
        grad_mixed, hidden, cotangent, attended, gains, packed, 0
    )
    query, keys, values = attn_bwd(joined, grad_attended, starts, lows, vlens, 0, length // QB)
    tokens_grad, grad_proj_in, sums_one = pull_tokens(query, keys, values, tokens, grad_hidden, gains, packed)

    late = jnp.concatenate([router_grad, sums_one[:2], sums_two[:2]], axis=0).T
    late = jnp.pad(late, ((0, 0), (0, 128 - late.shape[1])))
    reduced = scatter_all(jnp.concatenate([grad_proj_in, grad_proj_out, late], axis=1).astype(BF16))
    late = reduced[:, 4 * width:]
    return (
        layer_out[None],
        tokens_grad[None],
        reduced[:, : 3 * width],
        reduced[:, 3 * width: 4 * width],
        late[:, :experts],
        grad_weights[0][None],
        grad_weights[1].T[None],
        late[:, experts],
        late[:, experts + 1],
        late[:, experts + 2],
        late[:, experts + 3],
    )


def solution(mesh):
    in_specs = (
        P("fsdp", "dp", None, None),
        P("fsdp", "dp", None),
        P("fsdp", None),
        P("fsdp", "dp", None, None),
        P(("dp", "fsdp"), None),
        P(("dp", "fsdp"), None),
        P(("dp", "fsdp"), None),
        P("fsdp", None, "dp"),
        P("fsdp", "dp", None),
        P(("dp", "fsdp")),
        P(("dp", "fsdp")),
        P(("dp", "fsdp")),
        P(("dp", "fsdp")),
    )
    out_specs = (
        P("fsdp", "dp", None, None),
        P("fsdp", "dp", None, None),
        P(("dp", "fsdp"), None),
        P(("dp", "fsdp"), None),
        P(("dp", "fsdp"), None),
        P("fsdp", None, "dp"),
        P("fsdp", "dp", None),
        P(("dp", "fsdp")),
        P(("dp", "fsdp")),
        P(("dp", "fsdp")),
        P(("dp", "fsdp")),
    )
    return jax.shard_map(
        per_device, mesh=mesh, in_specs=in_specs, out_specs=out_specs, check_vma=False
    )
```

```python
import functools, math
import jax
import jax.numpy as jnp
import numpy as np
from jax import lax
from jax.experimental import pallas as pl
from jax.experimental.pallas import tpu as pltpu
from jax.sharding import PartitionSpec as P

NEGATIVE = -1e30
QB = 128
F32 = jnp.float32
BF16 = jnp.bfloat16
NT = (((1,), (1,)), ((), ()))
TN = (((0,), (0,)), ((), ()))


def dot(a, b):
    return jnp.dot(a, b, preferred_element_type=F32)


def dot_nt(a, b):
    return lax.dot_general(a, b, NT, preferred_element_type=F32)


def dot_tn(a, b):
    return lax.dot_general(a, b, TN, preferred_element_type=F32)


def iota(shape, axis):
    return lax.broadcasted_iota(jnp.int32, shape, axis)


def split_heads(x):
    low = iota(x.shape, 1) < 64
    zero = jnp.zeros_like(x)
    return jnp.concatenate([jnp.where(low, x, zero), jnp.where(low, zero, x)], axis=0)


def join_heads(x):
    half = x.shape[0] // 2
    low = iota((half, x.shape[1]), 1) < 64
    return jnp.where(low, x[:half], x[half:])


def attn_fwd_kernel(width, begin, count, lo_ref, vlen_ref, start_ref, joined_ref, out_ref, bias_ref):
    row = pl.program_id(0)
    vlen = vlen_ref[row]

    def block(step, _):
        qb = step + begin
        lo = lo_ref[row, qb]
        base = pl.multiple_of(qb * QB, QB)
        first = pl.multiple_of(lo * QB, QB)
        own = pl.ds(base, QB)
        target = pl.ds(pl.multiple_of(step * QB, QB), QB)

        def variant(blocks):
            span = blocks * QB
            keys = pl.ds(first, span)
            begins = jnp.broadcast_to(start_ref[0, pl.ds(qb, 1), :], (QB, QB)).T
            i = base + iota((QB, QB), 0)
            for b in range(blocks):
                j = first + b * QB + iota((QB, QB), 1)
                ok = ((j >= begins) & (j <= i) & (j < vlen)) | (j == i)
                bias_ref[:, b * QB:(b + 1) * QB] = jnp.where(ok, 0.0, NEGATIVE)
            bias = bias_ref[:, :span]
            bias = jnp.concatenate([bias, bias], axis=0)
            at = [pl.ds(lane, 128) for lane in range(0, width, 128)]
            key_at = [pl.ds(width + lane, 128) for lane in range(0, width, 128)]
            value_at = [pl.ds(2 * width + lane, 128) for lane in range(0, width, 128)]
            query = [split_heads(joined_ref[0, own, lanes] * jnp.asarray(0.125, BF16)) for lanes in at]
            scores = [dot_nt(q, joined_ref[0, keys, lanes]) for q, lanes in zip(query, key_at)]
            scores = [s + bias for s in scores]
            tops = [jnp.max(s, axis=1, keepdims=True) for s in scores]
            raised = [jnp.exp(s - top) for s, top in zip(scores, tops)]
            totals = [jnp.sum(p, axis=1, keepdims=True) for p in raised]
            out = [dot(p.astype(BF16), joined_ref[0, keys, lanes]) for p, lanes in zip(raised, value_at)]
            for o, total, lanes in zip(out, totals, at):
                out_ref[0, target, lanes] = join_heads(o * (1.0 / total)).astype(BF16)

        for blocks in range(1, 6):
            pl.when(qb - lo + 1 == blocks)(functools.partial(variant, blocks))
        return 0

    lax.fori_loop(0, count, block, 0)


def attn_fwd(joined, starts, lows, vlens, begin, count):
    rows, length, triple = joined.shape
    width = triple // 3
    spec = pltpu.PrefetchScalarGridSpec(
        num_scalar_prefetch=2,
        grid=(rows,),
        in_specs=[
            pl.BlockSpec((1, length // QB, QB), lambda r, *_: (r, 0, 0)),
            pl.BlockSpec((1, length, triple), lambda r, *_: (r, 0, 0)),
        ],
        out_specs=pl.BlockSpec((1, count * QB, width), lambda r, *_: (r, 0, 0)),
        scratch_shapes=[pltpu.VMEM((QB, 5 * QB), F32)],
    )
    return pl.pallas_call(
        functools.partial(attn_fwd_kernel, width, begin, count),
        grid_spec=spec,
        out_shape=jax.ShapeDtypeStruct((rows, count * QB, width), BF16),
        compiler_params=pltpu.CompilerParams(vmem_limit_bytes=48 << 20),
        cost_estimate=pl.CostEstimate(flops=rows * count * QB * 400 * 8 * 256 * 4, bytes_accessed=rows * length * triple * 2, transcendentals=0),
        name="attend",
    )(lows, vlens, starts, joined)


def attn_bwd_kernel(width, row_from, count, lo_ref, vlen_ref, start_ref, joined_ref, grad_ref, *rest):
    out_ref, dk_ref, dv_ref, bias_ref = rest[-4:]
    row = pl.program_id(0) + row_from
    vlen = vlen_ref[row]
    dk_ref[...] = jnp.zeros_like(dk_ref)
    dv_ref[...] = jnp.zeros_like(dv_ref)

    def block(step, _):
        qb = step
        lo = lo_ref[row, qb]
        base = pl.multiple_of(qb * QB, QB)
        first = pl.multiple_of(lo * QB, QB)
        own = pl.ds(base, QB)
        target = pl.ds(pl.multiple_of(step * QB, QB), QB)

        def variant(blocks):
            span = blocks * QB
            keys = pl.ds(first, span)
            begins = start_ref[0, pl.ds(qb, 1), :]
            i = base + iota((QB, QB), 1)
            for b in range(blocks):
                j = first + b * QB + iota((QB, QB), 0)
                ok = ((j >= begins) & (j <= i) & (j < vlen)) | (j == i)
                bias_ref[b * QB:(b + 1) * QB, :] = jnp.where(ok, 0.0, NEGATIVE)
            bias = bias_ref[:span, :]
            bias = jnp.concatenate([bias, bias], axis=1)
            at = [pl.ds(lane, 128) for lane in range(0, width, 128)]
            key_at = [pl.ds(width + lane, 128) for lane in range(0, width, 128)]
            value_at = [pl.ds(2 * width + lane, 128) for lane in range(0, width, 128)]
            query = [split_heads(joined_ref[0, own, lanes] * jnp.asarray(0.125, BF16)) for lanes in at]
            grads = [split_heads(grad_ref[0, target, lanes]) for lanes in at]
            scores = [dot_nt(joined_ref[0, keys, lanes], q) for q, lanes in zip(query, key_at)]
            change = [dot_nt(joined_ref[0, keys, lanes], g) for g, lanes in zip(grads, value_at)]
            scores = [s + bias for s in scores]
            tops = [jnp.max(s, axis=0, keepdims=True) for s in scores]
            prob = [jnp.exp(s - top) for s, top in zip(scores, tops)]
            totals = [1.0 / jnp.sum(p, axis=0, keepdims=True) for p in prob]
            prob = [p * total for p, total in zip(prob, totals)]
            scaled = [p * c for p, c in zip(prob, change)]
            sums = [jnp.sum(t, axis=0, keepdims=True) for t in scaled]
            moved = [(t - p * total).astype(BF16) for t, p, total in zip(scaled, prob, sums)]
            for p, g, lanes in zip(prob, grads, at):
                dv_ref[keys, lanes] += dot(p.astype(BF16), g)
            for m, q, lanes in zip(moved, query, at):
                dk_ref[keys, lanes] += dot(m, q)
            back = [dot_tn(m, joined_ref[0, keys, lanes]) for m, lanes in zip(moved, key_at)]
            for b, lanes in zip(back, at):
                out_ref[0, target, lanes] = (join_heads(b) * 0.125).astype(BF16)

        for blocks in range(1, 6):
            pl.when(qb - lo + 1 == blocks)(functools.partial(variant, blocks))
        return 0

    lax.fori_loop(0, count, block, 0)
    out_ref[0, :, width: 2 * width] = dk_ref[...].astype(BF16)
    out_ref[0, :, 2 * width:] = dv_ref[...].astype(BF16)


def attn_bwd(joined, grads, starts, lows, vlens, row_from, row_to, held=None):
    rows, length, triple = joined.shape
    width = triple // 3
    count = length // QB
    aliased = [] if held is None else [held]
    wide = pl.BlockSpec((1, length, triple), lambda r, *_: (r + row_from, 0, 0))
    return pl.pallas_call(
        functools.partial(attn_bwd_kernel, width, row_from, count),
        grid_spec=pltpu.PrefetchScalarGridSpec(
            num_scalar_prefetch=2,
            grid=(row_to - row_from,),
            in_specs=[
                pl.BlockSpec((1, count, QB), lambda r, *_: (r + row_from, 0, 0)),
                wide,
                pl.BlockSpec((1, length, width), lambda r, *_: (r + row_from, 0, 0)),
            ]
            + [pl.BlockSpec(memory_space=pltpu.HBM) for _ in aliased],
            out_specs=wide,
            scratch_shapes=[
                pltpu.VMEM((length, width), F32),
                pltpu.VMEM((length, width), F32),
                pltpu.VMEM((5 * QB, QB), F32),
            ],
        ),
        out_shape=jax.ShapeDtypeStruct(joined.shape, BF16),
        input_output_aliases={5: 0} if aliased else {},
        compiler_params=pltpu.CompilerParams(vmem_limit_bytes=48 << 20),
        cost_estimate=pl.CostEstimate(
            flops=(row_to - row_from) * length * 400 * 8 * 256 * 20,
            bytes_accessed=(row_to - row_from) * length * triple * 4,
            transcendentals=0,
        ),
        name="attend_back",
    )(lows, vlens, starts, joined, grads, *aliased)


def normalise(values):
    centred = values - jnp.mean(values, axis=-1, keepdims=True)
    inverse = lax.rsqrt(jnp.mean(centred * centred, axis=-1, keepdims=True) + 1e-05)
    return centred * inverse, inverse


def pull_norm(scaled, hat, inverse):
    return inverse * (
        scaled
        - jnp.mean(scaled, axis=-1, keepdims=True)
        - hat * jnp.mean(scaled * hat, axis=-1, keepdims=True)
    )


def constant_spec(shape, *where):
    where = where or (0,) * len(shape)
    return pl.BlockSpec(shape, lambda *_: where)


def join_kernel(tokens_ref, gains_ref, weight_ref, joined_ref):
    hat, _ = normalise(tokens_ref[0].astype(F32))
    normed = (hat * gains_ref[0:1] + gains_ref[1:2]).astype(BF16)
    joined_ref[0] = dot(normed, weight_ref[...]).astype(BF16)


def join_tokens(tokens, gains, packed, tile=512):
    rows, length, width = tokens.shape
    return pl.pallas_call(
        join_kernel,
        grid=(rows, length // tile),
        in_specs=[
            pl.BlockSpec((1, tile, width), lambda r, t: (r, t, 0)),
            constant_spec(gains.shape),
            constant_spec((width, 3 * width)),
        ],
        out_specs=pl.BlockSpec((1, tile, 3 * width), lambda r, t: (r, t, 0)),
        out_shape=jax.ShapeDtypeStruct((rows, length, 3 * width), BF16),
        compiler_params=pltpu.CompilerParams(vmem_limit_bytes=40 << 20),
        cost_estimate=pl.CostEstimate(
            flops=rows * length * width * width * 6, bytes_accessed=rows * length * width * 8, transcendentals=0
        ),
        name="join",
    )(tokens, gains, packed)


def mixed_kernel(attended_ref, tokens_ref, gains_ref, weight_ref, router_ref, hidden_ref, mixed_ref, logits_ref):
    hidden = tokens_ref[0].astype(F32) + dot(attended_ref[0], weight_ref[...])
    hidden_ref[0] = hidden
    hat, _ = normalise(hidden)
    mixed = (hat * gains_ref[2:3] + gains_ref[3:4]).astype(BF16)
    mixed_ref[0] = mixed
    logits_ref[0] = dot_nt(router_ref[...], mixed)


def mix_tokens(attended, tokens, gains, packed, router, offset, tile=512):
    rows, span, width = attended.shape
    block = pl.BlockSpec((1, tile, width), lambda r, t: (r, t, 0))
    return pl.pallas_call(
        mixed_kernel,
        grid=(rows, span // tile),
        in_specs=[
            block,
            pl.BlockSpec((1, tile, width), lambda r, t: (r, t + offset // tile, 0)),
            constant_spec(gains.shape),
            constant_spec((width, width), 0, 3),
            constant_spec(router.shape),
        ],
        out_specs=[block, block, pl.BlockSpec((1, router.shape[0], tile), lambda r, t: (r, 0, t))],
        out_shape=[
            jax.ShapeDtypeStruct((rows, span, width), F32),
            jax.ShapeDtypeStruct((rows, span, width), BF16),
            jax.ShapeDtypeStruct((rows, router.shape[0], span), F32),
        ],
        compiler_params=pltpu.CompilerParams(vmem_limit_bytes=40 << 20),
        cost_estimate=pl.CostEstimate(
            flops=rows * span * width * width * 2, bytes_accessed=rows * span * width * 10, transcendentals=0
        ),
        name="mix",
    )(attended, tokens, gains, packed, router)


def pool_kernel(experts, scale, slots_ref, gates_ref, values_ref, out_ref):
    rows, places = values_ref.shape[0], values_ref.shape[1]
    sub = 16

    def step(s, _):
        here = pl.ds(pl.multiple_of(s * sub, sub), sub)
        gates = gates_ref[here, :].astype(BF16).astype(F32)
        values = [values_ref[r, here, :].astype(F32) for r in range(rows)]
        for e in range(experts):
            total = sum(gates[:, r * experts + e: r * experts + e + 1] * values[r] for r in range(rows))
            out_ref[0, e, here, :] = (scale * total).astype(BF16)
        return 0

    lax.fori_loop(0, places // sub, step, 0, unroll=2)


def pool_tokens(slots, gates, values, experts, scale):
    rows, span, width = values.shape
    owners = slots.shape[0]
    places = span // owners
    return pl.pallas_call(
        functools.partial(pool_kernel, experts, scale),
        grid_spec=pltpu.PrefetchScalarGridSpec(
            num_scalar_prefetch=1,
            grid=(owners,),
            in_specs=[
                pl.BlockSpec((places, gates.shape[1]), lambda i, slots: (slots[i], 0)),
                pl.BlockSpec((rows, places, width), lambda i, slots: (0, slots[i], 0)),
            ],
            out_specs=pl.BlockSpec((1, experts, places, width), lambda i, slots: (i, 0, 0, 0)),
        ),
        out_shape=jax.ShapeDtypeStruct((owners, experts, places, width), BF16),
        compiler_params=pltpu.CompilerParams(vmem_limit_bytes=40 << 20),
        cost_estimate=pl.CostEstimate(
            flops=rows * span * width * 1000, bytes_accessed=rows * span * width * 8, transcendentals=0
        ),
        name="pool",
    )(slots, gates, values)


CUBIC = 0.044715
SLOPE = math.sqrt(2.0 / math.pi)


def expert_kernel(steps, pooled_ref, weights_ref, result_ref, act_ref, slope_ref, total_ref):
    step = pl.program_id(0)
    blocks, places, width = pooled_ref.shape
    pooled = pooled_ref[...].reshape(blocks * places, width)
    pre = dot(pooled, weights_ref[0, 0])
    square = pre * pre
    bent = jnp.tanh(SLOPE * pre * (1.0 + CUBIC * square))
    half = 0.5 * (1.0 + bent)
    act = (pre * half).astype(BF16)
    act_ref[0] = act
    slope_ref[0] = half + 0.5 * pre * (1.0 - bent * bent) * (SLOPE * (1.0 + 3.0 * CUBIC * square))
    result = dot_nt(act, weights_ref[0, 1])

    @pl.when(step == 0)
    def _():
        total_ref[...] = result

    @pl.when(step > 0)
    def _():
        total_ref[...] += result

    @pl.when(step == steps - 1)
    def _():
        result_ref[...] = total_ref[...].astype(BF16).reshape(blocks, places, width)


def run_experts(pooled, weights):
    blocks, places, width = pooled.shape
    steps, _, _, tile = weights.shape
    count = blocks * places
    return pl.pallas_call(
        functools.partial(expert_kernel, steps),
        grid=(steps,),
        in_specs=[constant_spec(pooled.shape), pl.BlockSpec((1, 2, width, tile), lambda i: (i, 0, 0, 0))],
        out_specs=[
            constant_spec(pooled.shape),
            pl.BlockSpec((1, count, tile), lambda i: (i, 0, 0)),
            pl.BlockSpec((1, count, tile), lambda i: (i, 0, 0)),
        ],
        out_shape=[
            jax.ShapeDtypeStruct(pooled.shape, BF16),
            jax.ShapeDtypeStruct((steps, count, tile), BF16),
            jax.ShapeDtypeStruct((steps, count, tile), F32),
        ],
        scratch_shapes=[pltpu.VMEM((count, width), F32)],
        compiler_params=pltpu.CompilerParams(vmem_limit_bytes=40 << 20),
        cost_estimate=pl.CostEstimate(
            flops=count * width * tile * steps * 8, bytes_accessed=width * tile * steps * 8, transcendentals=0
        ),
        name="experts",
    )(pooled, weights)


def expert_back_kernel(steps, slots_ref, pooled_ref, grads_ref, result_ref, act_ref, slope_ref, weights_ref, back_ref, grad_ref, total_ref):
    step = pl.program_id(0)
    blocks, places, width = pooled_ref.shape
    count = blocks * places
    pooled = pooled_ref[...].reshape(count, width)
    grads = grads_ref[...].reshape(count, width)
    act = act_ref[0]
    grad_pre = (dot(grads, weights_ref[0, 1]) * slope_ref[0]).astype(BF16)
    grad_ref[0, 0] = dot_tn(pooled, grad_pre).astype(BF16)
    grad_ref[0, 1] = dot_tn(grads, act).astype(BF16)
    part = dot_nt(grad_pre, weights_ref[0, 0])

    @pl.when(step == 0)
    def _():
        total_ref[...] = part

    @pl.when(step > 0)
    def _():
        total_ref[...] += part

    @pl.when(step == steps - 1)
    def _():
        grad_pooled = total_ref[...].astype(BF16)
        back_ref[:, :places] = grad_pooled.reshape(blocks, places, width)
        result = result_ref[...].reshape(count, width)
        product = result.astype(F32) * grads.astype(F32) + grad_pooled.astype(F32) * pooled.astype(F32)
        high = product.astype(BF16)
        rest = (product - high.astype(F32)).astype(BF16)
        ones = jnp.ones((16, width), BF16)
        sums = dot_nt(ones, high) + dot_nt(ones, rest)
        top = sums.astype(BF16)
        low = (sums - top.astype(F32)).astype(BF16)
        for b in range(blocks):
            here = slice(b * places, b * places + places)
            fill = jnp.zeros((16, width - 2 * places), BF16)
            back_ref[b, places:] = jnp.concatenate([top[:, here], low[:, here], fill], axis=1)


def pull_experts(slots, pooled, grads, result, act, slope, weights):
    blocks, places, width = pooled.shape
    steps, _, _, tile = weights.shape
    count = blocks * places
    return pl.pallas_call(
        functools.partial(expert_back_kernel, steps),
        grid_spec=pltpu.PrefetchScalarGridSpec(
            num_scalar_prefetch=1,
            grid=(steps,),
            in_specs=[constant_spec(pooled.shape)] * 3
            + [pl.BlockSpec((1, count, tile), lambda i, slots: (i, 0, 0))] * 2
            + [pl.BlockSpec((1, 2, width, tile), lambda i, slots: (i, 0, 0, 0))],
            out_specs=[
                constant_spec((blocks, places + 16, width)),
                pl.BlockSpec((1, 2, width, tile), lambda i, slots: (slots[i], 0, 0, 0)),
            ],
            scratch_shapes=[pltpu.VMEM((count, width), F32)],
        ),
        out_shape=[
            jax.ShapeDtypeStruct((blocks, places + 16, width), BF16),
            jax.ShapeDtypeStruct(weights.shape, BF16),
        ],
        compiler_params=pltpu.CompilerParams(vmem_limit_bytes=40 << 20),
        cost_estimate=pl.CostEstimate(
            flops=count * width * tile * steps * 12, bytes_accessed=width * tile * steps * 8, transcendentals=0
        ),
        name="pull_experts",
    )(slots, pooled, grads, result, act, slope, weights)


def spread_kernel(group, count, slots_ref, gates_ref, grads_ref, hidden_ref, *rest):
    parts, (out_ref, change_ref, result_ref) = rest[:count], rest[-3:]
    for k in range(count):
        @pl.when(pl.program_id(0) == k)
        def _():
            result_ref[...] = parts[k][...]

    rows, places = grads_ref.shape[0], grads_ref.shape[1]
    experts = result_ref.shape[0]
    sub = 16
    columns = gates_ref.shape[1]

    def step(s, _):
        here = pl.ds(pl.multiple_of(s * sub, sub), sub)
        results = [result_ref[e, here, :].astype(F32) * group for e in range(experts)]
        gates = gates_ref[here, :].astype(BF16).astype(F32)
        lane = iota((sub, columns), 1)
        changes = jnp.zeros((sub, columns), F32)
        for r in range(rows):
            grads = grads_ref[r, here, :].astype(F32)
            for e in range(experts):
                both = jnp.sum(grads * results[e], axis=1, keepdims=True)
                changes = jnp.where(lane == r * experts + e, both, changes)
            total = sum(gates[:, r * experts + e: r * experts + e + 1] * results[e] for e in range(experts))
            out_ref[r, here, :] = (hidden_ref[r, here, :] + total.astype(BF16).astype(F32)).astype(BF16)
        change_ref[0, here, :] = changes
        return 0

    lax.fori_loop(0, places // sub, step, 0, unroll=2)


def slot_of(found):
    found = list(found)
    step = found[-1] - found[0]
    return lambda i, slots: slots[found[0] + i * step]


def spread_tokens(found, slots, gates, cotangent, hidden, group, held):
    rows, span, width = hidden.shape
    parts = list(found.values())
    experts, places, _ = parts[0].shape
    at = slot_of(found)
    block = pl.BlockSpec((rows, places, width), lambda i, slots: (0, at(i, slots), 0))
    columns = gates.shape[1]
    aliased = [] if held is None else [held]
    return pl.pallas_call(
        functools.partial(spread_kernel, group, len(parts)),
        grid_spec=pltpu.PrefetchScalarGridSpec(
            num_scalar_prefetch=1,
            grid=(len(parts),),
            in_specs=[pl.BlockSpec((places, columns), lambda i, slots: (at(i, slots), 0)), block, block]
            + [constant_spec(part.shape) for part in parts]
            + [pl.BlockSpec(memory_space=pltpu.HBM) for _ in aliased],
            out_specs=[block, pl.BlockSpec((1, places, columns), lambda i, slots: (i, 0, 0))],
            scratch_shapes=[pltpu.VMEM(parts[0].shape, BF16)],
        ),
        out_shape=[
            jax.ShapeDtypeStruct((rows, span, width), BF16),
            jax.ShapeDtypeStruct((len(parts), places, columns), F32),
        ],
        input_output_aliases={4 + len(parts): 0} if aliased else {},
        compiler_params=pltpu.CompilerParams(vmem_limit_bytes=24 << 20),
        cost_estimate=pl.CostEstimate(
            flops=len(parts) * rows * places * width * 5000, bytes_accessed=rows * places * width * 10, transcendentals=0
        ),
        name="spread",
    )(slots, gates, cotangent, hidden, *parts, *aliased)


def pull_kernel(first, count, slots_ref, gates_ref, change_ref, mixed_ref, hidden_ref, cotangent_ref, attended_ref, router_ref, gains_ref, weight_ref, *rest):
    parts, rest = rest[:count], rest[count:]
    out_ref, low_ref, router_grad_ref, project_ref, sums_ref, pooled_ref, logits_ref, grad_ref = rest[-8:]

    @pl.when(pl.program_id(0) == 0)
    def _():
        if first:
            router_grad_ref[...] = jnp.zeros_like(router_grad_ref)
            project_ref[...] = jnp.zeros_like(project_ref)
            sums_ref[...] = jnp.zeros_like(sums_ref)
        else:
            router_grad_ref[...] = rest[2][...]
            project_ref[...] = rest[3][...]
            sums_ref[...] = rest[4][...]

    for k in range(count):
        @pl.when(pl.program_id(0) == k)
        def _():
            pooled_ref[...] = parts[k][...]

    rows, places, width = mixed_ref.shape
    experts = pooled_ref.shape[0]
    sub = 16
    columns = gates_ref.shape[1]
    inner = jnp.zeros((places, columns), F32)
    for e in range(experts):
        pick = (iota((16, columns), 0) == 0) & (iota((16, columns), 1) % experts == e)
        pick = jnp.where(pick, 1.0, 0.0).astype(BF16)
        inner += dot_tn(pooled_ref[e, places:, :places], pick) + dot_tn(pooled_ref[e, places:, places: 2 * places], pick)

    def change(s, _):
        here = pl.ds(pl.multiple_of(s * sub, sub), sub)
        pooled = [pooled_ref[e, here, :].astype(F32) for e in range(experts)]
        lane = iota((sub, columns), 1)
        changes = jnp.zeros((sub, columns), F32)
        for r in range(rows):
            mixed = mixed_ref[r, here, :].astype(F32)
            for e in range(experts):
                both = jnp.sum(pooled[e] * mixed, axis=1, keepdims=True)
                changes = jnp.where(lane == r * experts + e, both, changes)
        logits_ref[here, :] = changes
        return 0

    lax.fori_loop(0, places // sub, change, 0, unroll=2)
    changes = (logits_ref[...] + change_ref[0]).astype(BF16).astype(F32)
    low = (gates_ref[...] * (changes - inner)).astype(BF16)
    for r in range(rows):
        grad_ref[r] = dot(low, router_ref[r])
        router_grad_ref[...] += dot_tn(low, mixed_ref[r])[r * experts: r * experts + experts]

    def spread(s, _):
        here = pl.ds(pl.multiple_of(s * sub, sub), sub)
        pooled = [pooled_ref[e, here, :].astype(F32) for e in range(experts)]
        gates = gates_ref[here, :].astype(BF16).astype(F32)
        for r in range(rows):
            grad_ref[r, here, :] = sum(
                (gates[:, r * experts + e: r * experts + e + 1] * pooled[e] for e in range(experts)),
                grad_ref[r, here, :],
            )
        return 0

    lax.fori_loop(0, places // sub, spread, 0, unroll=2)

    for r in range(rows):
        grads = grad_ref[r].astype(BF16).astype(F32)
        hat, inverse = normalise(hidden_ref[r])
        sums_ref[0:1] += jnp.sum(grads * hat, axis=0, keepdims=True)
        sums_ref[1:2] += jnp.sum(grads, axis=0, keepdims=True)
        total = cotangent_ref[r].astype(F32) + pull_norm(grads * gains_ref[2:3], hat, inverse)
        out_ref[r] = total
        total = total.astype(BF16)
        project_ref[...] += dot_tn(attended_ref[r], total)
        low_ref[r] = dot_nt(total, weight_ref[...]).astype(BF16)


def pull_slots(found, slots, gates, change, mixed, hidden, cotangent, attended, router, gains, packed, held):
    rows, span, width = mixed.shape
    parts = list(found.values())
    experts, depth, _ = parts[0].shape
    places = span // slots.shape[0]
    at = slot_of(found)
    block = pl.BlockSpec((rows, places, width), lambda i, slots: (0, at(i, slots), 0))
    columns = gates.shape[1]
    sums = [(experts, width), (width, width), (8, width)]
    ins = [
        pl.BlockSpec((places, columns), lambda i, slots: (at(i, slots), 0)),
        pl.BlockSpec((1, places, columns), lambda i, slots: (i, 0, 0)),
        block,
        block,
        block,
        block,
        constant_spec(router.shape),
        constant_spec(gains.shape),
        constant_spec((width, width), 0, 3),
    ] + [constant_spec(part.shape) for part in parts]
    aliases = {}
    if held is not None:
        aliases = {len(ins) + 1: 0, len(ins) + 2: 1}
        ins += [pl.BlockSpec(memory_space=pltpu.HBM)] * 2 + [constant_spec(shape) for shape in sums]
    return pl.pallas_call(
        functools.partial(pull_kernel, held is None, len(parts)),
        grid_spec=pltpu.PrefetchScalarGridSpec(
            num_scalar_prefetch=1,
            grid=(len(parts),),
            in_specs=ins,
            out_specs=[block, block] + [constant_spec(shape) for shape in sums],
            scratch_shapes=[
                pltpu.VMEM(parts[0].shape, BF16),
                pltpu.VMEM((places, columns), F32),
                pltpu.VMEM((rows, places, width), F32),
            ],
        ),
        out_shape=[jax.ShapeDtypeStruct((rows, span, width), F32), jax.ShapeDtypeStruct((rows, span, width), BF16)]
        + [jax.ShapeDtypeStruct(shape, F32) for shape in sums],
        input_output_aliases=aliases,
        compiler_params=pltpu.CompilerParams(vmem_limit_bytes=32 << 20),
        cost_estimate=pl.CostEstimate(
            flops=len(parts) * rows * places * width * width * 20,
            bytes_accessed=rows * places * width * 20,
            transcendentals=0,
        ),
        name="pull_slots",
    )(slots, gates, change, mixed, hidden, cotangent, attended, router, gains, packed, *parts, *(held or ()))


def project_kernel(grads_ref, tokens_ref, product_ref, sums_ref):
    @pl.when((pl.program_id(0) == 0) & (pl.program_id(1) == 0))
    def _():
        product_ref[...] = jnp.zeros_like(product_ref)
        sums_ref[...] = jnp.zeros_like(sums_ref)

    hat = normalise(tokens_ref[0].astype(F32))[0].astype(BF16)
    ones = jnp.ones((hat.shape[0], 8), BF16)
    product_ref[...] += dot_tn(hat, grads_ref[0])
    sums_ref[...] += dot_tn(ones, grads_ref[0])


def project_grads(grads, tokens, tile=512):
    rows, length, width = tokens.shape
    shapes = [(width, 3 * width), (8, 3 * width)]
    return pl.pallas_call(
        project_kernel,
        grid=(rows, length // tile),
        in_specs=[
            pl.BlockSpec((1, tile, 3 * width), lambda r, t: (r, t, 0)),
            pl.BlockSpec((1, tile, width), lambda r, t: (r, t, 0)),
        ],
        out_specs=[constant_spec(shape) for shape in shapes],
        out_shape=[jax.ShapeDtypeStruct(shape, F32) for shape in shapes],
        compiler_params=pltpu.CompilerParams(vmem_limit_bytes=40 << 20),
        cost_estimate=pl.CostEstimate(
            flops=rows * length * width * width * 6, bytes_accessed=rows * length * width * 12, transcendentals=0
        ),
        name="project_grads",
    )(grads, tokens)


def tokens_kernel(grads_ref, tokens_ref, hidden_ref, gains_ref, weight_ref, out_ref):
    hat, inverse = normalise(tokens_ref[0].astype(F32))
    grads = dot_nt(grads_ref[0], weight_ref[...])
    out_ref[0] = hidden_ref[0] + pull_norm(grads * gains_ref[0:1], hat, inverse)


def pull_tokens(grads, tokens, hidden, gains, packed, tile=512):
    rows, length, width = tokens.shape
    block = pl.BlockSpec((1, tile, width), lambda r, t: (r, t, 0))
    return pl.pallas_call(
        tokens_kernel,
        grid=(rows, length // tile),
        in_specs=[
            pl.BlockSpec((1, tile, 3 * width), lambda r, t: (r, t, 0)),
            block,
            block,
            constant_spec(gains.shape),
            constant_spec((width, 3 * width)),
        ],
        out_specs=block,
        out_shape=jax.ShapeDtypeStruct((rows, length, width), F32),
        compiler_params=pltpu.CompilerParams(vmem_limit_bytes=40 << 20),
        cost_estimate=pl.CostEstimate(
            flops=rows * length * width * width * 20, bytes_accessed=rows * length * width * 16, transcendentals=0
        ),
        name="pull_tokens",
    )(grads, tokens, hidden, gains, packed)


def ring_order(size):
    inner = 2 if size % 2 == 0 and size > 2 else 1
    outer = size // inner
    up = [z * inner for z in range(outer)]
    if inner == 1:
        return up
    return up + [z * inner + 1 for z in reversed(range(outer))]


def shift(value, order, step):
    count = len(order)
    return lax.ppermute(value, "dp", [(order[i], order[(i + step) % count]) for i in range(count)])


def flip(value, bit, axis="fsdp"):
    count = lax.axis_size(axis)
    return lax.ppermute(value, axis, [(i, i ^ bit) for i in range(count)])


def turn(value, step, axis="dp"):
    count = lax.axis_size(axis)
    return lax.ppermute(value, axis, [(i, (i + step) % count) for i in range(count)])


def take(values, index):
    starts = (index,) + (jnp.uint32(0),) * (values.ndim - 1)
    return lax.dynamic_slice(values, starts, (1,) + values.shape[1:])[0]


def put(values, value, index):
    return lax.dynamic_update_slice(values, value[None], (index,) + (jnp.uint32(0),) * value.ndim)


def add(a, b):
    return (a.astype(F32) + b.astype(F32)).astype(BF16)


def together(*values):
    return lax.optimization_barrier(values)


class Ring:
    def __init__(self, value, order):
        self.order, self.done = order, 0
        self.ahead = self.behind = value

    def left(self):
        return self.done < len(self.order) // 2

    def step(self, *beside):
        count = len(self.order)
        self.done += 1
        found = {count - self.done: shift(self.ahead, self.order, 1)}
        if 2 * self.done < count:
            found[self.done] = shift(self.behind, self.order, -1)
        values = together(*found.values(), *beside)
        found = dict(zip(found, values))
        self.ahead = found[count - self.done]
        self.behind = found.get(self.done)
        return found, list(values[len(found):])


def gather_all(value, order, spots):
    count = len(order)
    size = lax.axis_size("fsdp")
    whole = put(jnp.zeros((count,) + value.shape, value.dtype), value, spots[0])
    ring = Ring(value, order)
    while ring.left():
        for slot, part in ring.step()[0].items():
            whole = put(whole, part, spots[slot])
    here = lax.axis_index("fsdp")
    whole = whole[:, None]
    bit = size // 2
    while bit:
        other = flip(whole, bit)
        upper = (here & bit) != 0
        whole = jnp.stack([jnp.where(upper, other, whole), jnp.where(upper, whole, other)], axis=1)
        whole = whole.swapaxes(1, 2).reshape((count, -1) + value.shape)
        bit //= 2
    return whole


def scatter_all(values, steps):
    owners, size = lax.axis_size("dp"), lax.axis_size("fsdp")
    bits = size.bit_length() - 1
    here = lax.axis_index("fsdp")
    width = values.shape[1]
    pair = pair_of(owners)
    held = values.reshape((owners // pair, pair) + (2,) * bits + (-1, width))
    for level in range(bits):
        axis = bits + 1 - level
        upper = ((here >> level) & 1) != 0
        low, high = (lax.index_in_dim(held, i, axis, keepdims=False) for i in (0, 1))
        held = add(jnp.where(upper, high, low), flip(jnp.where(upper, low, high), 1 << level))
    if pair == 2:
        upper = (lax.axis_index("dp") & 1) != 0
        low, high = held[:, 0], held[:, 1]
        held = add(jnp.where(upper, high, low), flip(jnp.where(upper, low, high), 1, "dp"))
    else:
        held = held[:, 0]
    return sum(
        (turn(take(held, steps[k]), k * pair).astype(F32) for k in range(1, owners // pair)),
        take(held, steps[0]).astype(F32),
    )


def pair_of(owners):
    return 2 if owners % 2 == 0 else 1


def exchange(values):
    return jnp.stack([values[0]] + [flip(values[k], k) for k in range(1, values.shape[0])])


def per_device(
    tokens,
    segment_ids,
    pad_tokens,
    cotangent,
    project_in,
    project_out,
    router_weight,
    expert_in,
    expert_out,
    first_gain,
    first_bias,
    second_gain,
    second_bias,
):
    blocks_here, rows, length, width = tokens.shape
    tokens = tokens.reshape(rows, length, width)
    cotangent = cotangent.reshape(rows, length, width)
    segments = segment_ids.reshape(rows, length)
    group = pad_tokens.shape[1]
    owners = lax.axis_size("dp")
    experts = router_weight.shape[1]
    order = ring_order(owners)
    data_index = lax.axis_index("dp")
    expert_index = lax.axis_index("fsdp")
    places = length // owners

    pair = pair_of(owners)
    lines = owners // pair
    ring = np.array([[order[(order.index(d) + k) % owners] for k in range(owners)] for d in range(owners)], np.int32)
    place = np.array(
        [[(o % pair ^ d % pair) * lines + (o // pair - d // pair) % lines for o in ring[d]] for d in range(owners)],
        np.int32,
    )
    line = np.array([[(d // pair + k) % lines for k in range(lines)] for d in range(owners)], np.int32)
    tables = np.concatenate([ring, place, line], axis=1)
    tables = lax.dynamic_slice(
        jnp.asarray(tables), (data_index.astype(jnp.uint32), jnp.uint32(0)), (1, tables.shape[1])
    )[0]
    slots, shares = tables[:owners], tables[owners: 2 * owners]
    spots = [tables[k].astype(jnp.uint32) for k in range(owners)]
    steps = [tables[2 * owners + k].astype(jnp.uint32) for k in range(lines)]

    vectors = jnp.stack([first_gain, first_bias, second_gain, second_bias], axis=1)
    small = jnp.concatenate([router_weight, vectors], axis=1)
    small = jnp.pad(small, ((0, 0), (0, 128 - small.shape[1])))
    packed = jnp.concatenate([project_in, project_out, small], axis=1)
    weights = jnp.stack([expert_in[0], expert_out[0].T])
    packed, weights = together(packed, weights)
    packed = gather_all(packed, order, spots)
    packed = packed.reshape(width, packed.shape[-1])
    packed, weights = together(packed, weights)
    kept = {0: weights}
    weights = Ring(weights, order)
    small = packed[:, 4 * width:].T
    mine = (jnp.arange(experts)[:, None] ^ jnp.arange(experts)[None, :]) == expert_index
    router = jnp.sum(jnp.where(mine[:, :, None], small[None, :experts], 0), axis=1).astype(BF16)
    spread_router = jnp.stack(
        [jnp.pad(router, ((r * experts, (rows - 1 - r) * experts), (0, 0))) for r in range(rows)]
    )
    gains = jnp.pad(small[experts: experts + 4].astype(F32), ((0, 4), (0, 0)))

    own_pads = lax.dynamic_slice_in_dim(pad_tokens[0], data_index * rows, rows, 0)
    vlens = (length - own_pads).astype(jnp.int32)
    starts = jnp.zeros_like(segments)
    for doc in range(1, 4):
        before = jnp.sum((segments < doc).astype(jnp.int32), axis=1, keepdims=True)
        starts = jnp.where(segments == doc, before, starts)
    starts = starts.reshape(rows, length // QB, QB)
    lows = starts[:, :, 0] // QB

    def meanwhile(value):
        if not weights.left():
            return value
        found, (value,) = weights.step(value)
        kept.update(found)
        return value

    joined = meanwhile(join_tokens(tokens, gains, packed))
    attended = meanwhile(attn_fwd(joined, starts, lows, vlens, 0, length // QB))
    hidden, mixed, logits = mix_tokens(
        attended, tokens, gains, packed, jnp.pad(router, ((0, 16 - experts), (0, 0))), 0
    )
    logits = meanwhile(logits)[:, :experts]
    valid = (jnp.arange(length)[None, :] < vlens[:, None])[:, None, :]
    highest = jnp.max(jnp.where(valid, logits, NEGATIVE), axis=0)
    total = jnp.sum(jnp.where(valid, jnp.exp(logits - highest), 0.0), axis=0)
    stats = jnp.stack([highest, total])[None]
    if pair == 2:
        stats = jnp.concatenate([stats, flip(stats, 1, "dp")])
    stats = jnp.concatenate([stats] + [turn(stats, k * pair) for k in range(1, lines)])
    tops = jnp.max(stats[:, 0], axis=0)
    total = jnp.sum(stats[:, 1] * jnp.exp(stats[:, 0] - tops), axis=0)
    gates = jnp.where(valid, jnp.exp(jnp.where(valid, logits - tops, NEGATIVE)) / total, 0.0)
    gates = gates.reshape(rows * experts, length).T
    pooled = meanwhile(pool_tokens(slots, gates, mixed, experts, 1.0))
    while weights.left():
        kept.update(weights.step()[0])
    weights = jnp.stack([kept[k] for k in range(owners)])
    grads = pool_tokens(slots, gates, cotangent, experts, float(group))

    half = experts // 2
    first = [(pooled[:, :half], 1), (pooled[:, half:], -1)]
    second = [(grads[:, :half], 1), (grads[:, half:], -1)]
    held = [part[-way % owners] for part, way in first]
    later = [part[-way % owners] for part, way in second]
    for step in range(owners - 1):
        came = [shift(value, order, way) for value, (_, way) in zip(held, first)]
        *came, one, two = together(*came, *later)
        held = [add(value, part[-way * (2 + step) % owners]) for value, (part, way) in zip(came, first)]
        came = [shift(value, order, way) for value, (_, way) in zip([one, two], second)]
        later = [add(value, part[-way * (2 + step) % owners]) for value, (part, way) in zip(came, second)]
    pooled = exchange(jnp.concatenate(held, axis=0))
    result, act, slope = run_experts(pooled, weights)
    grads = exchange(jnp.concatenate(later, axis=0))
    grad_pooled, grad_weights = pull_experts(shares, pooled, grads, result, act, slope, weights)

    result = exchange(result)
    back = exchange(grad_pooled)

    def spread(found, out):
        return spread_tokens(found, slots, gates, cotangent, hidden, group, out)

    def pull(found, change, out):
        return pull_slots(
            found, slots, gates, change, mixed, hidden, cotangent, attended, spread_router, gains, packed, out
        )

    turns = owners // 2
    ring, groups = Ring(result, order), [{0: result}]
    out, pulled, changes = None, None, []
    for step in range(turns):
        if step == 0:
            found, (grad_weights,) = ring.step(grad_weights)
        else:
            out, change = spread(groups[step - 1], out)
            found, (out, change) = ring.step(out, change)
            changes.append(change)
        groups.append(found)
    ring, arrived = Ring(together(back, *found.values())[0], order), [{0: back}]
    for step in range(turns):
        if step < 2:
            out, change = spread(groups[turns - 1 + step], out)
            changes.append(change)
        if step > 0:
            pulled = pull(arrived[step - 1], changes[step - 1], pulled)
        if step == turns - 1:
            pulled = pull(arrived[step], changes[step], pulled)
        found, (out, *held) = ring.step(out, *(pulled or ()))
        pulled = held or None
        arrived.append(found)
    pulled = pull(arrived[turns], changes[turns], pulled)
    layer_out = out
    grad_hidden, grad_attended, router_grad, grad_proj_out, sums_two = pulled
    grad_attended, grad_weights = together(grad_attended, grad_weights)
    split = rows - max(1, rows // 4)
    if pair == 2:
        came = flip(grad_weights[lines:], 1, "dp")
    grads = attn_bwd(joined, grad_attended, starts, lows, vlens, 0, split)
    grad_weights = grad_weights[:lines]
    if pair == 2:
        came, grads = together(came, grads)
        grad_weights = add(grad_weights, came)
    came = [turn(grad_weights[k], k * pair) for k in range(1, lines)]
    grads = attn_bwd(joined, grad_attended, starts, lows, vlens, split, rows, grads)
    product, sums_one = project_grads(grads, tokens)
    product, *came = together(product, *came)
    grad_weights = sum((value.astype(F32) for value in came), grad_weights[0].astype(F32))
    full_in = packed[:, : 3 * width].astype(F32)
    sums_one = sums_one[:1]
    grad_proj_in = gains[0][:, None] * product + gains[1][:, None] * sums_one
    sums_one = jnp.stack([jnp.sum(full_in * product, axis=1), jnp.sum(full_in * sums_one, axis=1)])
    tokens_grad = pull_tokens(grads, tokens, grad_hidden, gains, packed)
    router_grad = jnp.sum(jnp.where(mine[:, :, None], router_grad[None], 0.0), axis=1)

    late = jnp.concatenate([router_grad, sums_one, sums_two[:2]], axis=0).T
    late = jnp.pad(late, ((0, 0), (0, 128 - late.shape[1])))
    reduced = scatter_all(jnp.concatenate([grad_proj_in, grad_proj_out, late], axis=1).astype(BF16), steps)
    late = reduced[:, 4 * width:]
    return (
        layer_out[None],
        tokens_grad[None],
        reduced[:, : 3 * width],
        reduced[:, 3 * width: 4 * width],
        late[:, :experts],
        grad_weights[0][None],
        grad_weights[1].T[None],
        late[:, experts],
        late[:, experts + 1],
        late[:, experts + 2],
        late[:, experts + 3],
    )


def solution(mesh):
    in_specs = (
        P("fsdp", "dp", None, None),
        P("fsdp", "dp", None),
        P("fsdp", None),
        P("fsdp", "dp", None, None),
        P(("dp", "fsdp"), None),
        P(("dp", "fsdp"), None),
        P(("dp", "fsdp"), None),
        P("fsdp", None, "dp"),
        P("fsdp", "dp", None),
        P(("dp", "fsdp")),
        P(("dp", "fsdp")),
        P(("dp", "fsdp")),
        P(("dp", "fsdp")),
    )
    out_specs = (
        P("fsdp", "dp", None, None),
        P("fsdp", "dp", None, None),
        P(("dp", "fsdp"), None),
        P(("dp", "fsdp"), None),
        P(("dp", "fsdp"), None),
        P("fsdp", None, "dp"),
        P("fsdp", "dp", None),
        P(("dp", "fsdp")),
        P(("dp", "fsdp")),
        P(("dp", "fsdp")),
        P(("dp", "fsdp")),
    )
    return jax.shard_map(
        per_device, mesh=mesh, in_specs=in_specs, out_specs=out_specs, check_vma=False
    )
```

```python
import functools, math
import jax
import jax.numpy as jnp
import numpy as np
from jax import lax
from jax.experimental import pallas as pl
from jax.experimental.pallas import tpu as pltpu
from jax.sharding import PartitionSpec as P

NEGATIVE = -1e30
QB = 128
F32 = jnp.float32
BF16 = jnp.bfloat16
NT = (((1,), (1,)), ((), ()))
TN = (((0,), (0,)), ((), ()))


def dot(a, b):
    return jnp.dot(a, b, preferred_element_type=F32)


def dot_nt(a, b):
    return lax.dot_general(a, b, NT, preferred_element_type=F32)


def dot_tn(a, b):
    return lax.dot_general(a, b, TN, preferred_element_type=F32)


def iota(shape, axis):
    return lax.broadcasted_iota(jnp.int32, shape, axis)


def split_heads(x):
    low = iota(x.shape, 1) < 64
    zero = jnp.zeros_like(x)
    return jnp.concatenate([jnp.where(low, x, zero), jnp.where(low, zero, x)], axis=0)


def join_heads(x):
    half = x.shape[0] // 2
    low = iota((half, x.shape[1]), 1) < 64
    return jnp.where(low, x[:half], x[half:])


def attn_fwd_kernel(width, batch, count, lo_ref, vlen_ref, start_ref, joined_ref, out_ref, log_ref, bias_ref):
    row = pl.program_id(0) * batch

    def block(qb, _):
        lo = functools.reduce(jnp.minimum, [lo_ref[row + r, qb] for r in range(batch)])
        base = pl.multiple_of(qb * QB, QB)
        first = pl.multiple_of(lo * QB, QB)
        own = pl.ds(base, QB)

        def variant(blocks):
            span = blocks * QB
            keys = pl.ds(first, span)
            i = base + iota((QB, QB), 0)
            bias = []
            for r in range(batch):
                begins = jnp.broadcast_to(start_ref[r, pl.ds(qb, 1), :], (QB, QB)).T
                for b in range(blocks):
                    j = first + b * QB + iota((QB, QB), 1)
                    ok = ((j >= begins) & (j <= i) & (j < vlen_ref[row + r])) | (j == i)
                    bias_ref[r, :, b * QB:(b + 1) * QB] = jnp.where(ok, 0.0, NEGATIVE)
                bias.append(jnp.concatenate([bias_ref[r, :, :span]] * 2, axis=0))
            work = [(r, lane) for r in range(batch) for lane in range(0, width, 128)]
            query = [split_heads(joined_ref[r, own, pl.ds(at, 128)] * jnp.asarray(0.125, BF16)) for r, at in work]
            scores = [dot_nt(q, joined_ref[r, keys, pl.ds(width + at, 128)]) for q, (r, at) in zip(query, work)]
            scores = [s + bias[r] for s, (r, _) in zip(scores, work)]
            tops = [jnp.max(s, axis=1, keepdims=True) for s in scores]
            raised = [jnp.exp(s - top) for s, top in zip(scores, tops)]
            totals = [jnp.sum(p, axis=1, keepdims=True) for p in raised]
            out = [
                dot(p.astype(BF16), joined_ref[r, keys, pl.ds(2 * width + at, 128)]) for p, (r, at) in zip(raised, work)
            ]
            for o, total, (r, at) in zip(out, totals, work):
                out_ref[r, own, pl.ds(at, 128)] = join_heads(o * (1.0 / total)).astype(BF16)
            lane = iota((QB, QB), 1)
            for r in range(batch):
                tile = jnp.zeros((QB, QB), F32)
                for top, total, (other, at) in zip(tops, totals, work):
                    if other == r:
                        log = top + jnp.log(total)
                        tile = jnp.where(lane == at // 64, log[:QB], tile)
                        tile = jnp.where(lane == at // 64 + 1, log[QB:], tile)
                log_ref[r, pl.ds(qb, 1)] = tile.T[None, : log_ref.shape[2]]

        for blocks in range(1, 6):
            pl.when(qb - lo + 1 == blocks)(functools.partial(variant, blocks))
        return 0

    lax.fori_loop(0, count, block, 0)


def attn_fwd(joined, starts, lows, vlens, batch=2):
    rows, length, triple = joined.shape
    width = triple // 3
    count = length // QB
    return pl.pallas_call(
        functools.partial(attn_fwd_kernel, width, batch, count),
        grid_spec=pltpu.PrefetchScalarGridSpec(
            num_scalar_prefetch=2,
            grid=(rows // batch,),
            in_specs=[
                pl.BlockSpec((batch, count, QB), lambda r, *_: (r, 0, 0)),
                pl.BlockSpec((batch, length, triple), lambda r, *_: (r, 0, 0)),
            ],
            out_specs=[
                pl.BlockSpec((batch, length, width), lambda r, *_: (r, 0, 0)),
                pl.BlockSpec((batch, count, width // 64, QB), lambda r, *_: (r, 0, 0, 0)),
            ],
            scratch_shapes=[pltpu.VMEM((batch, QB, 5 * QB), F32)],
        ),
        out_shape=[
            jax.ShapeDtypeStruct((rows, length, width), BF16),
            jax.ShapeDtypeStruct((rows, count, width // 64, QB), F32),
        ],
        compiler_params=pltpu.CompilerParams(vmem_limit_bytes=48 << 20),
        cost_estimate=pl.CostEstimate(
            flops=rows * length * 400 * 8 * 256 * 4, bytes_accessed=rows * length * triple * 2, transcendentals=0
        ),
        name="attend",
    )(lows, vlens, starts, joined)


def attn_bwd_kernel(width, row_from, batch, count, lo_ref, vlen_ref, start_ref, joined_ref, grad_ref, attended_ref, log_ref, *rest):
    out_ref, dk_ref, dv_ref, bias_ref = rest[-4:]
    row = pl.program_id(0) * batch + row_from
    dk_ref[...] = jnp.zeros_like(dk_ref)
    dv_ref[...] = jnp.zeros_like(dv_ref)

    def block(qb, _):
        lo = functools.reduce(jnp.minimum, [lo_ref[row + r, qb] for r in range(batch)])
        base = pl.multiple_of(qb * QB, QB)
        first = pl.multiple_of(lo * QB, QB)
        own = pl.ds(base, QB)

        def variant(blocks):
            span = blocks * QB
            keys = pl.ds(first, span)
            i = base + iota((QB, QB), 1)
            pick = jnp.where(iota((16, width), 1) // 64 == iota((16, width), 0), 1.0, 0.0).astype(BF16)
            bias, sums = [], []
            for r in range(batch):
                begins = start_ref[r, pl.ds(qb, 1), :]
                for b in range(blocks):
                    j = first + b * QB + iota((QB, QB), 0)
                    ok = ((j >= begins) & (j <= i) & (j < vlen_ref[row + r])) | (j == i)
                    bias_ref[r, b * QB:(b + 1) * QB, :] = jnp.where(ok, 0.0, NEGATIVE)
                bias.append(jnp.concatenate([bias_ref[r, :span, :]] * 2, axis=1))
                product = grad_ref[r, own, :].astype(F32) * attended_ref[r, own, :].astype(F32)
                high = product.astype(BF16)
                sums.append(dot_nt(pick, high) + dot_nt(pick, (product - high.astype(F32)).astype(BF16)))
            work = [(r, lane) for r in range(batch) for lane in range(0, width, 128)]
            query = [split_heads(joined_ref[r, own, pl.ds(at, 128)] * jnp.asarray(0.125, BF16)) for r, at in work]
            grads = [split_heads(grad_ref[r, own, pl.ds(at, 128)]) for r, at in work]
            prob, moved = [], []
            for q, g, (r, at) in zip(query, grads, work):
                head = at // 64
                log = log_ref[r, qb]
                log = jnp.concatenate([log[head: head + 1], log[head + 1: head + 2]], axis=1)
                total = jnp.concatenate([sums[r][head: head + 1], sums[r][head + 1: head + 2]], axis=1)
                scores = dot_nt(joined_ref[r, keys, pl.ds(width + at, 128)], q)
                change = dot_nt(joined_ref[r, keys, pl.ds(2 * width + at, 128)], g)
                p = jnp.exp(scores + bias[r] - log)
                prob.append(p.astype(BF16))
                moved.append((p * (change - total)).astype(BF16))
            for p, g, (r, at) in zip(prob, grads, work):
                dv_ref[r, keys, pl.ds(at, 128)] += dot(p, g)
            for m, q, (r, at) in zip(moved, query, work):
                dk_ref[r, keys, pl.ds(at, 128)] += dot(m, q)
            back = [dot_tn(m, joined_ref[r, keys, pl.ds(width + at, 128)]) for m, (r, at) in zip(moved, work)]
            for b, (r, at) in zip(back, work):
                out_ref[r, own, pl.ds(at, 128)] = (join_heads(b) * 0.125).astype(BF16)

        for blocks in range(1, 6):
            pl.when(qb - lo + 1 == blocks)(functools.partial(variant, blocks))
        return 0

    lax.fori_loop(0, count, block, 0)
    out_ref[:, :, width: 2 * width] = dk_ref[...].astype(BF16)
    out_ref[:, :, 2 * width:] = dv_ref[...].astype(BF16)


def attn_bwd(joined, grads, attended, logs, starts, lows, vlens, row_from, row_to, held=None, batch=1):
    rows, length, triple = joined.shape
    width = triple // 3
    count = length // QB
    aliased = [] if held is None else [held]
    skip = row_from // batch
    wide = pl.BlockSpec((batch, length, triple), lambda r, *_: (r + skip, 0, 0))
    slim = pl.BlockSpec((batch, length, width), lambda r, *_: (r + skip, 0, 0))
    return pl.pallas_call(
        functools.partial(attn_bwd_kernel, width, row_from, batch, count),
        grid_spec=pltpu.PrefetchScalarGridSpec(
            num_scalar_prefetch=2,
            grid=((row_to - row_from) // batch,),
            in_specs=[
                pl.BlockSpec((batch, count, QB), lambda r, *_: (r + skip, 0, 0)),
                wide,
                slim,
                slim,
                pl.BlockSpec((batch,) + logs.shape[1:], lambda r, *_: (r + skip, 0, 0, 0)),
            ]
            + [pl.BlockSpec(memory_space=pltpu.HBM) for _ in aliased],
            out_specs=wide,
            scratch_shapes=[
                pltpu.VMEM((batch, length, width), F32),
                pltpu.VMEM((batch, length, width), F32),
                pltpu.VMEM((batch, 5 * QB, QB), F32),
            ],
        ),
        out_shape=jax.ShapeDtypeStruct(joined.shape, BF16),
        input_output_aliases={7: 0} if aliased else {},
        compiler_params=pltpu.CompilerParams(vmem_limit_bytes=48 << 20),
        cost_estimate=pl.CostEstimate(
            flops=(row_to - row_from) * length * 400 * 8 * 256 * 20,
            bytes_accessed=(row_to - row_from) * length * triple * 4,
            transcendentals=0,
        ),
        name="attend_back",
    )(lows, vlens, starts, joined, grads, attended, logs, *aliased)


def normalise(values):
    centred = values - jnp.mean(values, axis=-1, keepdims=True)
    inverse = lax.rsqrt(jnp.mean(centred * centred, axis=-1, keepdims=True) + 1e-05)
    return centred * inverse, inverse


def pull_norm(scaled, hat, inverse):
    return inverse * (
        scaled
        - jnp.mean(scaled, axis=-1, keepdims=True)
        - hat * jnp.mean(scaled * hat, axis=-1, keepdims=True)
    )


PIECE = 256


def pieces(count):
    return [slice(at, min(at + PIECE, count)) for at in range(0, count, PIECE)]


def constant_spec(shape, *where):
    where = where or (0,) * len(shape)
    return pl.BlockSpec(shape, lambda *_: where)


def join_kernel(tokens_ref, gains_ref, weight_ref, joined_ref):
    for at in pieces(tokens_ref.shape[1]):
        hat, _ = normalise(tokens_ref[0, at].astype(F32))
        normed = (hat * gains_ref[0:1] + gains_ref[1:2]).astype(BF16)
        joined_ref[0, at] = dot(normed, weight_ref[...]).astype(BF16)


def join_tokens(tokens, gains, packed, tile=1024):
    rows, length, width = tokens.shape
    return pl.pallas_call(
        join_kernel,
        grid=(rows, length // tile),
        in_specs=[
            pl.BlockSpec((1, tile, width), lambda r, t: (r, t, 0)),
            constant_spec(gains.shape),
            constant_spec((width, 3 * width)),
        ],
        out_specs=pl.BlockSpec((1, tile, 3 * width), lambda r, t: (r, t, 0)),
        out_shape=jax.ShapeDtypeStruct((rows, length, 3 * width), BF16),
        compiler_params=pltpu.CompilerParams(vmem_limit_bytes=40 << 20),
        cost_estimate=pl.CostEstimate(
            flops=rows * length * width * width * 6, bytes_accessed=rows * length * width * 8, transcendentals=0
        ),
        name="join",
    )(tokens, gains, packed)


def mixed_kernel(attended_ref, tokens_ref, gains_ref, weight_ref, router_ref, hidden_ref, mixed_ref, logits_ref):
    hidden = tokens_ref[0].astype(F32) + dot(attended_ref[0], weight_ref[...])
    hidden_ref[0] = hidden
    hat, _ = normalise(hidden)
    mixed = (hat * gains_ref[2:3] + gains_ref[3:4]).astype(BF16)
    mixed_ref[0] = mixed
    logits_ref[0] = dot_nt(router_ref[...], mixed)


def mix_tokens(attended, tokens, gains, packed, router, offset, tile=1024):
    rows, span, width = attended.shape
    block = pl.BlockSpec((1, tile, width), lambda r, t: (r, t, 0))
    return pl.pallas_call(
        mixed_kernel,
        grid=(rows, span // tile),
        in_specs=[
            block,
            pl.BlockSpec((1, tile, width), lambda r, t: (r, t + offset // tile, 0)),
            constant_spec(gains.shape),
            constant_spec((width, width), 0, 3),
            constant_spec(router.shape),
        ],
        out_specs=[block, block, pl.BlockSpec((1, router.shape[0], tile), lambda r, t: (r, 0, t))],
        out_shape=[
            jax.ShapeDtypeStruct((rows, span, width), F32),
            jax.ShapeDtypeStruct((rows, span, width), BF16),
            jax.ShapeDtypeStruct((rows, router.shape[0], span), F32),
        ],
        compiler_params=pltpu.CompilerParams(vmem_limit_bytes=40 << 20),
        cost_estimate=pl.CostEstimate(
            flops=rows * span * width * width * 2, bytes_accessed=rows * span * width * 10, transcendentals=0
        ),
        name="mix",
    )(attended, tokens, gains, packed, router)


def pool_kernel(experts, scale, slots_ref, gates_ref, values_ref, out_ref):
    rows, places = values_ref.shape[0], values_ref.shape[1]
    sub = 16

    def step(s, _):
        here = pl.ds(pl.multiple_of(s * sub, sub), sub)
        gates = gates_ref[here, :].astype(BF16).astype(F32)
        values = [values_ref[r, here, :].astype(F32) for r in range(rows)]
        for e in range(experts):
            total = sum(gates[:, r * experts + e: r * experts + e + 1] * values[r] for r in range(rows))
            out_ref[0, e, here, :] = (scale * total).astype(BF16)
        return 0

    lax.fori_loop(0, places // sub, step, 0, unroll=8)


def pool_tokens(slots, gates, values, experts, scale):
    rows, span, width = values.shape
    owners = slots.shape[0]
    places = span // owners
    return pl.pallas_call(
        functools.partial(pool_kernel, experts, scale),
        grid_spec=pltpu.PrefetchScalarGridSpec(
            num_scalar_prefetch=1,
            grid=(owners,),
            in_specs=[
                pl.BlockSpec((places, gates.shape[1]), lambda i, slots: (slots[i], 0)),
                pl.BlockSpec((rows, places, width), lambda i, slots: (0, slots[i], 0)),
            ],
            out_specs=pl.BlockSpec((1, experts, places, width), lambda i, slots: (i, 0, 0, 0)),
        ),
        out_shape=jax.ShapeDtypeStruct((owners, experts, places, width), BF16),
        compiler_params=pltpu.CompilerParams(vmem_limit_bytes=40 << 20),
        cost_estimate=pl.CostEstimate(
            flops=rows * span * width * 1000, bytes_accessed=rows * span * width * 8, transcendentals=0
        ),
        name="pool",
    )(slots, gates, values)


CUBIC = 0.044715
SLOPE = math.sqrt(2.0 / math.pi)


def expert_kernel(steps, pooled_ref, weights_ref, result_ref, act_ref, slope_ref, total_ref):
    step = pl.program_id(0)
    blocks, places, width = pooled_ref.shape
    pooled = pooled_ref[...].reshape(blocks * places, width)
    pre = dot(pooled, weights_ref[0, 0])
    square = pre * pre
    bent = jnp.tanh(SLOPE * pre * (1.0 + CUBIC * square))
    half = 0.5 * (1.0 + bent)
    act = (pre * half).astype(BF16)
    act_ref[0] = act
    slope_ref[0] = half + 0.5 * pre * (1.0 - bent * bent) * (SLOPE * (1.0 + 3.0 * CUBIC * square))
    result = dot_nt(act, weights_ref[0, 1])

    @pl.when(step == 0)
    def _():
        total_ref[...] = result

    @pl.when(step > 0)
    def _():
        total_ref[...] += result

    @pl.when(step == steps - 1)
    def _():
        result_ref[...] = total_ref[...].astype(BF16).reshape(blocks, places, width)


def run_experts(pooled, weights):
    blocks, places, width = pooled.shape
    steps, _, _, tile = weights.shape
    count = blocks * places
    return pl.pallas_call(
        functools.partial(expert_kernel, steps),
        grid=(steps,),
        in_specs=[constant_spec(pooled.shape), pl.BlockSpec((1, 2, width, tile), lambda i: (i, 0, 0, 0))],
        out_specs=[
            constant_spec(pooled.shape),
            pl.BlockSpec((1, count, tile), lambda i: (i, 0, 0)),
            pl.BlockSpec((1, count, tile), lambda i: (i, 0, 0)),
        ],
        out_shape=[
            jax.ShapeDtypeStruct(pooled.shape, BF16),
            jax.ShapeDtypeStruct((steps, count, tile), BF16),
            jax.ShapeDtypeStruct((steps, count, tile), F32),
        ],
        scratch_shapes=[pltpu.VMEM((count, width), F32)],
        compiler_params=pltpu.CompilerParams(vmem_limit_bytes=40 << 20),
        cost_estimate=pl.CostEstimate(
            flops=count * width * tile * steps * 8, bytes_accessed=width * tile * steps * 8, transcendentals=0
        ),
        name="experts",
    )(pooled, weights)


def expert_back_kernel(steps, slots_ref, pooled_ref, grads_ref, result_ref, act_ref, slope_ref, weights_ref, back_ref, grad_ref, total_ref):
    step = pl.program_id(0)
    blocks, places, width = pooled_ref.shape
    count = blocks * places
    pooled = pooled_ref[...].reshape(count, width)
    grads = grads_ref[...].reshape(count, width)
    act = act_ref[0]
    grad_pre = (dot(grads, weights_ref[0, 1]) * slope_ref[0]).astype(BF16)
    grad_ref[0, 0] = dot_tn(pooled, grad_pre).astype(BF16)
    grad_ref[0, 1] = dot_tn(grads, act).astype(BF16)
    part = dot_nt(grad_pre, weights_ref[0, 0])

    @pl.when(step == 0)
    def _():
        total_ref[...] = part

    @pl.when(step > 0)
    def _():
        total_ref[...] += part

    @pl.when(step == steps - 1)
    def _():
        grad_pooled = total_ref[...].astype(BF16)
        back_ref[:, :places] = grad_pooled.reshape(blocks, places, width)
        result = result_ref[...].reshape(count, width)
        product = result.astype(F32) * grads.astype(F32) + grad_pooled.astype(F32) * pooled.astype(F32)
        high = product.astype(BF16)
        rest = (product - high.astype(F32)).astype(BF16)
        ones = jnp.ones((16, width), BF16)
        sums = dot_nt(ones, high) + dot_nt(ones, rest)
        top = sums.astype(BF16)
        low = (sums - top.astype(F32)).astype(BF16)
        for b in range(blocks):
            here = slice(b * places, b * places + places)
            fill = jnp.zeros((16, width - 2 * places), BF16)
            back_ref[b, places:] = jnp.concatenate([top[:, here], low[:, here], fill], axis=1)


def pull_experts(slots, pooled, grads, result, act, slope, weights):
    blocks, places, width = pooled.shape
    steps, _, _, tile = weights.shape
    count = blocks * places
    return pl.pallas_call(
        functools.partial(expert_back_kernel, steps),
        grid_spec=pltpu.PrefetchScalarGridSpec(
            num_scalar_prefetch=1,
            grid=(steps,),
            in_specs=[constant_spec(pooled.shape)] * 3
            + [pl.BlockSpec((1, count, tile), lambda i, slots: (i, 0, 0))] * 2
            + [pl.BlockSpec((1, 2, width, tile), lambda i, slots: (i, 0, 0, 0))],
            out_specs=[
                constant_spec((blocks, places + 16, width)),
                pl.BlockSpec((1, 2, width, tile), lambda i, slots: (slots[i], 0, 0, 0)),
            ],
            scratch_shapes=[pltpu.VMEM((count, width), F32)],
        ),
        out_shape=[
            jax.ShapeDtypeStruct((blocks, places + 16, width), BF16),
            jax.ShapeDtypeStruct(weights.shape, BF16),
        ],
        compiler_params=pltpu.CompilerParams(vmem_limit_bytes=40 << 20),
        cost_estimate=pl.CostEstimate(
            flops=count * width * tile * steps * 12, bytes_accessed=width * tile * steps * 8, transcendentals=0
        ),
        name="pull_experts",
    )(slots, pooled, grads, result, act, slope, weights)


def spread_kernel(group, count, slots_ref, gates_ref, grads_ref, hidden_ref, *rest):
    parts, (out_ref, change_ref, result_ref) = rest[:count], rest[-3:]
    for k in range(count):
        @pl.when(pl.program_id(0) == k)
        def _():
            result_ref[...] = parts[k][...]

    rows, places = grads_ref.shape[0], grads_ref.shape[1]
    experts = result_ref.shape[0]
    sub = 16
    columns = gates_ref.shape[1]

    def step(s, _):
        here = pl.ds(pl.multiple_of(s * sub, sub), sub)
        results = [result_ref[e, here, :].astype(F32) * group for e in range(experts)]
        gates = gates_ref[here, :].astype(BF16).astype(F32)
        lane = iota((sub, columns), 1)
        changes = jnp.zeros((sub, columns), F32)
        for r in range(rows):
            grads = grads_ref[r, here, :].astype(F32)
            for e in range(experts):
                both = jnp.sum(grads * results[e], axis=1, keepdims=True)
                changes = jnp.where(lane == r * experts + e, both, changes)
            total = sum(gates[:, r * experts + e: r * experts + e + 1] * results[e] for e in range(experts))
            out_ref[r, here, :] = (hidden_ref[r, here, :] + total.astype(BF16).astype(F32)).astype(BF16)
        change_ref[0, here, :] = changes
        return 0

    lax.fori_loop(0, places // sub, step, 0, unroll=8)


def slot_of(found):
    found = list(found)
    step = found[-1] - found[0]
    return lambda i, slots: slots[found[0] + i * step]


def spread_tokens(found, slots, gates, cotangent, hidden, group, held):
    rows, span, width = hidden.shape
    parts = list(found.values())
    experts, places, _ = parts[0].shape
    at = slot_of(found)
    block = pl.BlockSpec((rows, places, width), lambda i, slots: (0, at(i, slots), 0))
    columns = gates.shape[1]
    aliased = [] if held is None else [held]
    return pl.pallas_call(
        functools.partial(spread_kernel, group, len(parts)),
        grid_spec=pltpu.PrefetchScalarGridSpec(
            num_scalar_prefetch=1,
            grid=(len(parts),),
            in_specs=[pl.BlockSpec((places, columns), lambda i, slots: (at(i, slots), 0)), block, block]
            + [constant_spec(part.shape) for part in parts]
            + [pl.BlockSpec(memory_space=pltpu.HBM) for _ in aliased],
            out_specs=[block, pl.BlockSpec((1, places, columns), lambda i, slots: (i, 0, 0))],
            scratch_shapes=[pltpu.VMEM(parts[0].shape, BF16)],
        ),
        out_shape=[
            jax.ShapeDtypeStruct((rows, span, width), BF16),
            jax.ShapeDtypeStruct((len(parts), places, columns), F32),
        ],
        input_output_aliases={4 + len(parts): 0} if aliased else {},
        compiler_params=pltpu.CompilerParams(vmem_limit_bytes=58 << 20),
        cost_estimate=pl.CostEstimate(
            flops=len(parts) * rows * places * width * 5000, bytes_accessed=rows * places * width * 10, transcendentals=0
        ),
        name="spread",
    )(slots, gates, cotangent, hidden, *parts, *aliased)


def pull_kernel(first, count, slots_ref, gates_ref, change_ref, mixed_ref, hidden_ref, cotangent_ref, attended_ref, router_ref, gains_ref, weight_ref, *rest):
    parts, rest = rest[:count], rest[count:]
    out_ref, low_ref, router_grad_ref, project_ref, sums_ref, pooled_ref, logits_ref, grad_ref = rest[-8:]

    @pl.when(pl.program_id(0) == 0)
    def _():
        if first:
            router_grad_ref[...] = jnp.zeros_like(router_grad_ref)
            project_ref[...] = jnp.zeros_like(project_ref)
            sums_ref[...] = jnp.zeros_like(sums_ref)
        else:
            router_grad_ref[...] = rest[2][...]
            project_ref[...] = rest[3][...]
            sums_ref[...] = rest[4][...]

    for k in range(count):
        @pl.when(pl.program_id(0) == k)
        def _():
            pooled_ref[...] = parts[k][...]

    rows, places, width = mixed_ref.shape
    experts = pooled_ref.shape[0]
    sub = 16
    columns = gates_ref.shape[1]
    inner = jnp.zeros((places, columns), F32)
    for e in range(experts):
        pick = (iota((16, columns), 0) == 0) & (iota((16, columns), 1) % experts == e)
        pick = jnp.where(pick, 1.0, 0.0).astype(BF16)
        inner += dot_tn(pooled_ref[e, places:, :places], pick) + dot_tn(pooled_ref[e, places:, places: 2 * places], pick)

    def change(s, _):
        here = pl.ds(pl.multiple_of(s * sub, sub), sub)
        pooled = [pooled_ref[e, here, :].astype(F32) for e in range(experts)]
        lane = iota((sub, columns), 1)
        changes = jnp.zeros((sub, columns), F32)
        for r in range(rows):
            mixed = mixed_ref[r, here, :].astype(F32)
            for e in range(experts):
                both = jnp.sum(pooled[e] * mixed, axis=1, keepdims=True)
                changes = jnp.where(lane == r * experts + e, both, changes)
        logits_ref[here, :] = changes
        return 0

    lax.fori_loop(0, places // sub, change, 0, unroll=8)
    changes = (logits_ref[...] + change_ref[0]).astype(BF16).astype(F32)
    low = (gates_ref[...] * (changes - inner)).astype(BF16)
    for r in range(rows):
        grad_ref[r] = dot(low, router_ref[r])
        router_grad_ref[...] += dot_tn(low, mixed_ref[r])[r * experts: r * experts + experts]

    def spread(s, _):
        here = pl.ds(pl.multiple_of(s * sub, sub), sub)
        pooled = [pooled_ref[e, here, :].astype(F32) for e in range(experts)]
        gates = gates_ref[here, :].astype(BF16).astype(F32)
        for r in range(rows):
            grad_ref[r, here, :] = sum(
                (gates[:, r * experts + e: r * experts + e + 1] * pooled[e] for e in range(experts)),
                grad_ref[r, here, :],
            )
        return 0

    lax.fori_loop(0, places // sub, spread, 0, unroll=8)

    for r in range(rows):
        grads = grad_ref[r].astype(BF16).astype(F32)
        hat, inverse = normalise(hidden_ref[r])
        sums_ref[0:1] += jnp.sum(grads * hat, axis=0, keepdims=True)
        sums_ref[1:2] += jnp.sum(grads, axis=0, keepdims=True)
        total = cotangent_ref[r].astype(F32) + pull_norm(grads * gains_ref[2:3], hat, inverse)
        out_ref[r] = total
        total = total.astype(BF16)
        project_ref[...] += dot_tn(attended_ref[r], total)
        low_ref[r] = dot_nt(total, weight_ref[...]).astype(BF16)


def pull_slots(found, slots, gates, change, mixed, hidden, cotangent, attended, router, gains, packed, held):
    rows, span, width = mixed.shape
    parts = list(found.values())
    experts, depth, _ = parts[0].shape
    places = span // slots.shape[0]
    at = slot_of(found)
    block = pl.BlockSpec((rows, places, width), lambda i, slots: (0, at(i, slots), 0))
    columns = gates.shape[1]
    sums = [(experts, width), (width, width), (8, width)]
    ins = [
        pl.BlockSpec((places, columns), lambda i, slots: (at(i, slots), 0)),
        pl.BlockSpec((1, places, columns), lambda i, slots: (i, 0, 0)),
        block,
        block,
        block,
        block,
        constant_spec(router.shape),
        constant_spec(gains.shape),
        constant_spec((width, width), 0, 3),
    ] + [constant_spec(part.shape) for part in parts]
    aliases = {}
    if held is not None:
        aliases = {len(ins) + 1: 0, len(ins) + 2: 1}
        ins += [pl.BlockSpec(memory_space=pltpu.HBM)] * 2 + [constant_spec(shape) for shape in sums]
    return pl.pallas_call(
        functools.partial(pull_kernel, held is None, len(parts)),
        grid_spec=pltpu.PrefetchScalarGridSpec(
            num_scalar_prefetch=1,
            grid=(len(parts),),
            in_specs=ins,
            out_specs=[block, block] + [constant_spec(shape) for shape in sums],
            scratch_shapes=[
                pltpu.VMEM(parts[0].shape, BF16),
                pltpu.VMEM((places, columns), F32),
                pltpu.VMEM((rows, places, width), F32),
            ],
        ),
        out_shape=[jax.ShapeDtypeStruct((rows, span, width), F32), jax.ShapeDtypeStruct((rows, span, width), BF16)]
        + [jax.ShapeDtypeStruct(shape, F32) for shape in sums],
        input_output_aliases=aliases,
        compiler_params=pltpu.CompilerParams(vmem_limit_bytes=58 << 20),
        cost_estimate=pl.CostEstimate(
            flops=len(parts) * rows * places * width * width * 20,
            bytes_accessed=rows * places * width * 20,
            transcendentals=0,
        ),
        name="pull_slots",
    )(slots, gates, change, mixed, hidden, cotangent, attended, router, gains, packed, *parts, *(held or ()))


def project_kernel(grads_ref, tokens_ref, product_ref, sums_ref):
    @pl.when((pl.program_id(0) == 0) & (pl.program_id(1) == 0))
    def _():
        product_ref[...] = jnp.zeros_like(product_ref)
        sums_ref[...] = jnp.zeros_like(sums_ref)

    hat = normalise(tokens_ref[0].astype(F32))[0].astype(BF16)
    ones = jnp.ones((hat.shape[0], 8), BF16)
    product_ref[...] += dot_tn(hat, grads_ref[0])
    sums_ref[...] += dot_tn(ones, grads_ref[0])


def project_grads(grads, tokens, tile=1024):
    rows, length, width = tokens.shape
    shapes = [(width, 3 * width), (8, 3 * width)]
    return pl.pallas_call(
        project_kernel,
        grid=(rows, length // tile),
        in_specs=[
            pl.BlockSpec((1, tile, 3 * width), lambda r, t: (r, t, 0)),
            pl.BlockSpec((1, tile, width), lambda r, t: (r, t, 0)),
        ],
        out_specs=[constant_spec(shape) for shape in shapes],
        out_shape=[jax.ShapeDtypeStruct(shape, F32) for shape in shapes],
        compiler_params=pltpu.CompilerParams(vmem_limit_bytes=40 << 20),
        cost_estimate=pl.CostEstimate(
            flops=rows, bytes_accessed=rows, transcendentals=0
        ),
        name="project_grads",
    )(grads, tokens)


def tokens_kernel(grads_ref, tokens_ref, hidden_ref, gains_ref, weight_ref, *rest):
    out_ref = rest[-1]
    for at in pieces(tokens_ref.shape[1]):
        hat, inverse = normalise(tokens_ref[0, at].astype(F32))
        grads = dot_nt(grads_ref[0, at], weight_ref[...])
        out_ref[0, at] = hidden_ref[0, at] + pull_norm(grads * gains_ref[0:1], hat, inverse)


def pull_tokens(grads, tokens, hidden, gains, packed, row_from, row_to, held=None, tile=1024):
    rows, length, width = tokens.shape
    block = pl.BlockSpec((1, tile, width), lambda r, t: (r + row_from, t, 0))
    aliased = [] if held is None else [held]
    return pl.pallas_call(
        tokens_kernel,
        grid=(row_to - row_from, length // tile),
        in_specs=[
            pl.BlockSpec((1, tile, 3 * width), lambda r, t: (r + row_from, t, 0)),
            block,
            block,
            constant_spec(gains.shape),
            constant_spec((width, 3 * width)),
        ]
        + [pl.BlockSpec(memory_space=pltpu.HBM) for _ in aliased],
        out_specs=block,
        out_shape=jax.ShapeDtypeStruct((rows, length, width), F32),
        input_output_aliases={5: 0} if aliased else {},
        compiler_params=pltpu.CompilerParams(vmem_limit_bytes=58 << 20),
        cost_estimate=pl.CostEstimate(
            flops=(row_to - row_from) * length * width * width * 20,
            bytes_accessed=(row_to - row_from) * length * width * 16,
            transcendentals=0,
        ),
        name="pull_tokens",
    )(grads, tokens, hidden, gains, packed, *aliased)


LAG = 0


def ring_order(size):
    inner = 2 if size % 2 == 0 and size > 2 else 1
    outer = size // inner
    up = [z * inner for z in range(outer)]
    if inner == 1:
        return up
    return up + [z * inner + 1 for z in reversed(range(outer))]


def shift(value, order, step):
    count = len(order)
    return lax.ppermute(value, "dp", [(order[i], order[(i + step) % count]) for i in range(count)])


def flip(value, bit, axis="fsdp"):
    count = lax.axis_size(axis)
    return lax.ppermute(value, axis, [(i, i ^ bit) for i in range(count)])


def turn(value, step, axis="dp"):
    count = lax.axis_size(axis)
    return lax.ppermute(value, axis, [(i, (i + step) % count) for i in range(count)])


def take(values, index):
    starts = (index,) + (jnp.uint32(0),) * (values.ndim - 1)
    return lax.dynamic_slice(values, starts, (1,) + values.shape[1:])[0]


def put(values, value, index):
    return lax.dynamic_update_slice(values, value[None], (index,) + (jnp.uint32(0),) * value.ndim)


def add(a, b):
    return (a.astype(F32) + b.astype(F32)).astype(BF16)


def together(*values):
    return lax.optimization_barrier(values)


class Ring:
    def __init__(self, value, order):
        self.order, self.done = order, 0
        self.ahead = self.behind = value

    def left(self):
        return self.done < len(self.order) // 2

    def after(self, *values):
        self.ahead, self.behind, *_ = together(self.ahead, self.behind, *values)

    def step(self, *beside):
        count = len(self.order)
        self.done += 1
        slot = count - self.done
        ahead, behind = self.ahead, self.behind
        middle = 2 * self.done == count and ahead.shape[0] % 2 == 0
        if middle:
            half = ahead.shape[0] // 2
            ahead, behind = ahead[:half], behind[half:]
        ahead = shift(ahead, self.order, 1)
        if 2 * self.done < count or middle:
            behind = shift(behind, self.order, -1)
        ahead, behind, *beside = together(ahead, behind, *beside)
        self.ahead, self.behind = ahead, behind
        if middle:
            return {slot: jnp.concatenate([ahead, behind], axis=0)}, beside
        return {slot: ahead, self.done: behind} if 2 * self.done < count else {slot: ahead}, beside


def gather_all(value, steps):
    pair = pair_of(lax.axis_size("dp"))
    lines = lax.axis_size("dp") // pair
    size = lax.axis_size("fsdp")
    here = lax.axis_index("fsdp")

    def both(value, bit, axis, index):
        other = flip(value, bit, axis)
        upper = (index & bit) != 0
        return jnp.stack([jnp.where(upper, other, value), jnp.where(upper, value, other)])

    value = both(value, 1, "dp", lax.axis_index("dp")) if pair == 2 else value[None]
    whole = put(jnp.zeros((lines,) + value.shape, value.dtype), value, steps[0])
    for k in range(1, lines):
        whole = put(whole, turn(value, -k * pair), steps[k])
    whole = whole.reshape((lines * pair, 1) + value.shape[1:])
    bit = size // 2
    while bit:
        whole = both(whole, bit, "fsdp", here)
        whole = jnp.moveaxis(whole, 0, 2)
        whole = whole.reshape((lines * pair, -1) + value.shape[1:])
        bit //= 2
    return whole


def scatter_all(values, steps, work):
    owners, size = lax.axis_size("dp"), lax.axis_size("fsdp")
    bits = size.bit_length() - 1
    here = lax.axis_index("fsdp")
    width = values.shape[1]
    pair = pair_of(owners)
    work = list(work)

    def half(held, axis, upper, bit, name):
        low, high = (lax.index_in_dim(held, i, axis, keepdims=False) for i in (0, 1))
        came = flip(jnp.where(upper, low, high), bit, name)
        if work:
            came, = work.pop(0)(came)
        return add(jnp.where(upper, high, low), came)

    held = values.reshape((owners // pair, pair) + (2,) * bits + (-1, width))
    for level in range(bits):
        held = half(held, bits + 1 - level, ((here >> level) & 1) != 0, 1 << level, "fsdp")
    held = half(held, 1, (lax.axis_index("dp") & 1) != 0, 1, "dp") if pair == 2 else held[:, 0]
    came = [turn(take(held, steps[k]), k * pair) for k in range(1, owners // pair)]
    while work:
        came = work.pop(0)(*came)
    return sum((value.astype(F32) for value in came), take(held, steps[0]).astype(F32))


def pair_of(owners):
    return 2 if owners % 2 == 0 else 1


def exchange(values):
    return jnp.stack([values[0]] + [flip(values[k], k) for k in range(1, values.shape[0])])


def per_device(
    tokens,
    segment_ids,
    pad_tokens,
    cotangent,
    project_in,
    project_out,
    router_weight,
    expert_in,
    expert_out,
    first_gain,
    first_bias,
    second_gain,
    second_bias,
):
    blocks_here, rows, length, width = tokens.shape
    tokens = tokens.reshape(rows, length, width)
    cotangent = cotangent.reshape(rows, length, width)
    segments = segment_ids.reshape(rows, length)
    group = pad_tokens.shape[1]
    owners = lax.axis_size("dp")
    experts = router_weight.shape[1]
    order = ring_order(owners)
    data_index = lax.axis_index("dp")
    expert_index = lax.axis_index("fsdp")
    places = length // owners

    pair = pair_of(owners)
    lines = owners // pair
    ring = np.array([[order[(order.index(d) + k) % owners] for k in range(owners)] for d in range(owners)], np.int32)
    place = np.array(
        [[(o % pair ^ d % pair) * lines + (o // pair - d // pair) % lines for o in ring[d]] for d in range(owners)],
        np.int32,
    )
    line = np.array([[(d // pair + k) % lines for k in range(lines)] for d in range(owners)], np.int32)
    tables = np.concatenate([ring, place, line], axis=1)
    tables = lax.dynamic_slice(
        jnp.asarray(tables), (data_index.astype(jnp.uint32), jnp.uint32(0)), (1, tables.shape[1])
    )[0]
    slots, shares = tables[:owners], tables[owners: 2 * owners]
    spots = [tables[k].astype(jnp.uint32) for k in range(owners)]
    steps = [tables[2 * owners + k].astype(jnp.uint32) for k in range(lines)]

    vectors = jnp.stack([first_gain, first_bias, second_gain, second_bias], axis=1)
    small = jnp.concatenate([router_weight, vectors], axis=1)
    small = jnp.pad(small, ((0, 0), (0, 128 - small.shape[1])))
    packed = jnp.concatenate([project_in, project_out, small], axis=1)
    weights = jnp.stack([expert_in[0], expert_out[0].T])
    packed = gather_all(packed, steps)
    packed = packed.reshape(width, packed.shape[-1])
    packed, weights = together(packed, weights)
    kept = {0: weights}
    weights = Ring(weights, order)
    small = packed[:, 4 * width:].T
    mine = (jnp.arange(experts)[:, None] ^ jnp.arange(experts)[None, :]) == expert_index
    router = jnp.sum(jnp.where(mine[:, :, None], small[None, :experts], 0), axis=1).astype(BF16)
    spread_router = jnp.stack(
        [jnp.pad(router, ((r * experts, (rows - 1 - r) * experts), (0, 0))) for r in range(rows)]
    )
    gains = jnp.pad(small[experts: experts + 4].astype(F32), ((0, 4), (0, 0)))

    own_pads = lax.dynamic_slice_in_dim(pad_tokens[0], data_index * rows, rows, 0)
    vlens = (length - own_pads).astype(jnp.int32)
    starts = jnp.zeros_like(segments)
    for doc in range(1, 4):
        before = jnp.sum((segments < doc).astype(jnp.int32), axis=1, keepdims=True)
        starts = jnp.where(segments == doc, before, starts)
    starts = starts.reshape(rows, length // QB, QB)
    lows = starts[:, :, 0] // QB

    def meanwhile(value):
        if not weights.left():
            return value
        found, (value,) = weights.step(value)
        kept.update(found)
        return value

    joined = meanwhile(join_tokens(tokens, gains, packed))
    attended, logs = attn_fwd(joined, starts, lows, vlens, 1)
    attended = meanwhile(attended)
    hidden, mixed, logits = mix_tokens(
        attended, tokens, gains, packed, jnp.pad(router, ((0, 16 - experts), (0, 0))), 0
    )
    logits = meanwhile(logits)[:, :experts]
    valid = (jnp.arange(length)[None, :] < vlens[:, None])[:, None, :]
    highest = jnp.max(jnp.where(valid, logits, NEGATIVE), axis=0)
    total = jnp.sum(jnp.where(valid, jnp.exp(logits - highest), 0.0), axis=0)
    stats = jnp.stack([highest, total])[None]
    if pair == 2:
        stats = jnp.concatenate([stats, flip(stats, 1, "dp")])
    stats = jnp.concatenate([stats] + [turn(stats, k * pair) for k in range(1, lines)])
    tops = jnp.max(stats[:, 0], axis=0)
    total = jnp.sum(stats[:, 1] * jnp.exp(stats[:, 0] - tops), axis=0)
    gates = jnp.where(valid, jnp.exp(jnp.where(valid, logits - tops, NEGATIVE)) / total, 0.0)
    gates = gates.reshape(rows * experts, length).T
    pooled = meanwhile(pool_tokens(slots, gates, mixed, experts, 1.0))
    while weights.left():
        kept.update(weights.step()[0])
    weights = jnp.stack([kept[k] for k in range(owners)])
    grads = pool_tokens(slots, gates, cotangent, experts, float(group))

    half = experts // 2
    first = [(pooled[:, :half], 1), (pooled[:, half:], -1)]
    second = [(grads[:, :half], 1), (grads[:, half:], -1)]
    held = [part[-way % owners] for part, way in first]
    later = [part[-way % owners] for part, way in second]
    for step in range(owners - 1 + LAG):
        if step < owners - 1:
            came = [shift(value, order, way) for value, (_, way) in zip(held, first)]
            *came, one, two = together(*came, *later)
            later = [one, two]
            held = [add(value, part[-way * (2 + step) % owners]) for value, (part, way) in zip(came, first)]
        back = step - LAG
        if back >= 0:
            came = [shift(value, order, way) for value, (_, way) in zip(later, second)]
            later = [add(value, part[-way * (2 + back) % owners]) for value, (part, way) in zip(came, second)]
    pooled = exchange(jnp.concatenate(held, axis=0))
    result, act, slope = run_experts(pooled, weights)
    grads = exchange(jnp.concatenate(later, axis=0))
    grad_pooled, grad_weights = pull_experts(shares, pooled, grads, result, act, slope, weights)

    result = exchange(result)
    back = exchange(grad_pooled)

    def pull(found, change, out):
        return pull_slots(
            found, slots, gates, change, mixed, hidden, cotangent, attended, spread_router, gains, packed, out
        )

    def spread(found, out):
        return spread_tokens(found, slots, gates, cotangent, hidden, group, out)

    turns = owners // 2
    first, second = Ring(result, order), Ring(back, order)
    found, (grad_weights,) = first.step(grad_weights)
    groups, arrived = [{0: result}, found], [{0: back}]
    out, pulled, changes = None, None, []
    for step in range(turns + 1):
        second.after(*groups[-1].values())
        work = []
        out, change = spread(groups[step], out)
        work = [out, change]
        if step > 0:
            pulled = pull(arrived[step - 1], changes[step - 1], pulled)
            work += pulled
        if first.left():
            found, work = first.step(*work)
            groups.append(found)
        if second.left():
            found, work = second.step(*work)
            arrived.append(found)
        out, change, *pulled = work
        pulled = pulled or None
        changes.append(change)
    layer_out = out
    pulled = pull(arrived[turns], changes[turns], pulled)
    grad_hidden, grad_attended, router_grad, grad_proj_out, sums_two = pulled
    grad_attended, grad_weights = together(grad_attended, grad_weights)
    split = rows - max(1, rows // 4)
    if pair == 2:
        came = flip(grad_weights[lines:], 1, "dp")
    grads = attn_bwd(joined, grad_attended, attended, logs, starts, lows, vlens, 0, split)
    grad_weights = grad_weights[:lines]
    if pair == 2:
        came, grads = together(came, grads)
        grad_weights = add(grad_weights, came)
    came = [turn(grad_weights[k], k * pair) for k in range(1, lines)]
    grads = attn_bwd(joined, grad_attended, attended, logs, starts, lows, vlens, split, rows, grads)
    product, sums_one = project_grads(grads, tokens)
    product, *came = together(product, *came)
    grad_weights = sum((value.astype(F32) for value in came), grad_weights[0].astype(F32))
    full_in = packed[:, : 3 * width].astype(F32)
    sums_one = sums_one[:1]
    grad_proj_in = gains[0][:, None] * product + gains[1][:, None] * sums_one
    sums_one = jnp.stack([jnp.sum(full_in * product, axis=1), jnp.sum(full_in * sums_one, axis=1)])
    router_grad = jnp.sum(jnp.where(mine[:, :, None], router_grad[None], 0.0), axis=1)

    late = jnp.concatenate([router_grad, sums_one, sums_two[:2]], axis=0).T
    late = jnp.pad(late, ((0, 0), (0, 128 - late.shape[1])))
    reduced = jnp.concatenate([grad_proj_in, grad_proj_out, late], axis=1).astype(BF16)
    made = {"grad": None}

    def rows_beside(start, stop):
        def run(*came):
            made["grad"] = pull_tokens(grads, tokens, grad_hidden, gains, packed, start, stop, made["grad"])
            *came, made["grad"] = together(*came, made["grad"])
            return came

        return run

    middle = rows - max(1, rows // 4)
    work = [lambda *came: came, rows_beside(0, middle), rows_beside(middle, rows)]
    reduced = scatter_all(reduced, steps, work)
    tokens_grad = made["grad"]
    late = reduced[:, 4 * width:]
    return (
        layer_out[None],
        tokens_grad[None],
        reduced[:, : 3 * width],
        reduced[:, 3 * width: 4 * width],
        late[:, :experts],
        grad_weights[0][None],
        grad_weights[1].T[None],
        late[:, experts],
        late[:, experts + 1],
        late[:, experts + 2],
        late[:, experts + 3],
    )


def solution(mesh):
    in_specs = (
        P("fsdp", "dp", None, None),
        P("fsdp", "dp", None),
        P("fsdp", None),
        P("fsdp", "dp", None, None),
        P(("dp", "fsdp"), None),
        P(("dp", "fsdp"), None),
        P(("dp", "fsdp"), None),
        P("fsdp", None, "dp"),
        P("fsdp", "dp", None),
        P(("dp", "fsdp")),
        P(("dp", "fsdp")),
        P(("dp", "fsdp")),
        P(("dp", "fsdp")),
    )
    out_specs = (
        P("fsdp", "dp", None, None),
        P("fsdp", "dp", None, None),
        P(("dp", "fsdp"), None),
        P(("dp", "fsdp"), None),
        P(("dp", "fsdp"), None),
        P("fsdp", None, "dp"),
        P("fsdp", "dp", None),
        P(("dp", "fsdp")),
        P(("dp", "fsdp")),
        P(("dp", "fsdp")),
        P(("dp", "fsdp")),
    )
    return jax.shard_map(
        per_device, mesh=mesh, in_specs=in_specs, out_specs=out_specs, check_vma=False
    )
```

```python
import functools, math
import jax
import jax.numpy as jnp
import numpy as np
from jax import lax
from jax.experimental import pallas as pl
from jax.experimental.pallas import tpu as pltpu
from jax.sharding import PartitionSpec as P

NEGATIVE = -1e30
QB = 128
F32 = jnp.float32
BF16 = jnp.bfloat16
NT = (((1,), (1,)), ((), ()))
TN = (((0,), (0,)), ((), ()))


def dot(a, b):
    return jnp.dot(a, b, preferred_element_type=F32)


def dot_nt(a, b):
    return lax.dot_general(a, b, NT, preferred_element_type=F32)


def dot_tn(a, b):
    return lax.dot_general(a, b, TN, preferred_element_type=F32)


def iota(shape, axis):
    return lax.broadcasted_iota(jnp.int32, shape, axis)


def split_heads(x):
    low = iota(x.shape, 1) < 64
    zero = jnp.zeros_like(x)
    return jnp.concatenate([jnp.where(low, x, zero), jnp.where(low, zero, x)], axis=0)


def join_heads(x):
    half = x.shape[0] // 2
    low = iota((half, x.shape[1]), 1) < 64
    return jnp.where(low, x[:half], x[half:])


def attn_fwd_kernel(width, batch, count, lo_ref, vlen_ref, start_ref, joined_ref, out_ref, log_ref, bias_ref):
    row = pl.program_id(0) * batch

    def block(qb, _):
        lo = functools.reduce(jnp.minimum, [lo_ref[row + r, qb] for r in range(batch)])
        base = pl.multiple_of(qb * QB, QB)
        first = pl.multiple_of(lo * QB, QB)
        own = pl.ds(base, QB)

        def variant(blocks):
            span = blocks * QB
            keys = pl.ds(first, span)
            i = base + iota((QB, QB), 0)
            bias = []
            for r in range(batch):
                begins = jnp.broadcast_to(start_ref[r, pl.ds(qb, 1), :], (QB, QB)).T
                for b in range(blocks):
                    j = first + b * QB + iota((QB, QB), 1)
                    ok = ((j >= begins) & (j <= i) & (j < vlen_ref[row + r])) | (j == i)
                    bias_ref[r, :, b * QB:(b + 1) * QB] = jnp.where(ok, 0.0, NEGATIVE)
                bias.append(jnp.concatenate([bias_ref[r, :, :span]] * 2, axis=0))
            work = [(r, lane) for r in range(batch) for lane in range(0, width, 128)]
            query = [split_heads(joined_ref[r, own, pl.ds(at, 128)] * jnp.asarray(0.125, BF16)) for r, at in work]
            scores = [dot_nt(q, joined_ref[r, keys, pl.ds(width + at, 128)]) for q, (r, at) in zip(query, work)]
            scores = [s + bias[r] for s, (r, _) in zip(scores, work)]
            tops = [jnp.max(s, axis=1, keepdims=True) for s in scores]
            raised = [jnp.exp(s - top) for s, top in zip(scores, tops)]
            totals = [jnp.sum(p, axis=1, keepdims=True) for p in raised]
            out = [
                dot(p.astype(BF16), joined_ref[r, keys, pl.ds(2 * width + at, 128)]) for p, (r, at) in zip(raised, work)
            ]
            for o, total, (r, at) in zip(out, totals, work):
                out_ref[r, own, pl.ds(at, 128)] = join_heads(o * (1.0 / total)).astype(BF16)
            lane = iota((QB, QB), 1)
            for r in range(batch):
                tile = jnp.zeros((QB, QB), F32)
                for top, total, (other, at) in zip(tops, totals, work):
                    if other == r:
                        log = top + jnp.log(total)
                        tile = jnp.where(lane == at // 64, log[:QB], tile)
                        tile = jnp.where(lane == at // 64 + 1, log[QB:], tile)
                log_ref[r, pl.ds(qb, 1)] = tile.T[None, : log_ref.shape[2]]

        for blocks in range(1, 6):
            pl.when(qb - lo + 1 == blocks)(functools.partial(variant, blocks))
        return 0

    lax.fori_loop(0, count, block, 0)


def attn_fwd(joined, starts, lows, vlens, batch=2):
    rows, length, triple = joined.shape
    width = triple // 3
    count = length // QB
    return pl.pallas_call(
        functools.partial(attn_fwd_kernel, width, batch, count),
        grid_spec=pltpu.PrefetchScalarGridSpec(
            num_scalar_prefetch=2,
            grid=(rows // batch,),
            in_specs=[
                pl.BlockSpec((batch, count, QB), lambda r, *_: (r, 0, 0)),
                pl.BlockSpec((batch, length, triple), lambda r, *_: (r, 0, 0)),
            ],
            out_specs=[
                pl.BlockSpec((batch, length, width), lambda r, *_: (r, 0, 0)),
                pl.BlockSpec((batch, count, width // 64, QB), lambda r, *_: (r, 0, 0, 0)),
            ],
            scratch_shapes=[pltpu.VMEM((batch, QB, 5 * QB), F32)],
        ),
        out_shape=[
            jax.ShapeDtypeStruct((rows, length, width), BF16),
            jax.ShapeDtypeStruct((rows, count, width // 64, QB), F32),
        ],
        compiler_params=pltpu.CompilerParams(vmem_limit_bytes=48 << 20),
        cost_estimate=pl.CostEstimate(
            flops=rows * length * 400 * 8 * 256 * 4, bytes_accessed=rows * length * triple * 2, transcendentals=0
        ),
        name="attend",
    )(lows, vlens, starts, joined)


def attn_bwd_kernel(width, row_from, batch, count, lo_ref, vlen_ref, start_ref, joined_ref, grad_ref, attended_ref, log_ref, *rest):
    out_ref, dk_ref, dv_ref, bias_ref = rest[-4:]
    row = pl.program_id(0) * batch + row_from
    dk_ref[...] = jnp.zeros_like(dk_ref)
    dv_ref[...] = jnp.zeros_like(dv_ref)

    def block(qb, _):
        lo = functools.reduce(jnp.minimum, [lo_ref[row + r, qb] for r in range(batch)])
        base = pl.multiple_of(qb * QB, QB)
        first = pl.multiple_of(lo * QB, QB)
        own = pl.ds(base, QB)

        def variant(blocks):
            span = blocks * QB
            keys = pl.ds(first, span)
            i = base + iota((QB, QB), 1)
            pick = jnp.where(iota((16, width), 1) // 64 == iota((16, width), 0), 1.0, 0.0).astype(BF16)
            bias, sums = [], []
            for r in range(batch):
                begins = start_ref[r, pl.ds(qb, 1), :]
                for b in range(blocks):
                    j = first + b * QB + iota((QB, QB), 0)
                    ok = ((j >= begins) & (j <= i) & (j < vlen_ref[row + r])) | (j == i)
                    bias_ref[r, b * QB:(b + 1) * QB, :] = jnp.where(ok, 0.0, NEGATIVE)
                bias.append(jnp.concatenate([bias_ref[r, :span, :]] * 2, axis=1))
                product = grad_ref[r, own, :].astype(F32) * attended_ref[r, own, :].astype(F32)
                high = product.astype(BF16)
                sums.append(dot_nt(pick, high) + dot_nt(pick, (product - high.astype(F32)).astype(BF16)))
            work = [(r, lane) for r in range(batch) for lane in range(0, width, 128)]
            query = [split_heads(joined_ref[r, own, pl.ds(at, 128)] * jnp.asarray(0.125, BF16)) for r, at in work]
            grads = [split_heads(grad_ref[r, own, pl.ds(at, 128)]) for r, at in work]
            prob, moved = [], []
            for q, g, (r, at) in zip(query, grads, work):
                head = at // 64
                log = log_ref[r, qb]
                log = jnp.concatenate([log[head: head + 1], log[head + 1: head + 2]], axis=1)
                total = jnp.concatenate([sums[r][head: head + 1], sums[r][head + 1: head + 2]], axis=1)
                scores = dot_nt(joined_ref[r, keys, pl.ds(width + at, 128)], q)
                change = dot_nt(joined_ref[r, keys, pl.ds(2 * width + at, 128)], g)
                p = jnp.exp(scores + bias[r] - log)
                prob.append(p.astype(BF16))
                moved.append((p * (change - total)).astype(BF16))
            for p, g, (r, at) in zip(prob, grads, work):
                dv_ref[r, keys, pl.ds(at, 128)] += dot(p, g)
            for m, q, (r, at) in zip(moved, query, work):
                dk_ref[r, keys, pl.ds(at, 128)] += dot(m, q)
            back = [dot_tn(m, joined_ref[r, keys, pl.ds(width + at, 128)]) for m, (r, at) in zip(moved, work)]
            for b, (r, at) in zip(back, work):
                out_ref[r, own, pl.ds(at, 128)] = (join_heads(b) * 0.125).astype(BF16)

        for blocks in range(1, 6):
            pl.when(qb - lo + 1 == blocks)(functools.partial(variant, blocks))
        return 0

    lax.fori_loop(0, count, block, 0)
    out_ref[:, :, width: 2 * width] = dk_ref[...].astype(BF16)
    out_ref[:, :, 2 * width:] = dv_ref[...].astype(BF16)


def attn_bwd(joined, grads, attended, logs, starts, lows, vlens, row_from, row_to, held=None, batch=1):
    rows, length, triple = joined.shape
    width = triple // 3
    count = length // QB
    aliased = [] if held is None else [held]
    skip = row_from // batch
    wide = pl.BlockSpec((batch, length, triple), lambda r, *_: (r + skip, 0, 0))
    slim = pl.BlockSpec((batch, length, width), lambda r, *_: (r + skip, 0, 0))
    return pl.pallas_call(
        functools.partial(attn_bwd_kernel, width, row_from, batch, count),
        grid_spec=pltpu.PrefetchScalarGridSpec(
            num_scalar_prefetch=2,
            grid=((row_to - row_from) // batch,),
            in_specs=[
                pl.BlockSpec((batch, count, QB), lambda r, *_: (r + skip, 0, 0)),
                wide,
                slim,
                slim,
                pl.BlockSpec((batch,) + logs.shape[1:], lambda r, *_: (r + skip, 0, 0, 0)),
            ]
            + [pl.BlockSpec(memory_space=pltpu.HBM) for _ in aliased],
            out_specs=wide,
            scratch_shapes=[
                pltpu.VMEM((batch, length, width), F32),
                pltpu.VMEM((batch, length, width), F32),
                pltpu.VMEM((batch, 5 * QB, QB), F32),
            ],
        ),
        out_shape=jax.ShapeDtypeStruct(joined.shape, BF16),
        input_output_aliases={7: 0} if aliased else {},
        compiler_params=pltpu.CompilerParams(vmem_limit_bytes=48 << 20),
        cost_estimate=pl.CostEstimate(
            flops=(row_to - row_from) * length * 400 * 8 * 256 * 20,
            bytes_accessed=(row_to - row_from) * length * triple * 4,
            transcendentals=0,
        ),
        name="attend_back",
    )(lows, vlens, starts, joined, grads, attended, logs, *aliased)


def normalise(values):
    centred = values - jnp.mean(values, axis=-1, keepdims=True)
    inverse = lax.rsqrt(jnp.mean(centred * centred, axis=-1, keepdims=True) + 1e-05)
    return centred * inverse, inverse


def pull_norm(scaled, hat, inverse):
    return inverse * (
        scaled
        - jnp.mean(scaled, axis=-1, keepdims=True)
        - hat * jnp.mean(scaled * hat, axis=-1, keepdims=True)
    )


PIECE = 256


def pieces(count):
    return [slice(at, min(at + PIECE, count)) for at in range(0, count, PIECE)]


def constant_spec(shape, *where):
    where = where or (0,) * len(shape)
    return pl.BlockSpec(shape, lambda *_: where)


def join_kernel(tokens_ref, gains_ref, weight_ref, joined_ref):
    for at in pieces(tokens_ref.shape[1]):
        hat, _ = normalise(tokens_ref[0, at].astype(F32))
        normed = (hat * gains_ref[0:1] + gains_ref[1:2]).astype(BF16)
        joined_ref[0, at] = dot(normed, weight_ref[...]).astype(BF16)


def join_tokens(tokens, gains, packed, tile=1024):
    rows, length, width = tokens.shape
    return pl.pallas_call(
        join_kernel,
        grid=(rows, length // tile),
        in_specs=[
            pl.BlockSpec((1, tile, width), lambda r, t: (r, t, 0)),
            constant_spec(gains.shape),
            constant_spec((width, 3 * width)),
        ],
        out_specs=pl.BlockSpec((1, tile, 3 * width), lambda r, t: (r, t, 0)),
        out_shape=jax.ShapeDtypeStruct((rows, length, 3 * width), BF16),
        compiler_params=pltpu.CompilerParams(vmem_limit_bytes=40 << 20),
        cost_estimate=pl.CostEstimate(
            flops=rows * length * width * width * 6, bytes_accessed=rows * length * width * 8, transcendentals=0
        ),
        name="join",
    )(tokens, gains, packed)


def mixed_kernel(attended_ref, tokens_ref, gains_ref, weight_ref, router_ref, hidden_ref, mixed_ref, logits_ref):
    hidden = tokens_ref[0].astype(F32) + dot(attended_ref[0], weight_ref[...])
    hidden_ref[0] = hidden
    hat, _ = normalise(hidden)
    mixed = (hat * gains_ref[2:3] + gains_ref[3:4]).astype(BF16)
    mixed_ref[0] = mixed
    logits_ref[0] = dot_nt(router_ref[...], mixed)


def mix_tokens(attended, tokens, gains, packed, router, offset, tile=1024):
    rows, span, width = attended.shape
    block = pl.BlockSpec((1, tile, width), lambda r, t: (r, t, 0))
    return pl.pallas_call(
        mixed_kernel,
        grid=(rows, span // tile),
        in_specs=[
            block,
            pl.BlockSpec((1, tile, width), lambda r, t: (r, t + offset // tile, 0)),
            constant_spec(gains.shape),
            constant_spec((width, width), 0, 3),
            constant_spec(router.shape),
        ],
        out_specs=[block, block, pl.BlockSpec((1, router.shape[0], tile), lambda r, t: (r, 0, t))],
        out_shape=[
            jax.ShapeDtypeStruct((rows, span, width), F32),
            jax.ShapeDtypeStruct((rows, span, width), BF16),
            jax.ShapeDtypeStruct((rows, router.shape[0], span), F32),
        ],
        compiler_params=pltpu.CompilerParams(vmem_limit_bytes=40 << 20),
        cost_estimate=pl.CostEstimate(
            flops=rows * span * width * width * 2, bytes_accessed=rows * span * width * 10, transcendentals=0
        ),
        name="mix",
    )(attended, tokens, gains, packed, router)


def pool_kernel(experts, scale, slots_ref, gates_ref, values_ref, out_ref):
    rows, places = values_ref.shape[0], values_ref.shape[1]
    sub = 16

    def step(s, _):
        here = pl.ds(pl.multiple_of(s * sub, sub), sub)
        gates = gates_ref[here, :].astype(BF16).astype(F32)
        values = [values_ref[r, here, :].astype(F32) for r in range(rows)]
        for e in range(experts):
            total = sum(gates[:, r * experts + e: r * experts + e + 1] * values[r] for r in range(rows))
            out_ref[0, e, here, :] = (scale * total).astype(BF16)
        return 0

    lax.fori_loop(0, places // sub, step, 0, unroll=8)


def pool_tokens(slots, gates, values, experts, scale):
    rows, span, width = values.shape
    owners = slots.shape[0]
    places = span // owners
    return pl.pallas_call(
        functools.partial(pool_kernel, experts, scale),
        grid_spec=pltpu.PrefetchScalarGridSpec(
            num_scalar_prefetch=1,
            grid=(owners,),
            in_specs=[
                pl.BlockSpec((places, gates.shape[1]), lambda i, slots: (slots[i], 0)),
                pl.BlockSpec((rows, places, width), lambda i, slots: (0, slots[i], 0)),
            ],
            out_specs=pl.BlockSpec((1, experts, places, width), lambda i, slots: (i, 0, 0, 0)),
        ),
        out_shape=jax.ShapeDtypeStruct((owners, experts, places, width), BF16),
        compiler_params=pltpu.CompilerParams(vmem_limit_bytes=40 << 20),
        cost_estimate=pl.CostEstimate(
            flops=rows * span * width * 1000, bytes_accessed=rows * span * width * 8, transcendentals=0
        ),
        name="pool",
    )(slots, gates, values)


CUBIC = 0.044715
SLOPE = math.sqrt(2.0 / math.pi)


def expert_kernel(steps, pooled_ref, weights_ref, result_ref, act_ref, slope_ref, total_ref):
    step = pl.program_id(0)
    blocks, places, width = pooled_ref.shape
    pooled = pooled_ref[...].reshape(blocks * places, width)
    pre = dot(pooled, weights_ref[0, 0])
    square = pre * pre
    bent = jnp.tanh(SLOPE * pre * (1.0 + CUBIC * square))
    half = 0.5 * (1.0 + bent)
    act = (pre * half).astype(BF16)
    act_ref[0] = act
    slope_ref[0] = half + 0.5 * pre * (1.0 - bent * bent) * (SLOPE * (1.0 + 3.0 * CUBIC * square))
    result = dot_nt(act, weights_ref[0, 1])

    @pl.when(step == 0)
    def _():
        total_ref[...] = result

    @pl.when(step > 0)
    def _():
        total_ref[...] += result

    @pl.when(step == steps - 1)
    def _():
        result_ref[...] = total_ref[...].astype(BF16).reshape(blocks, places, width)


def run_experts(pooled, weights):
    blocks, places, width = pooled.shape
    steps, _, _, tile = weights.shape
    count = blocks * places
    return pl.pallas_call(
        functools.partial(expert_kernel, steps),
        grid=(steps,),
        in_specs=[constant_spec(pooled.shape), pl.BlockSpec((1, 2, width, tile), lambda i: (i, 0, 0, 0))],
        out_specs=[
            constant_spec(pooled.shape),
            pl.BlockSpec((1, count, tile), lambda i: (i, 0, 0)),
            pl.BlockSpec((1, count, tile), lambda i: (i, 0, 0)),
        ],
        out_shape=[
            jax.ShapeDtypeStruct(pooled.shape, BF16),
            jax.ShapeDtypeStruct((steps, count, tile), BF16),
            jax.ShapeDtypeStruct((steps, count, tile), F32),
        ],
        scratch_shapes=[pltpu.VMEM((count, width), F32)],
        compiler_params=pltpu.CompilerParams(vmem_limit_bytes=40 << 20),
        cost_estimate=pl.CostEstimate(
            flops=count * width * tile * steps * 8, bytes_accessed=width * tile * steps * 8, transcendentals=0
        ),
        name="experts",
    )(pooled, weights)


def expert_back_kernel(steps, slots_ref, pooled_ref, grads_ref, result_ref, act_ref, slope_ref, weights_ref, back_ref, grad_ref, total_ref):
    step = pl.program_id(0)
    blocks, places, width = pooled_ref.shape
    count = blocks * places
    pooled = pooled_ref[...].reshape(count, width)
    grads = grads_ref[...].reshape(count, width)
    act = act_ref[0]
    grad_pre = (dot(grads, weights_ref[0, 1]) * slope_ref[0]).astype(BF16)
    grad_ref[0, 0] = dot_tn(pooled, grad_pre).astype(BF16)
    grad_ref[0, 1] = dot_tn(grads, act).astype(BF16)
    part = dot_nt(grad_pre, weights_ref[0, 0])

    @pl.when(step == 0)
    def _():
        total_ref[...] = part

    @pl.when(step > 0)
    def _():
        total_ref[...] += part

    @pl.when(step == steps - 1)
    def _():
        grad_pooled = total_ref[...].astype(BF16)
        back_ref[:, :places] = grad_pooled.reshape(blocks, places, width)
        result = result_ref[...].reshape(count, width)
        product = result.astype(F32) * grads.astype(F32) + grad_pooled.astype(F32) * pooled.astype(F32)
        high = product.astype(BF16)
        rest = (product - high.astype(F32)).astype(BF16)
        ones = jnp.ones((16, width), BF16)
        sums = dot_nt(ones, high) + dot_nt(ones, rest)
        top = sums.astype(BF16)
        low = (sums - top.astype(F32)).astype(BF16)
        for b in range(blocks):
            here = slice(b * places, b * places + places)
            fill = jnp.zeros((16, width - 2 * places), BF16)
            back_ref[b, places:] = jnp.concatenate([top[:, here], low[:, here], fill], axis=1)


def pull_experts(slots, pooled, grads, result, act, slope, weights):
    blocks, places, width = pooled.shape
    steps, _, _, tile = weights.shape
    count = blocks * places
    return pl.pallas_call(
        functools.partial(expert_back_kernel, steps),
        grid_spec=pltpu.PrefetchScalarGridSpec(
            num_scalar_prefetch=1,
            grid=(steps,),
            in_specs=[constant_spec(pooled.shape)] * 3
            + [pl.BlockSpec((1, count, tile), lambda i, slots: (i, 0, 0))] * 2
            + [pl.BlockSpec((1, 2, width, tile), lambda i, slots: (i, 0, 0, 0))],
            out_specs=[
                constant_spec((blocks, places + 16, width)),
                pl.BlockSpec((1, 2, width, tile), lambda i, slots: (slots[i], 0, 0, 0)),
            ],
            scratch_shapes=[pltpu.VMEM((count, width), F32)],
        ),
        out_shape=[
            jax.ShapeDtypeStruct((blocks, places + 16, width), BF16),
            jax.ShapeDtypeStruct(weights.shape, BF16),
        ],
        compiler_params=pltpu.CompilerParams(vmem_limit_bytes=40 << 20),
        cost_estimate=pl.CostEstimate(
            flops=count * width * tile * steps * 12, bytes_accessed=width * tile * steps * 8, transcendentals=0
        ),
        name="pull_experts",
    )(slots, pooled, grads, result, act, slope, weights)


def spread_kernel(group, count, slots_ref, gates_ref, grads_ref, hidden_ref, *rest):
    parts, (out_ref, change_ref, result_ref) = rest[:count], rest[-3:]
    for k in range(count):
        @pl.when(pl.program_id(0) == k)
        def _():
            result_ref[...] = parts[k][...]

    rows, places = grads_ref.shape[0], grads_ref.shape[1]
    experts = result_ref.shape[0]
    sub = 16
    columns = gates_ref.shape[1]

    def step(s, _):
        here = pl.ds(pl.multiple_of(s * sub, sub), sub)
        results = [result_ref[e, here, :].astype(F32) * group for e in range(experts)]
        gates = gates_ref[here, :].astype(BF16).astype(F32)
        lane = iota((sub, columns), 1)
        changes = jnp.zeros((sub, columns), F32)
        for r in range(rows):
            grads = grads_ref[r, here, :].astype(F32)
            for e in range(experts):
                both = jnp.sum(grads * results[e], axis=1, keepdims=True)
                changes = jnp.where(lane == r * experts + e, both, changes)
            total = sum(gates[:, r * experts + e: r * experts + e + 1] * results[e] for e in range(experts))
            out_ref[r, here, :] = (hidden_ref[r, here, :] + total.astype(BF16).astype(F32)).astype(BF16)
        change_ref[0, here, :] = changes
        return 0

    lax.fori_loop(0, places // sub, step, 0, unroll=8)


def slot_of(found):
    found = list(found)
    step = found[-1] - found[0]
    return lambda i, slots: slots[found[0] + i * step]


def spread_tokens(found, slots, gates, cotangent, hidden, group, held):
    rows, span, width = hidden.shape
    parts = list(found.values())
    experts, places, _ = parts[0].shape
    at = slot_of(found)
    block = pl.BlockSpec((rows, places, width), lambda i, slots: (0, at(i, slots), 0))
    columns = gates.shape[1]
    aliased = [] if held is None else [held]
    return pl.pallas_call(
        functools.partial(spread_kernel, group, len(parts)),
        grid_spec=pltpu.PrefetchScalarGridSpec(
            num_scalar_prefetch=1,
            grid=(len(parts),),
            in_specs=[pl.BlockSpec((places, columns), lambda i, slots: (at(i, slots), 0)), block, block]
            + [constant_spec(part.shape) for part in parts]
            + [pl.BlockSpec(memory_space=pltpu.HBM) for _ in aliased],
            out_specs=[block, pl.BlockSpec((1, places, columns), lambda i, slots: (i, 0, 0))],
            scratch_shapes=[pltpu.VMEM(parts[0].shape, BF16)],
        ),
        out_shape=[
            jax.ShapeDtypeStruct((rows, span, width), BF16),
            jax.ShapeDtypeStruct((len(parts), places, columns), F32),
        ],
        input_output_aliases={4 + len(parts): 0} if aliased else {},
        compiler_params=pltpu.CompilerParams(vmem_limit_bytes=58 << 20),
        cost_estimate=pl.CostEstimate(
            flops=len(parts) * rows * places * width * 5000, bytes_accessed=rows * places * width * 10, transcendentals=0
        ),
        name="spread",
    )(slots, gates, cotangent, hidden, *parts, *aliased)


def pull_kernel(first, count, slots_ref, gates_ref, change_ref, mixed_ref, hidden_ref, cotangent_ref, attended_ref, router_ref, gains_ref, weight_ref, *rest):
    parts, rest = rest[:count], rest[count:]
    out_ref, low_ref, router_grad_ref, project_ref, sums_ref, pooled_ref, logits_ref, grad_ref = rest[-8:]

    @pl.when(pl.program_id(0) == 0)
    def _():
        if first:
            router_grad_ref[...] = jnp.zeros_like(router_grad_ref)
            project_ref[...] = jnp.zeros_like(project_ref)
            sums_ref[...] = jnp.zeros_like(sums_ref)
        else:
            router_grad_ref[...] = rest[2][...]
            project_ref[...] = rest[3][...]
            sums_ref[...] = rest[4][...]

    for k in range(count):
        @pl.when(pl.program_id(0) == k)
        def _():
            pooled_ref[...] = parts[k][...]

    rows, places, width = mixed_ref.shape
    experts = pooled_ref.shape[0]
    sub = 16
    columns = gates_ref.shape[1]
    inner = jnp.zeros((places, columns), F32)
    for e in range(experts):
        pick = (iota((16, columns), 0) == 0) & (iota((16, columns), 1) % experts == e)
        pick = jnp.where(pick, 1.0, 0.0).astype(BF16)
        inner += dot_tn(pooled_ref[e, places:, :places], pick) + dot_tn(pooled_ref[e, places:, places: 2 * places], pick)

    def change(s, _):
        here = pl.ds(pl.multiple_of(s * sub, sub), sub)
        pooled = [pooled_ref[e, here, :].astype(F32) for e in range(experts)]
        lane = iota((sub, columns), 1)
        changes = jnp.zeros((sub, columns), F32)
        for r in range(rows):
            mixed = mixed_ref[r, here, :].astype(F32)
            for e in range(experts):
                both = jnp.sum(pooled[e] * mixed, axis=1, keepdims=True)
                changes = jnp.where(lane == r * experts + e, both, changes)
        logits_ref[here, :] = changes
        return 0

    lax.fori_loop(0, places // sub, change, 0, unroll=8)
    changes = (logits_ref[...] + change_ref[0]).astype(BF16).astype(F32)
    low = (gates_ref[...] * (changes - inner)).astype(BF16)
    for r in range(rows):
        grad_ref[r] = dot(low, router_ref[r])
        router_grad_ref[...] += dot_tn(low, mixed_ref[r])[r * experts: r * experts + experts]

    def spread(s, _):
        here = pl.ds(pl.multiple_of(s * sub, sub), sub)
        pooled = [pooled_ref[e, here, :].astype(F32) for e in range(experts)]
        gates = gates_ref[here, :].astype(BF16).astype(F32)
        for r in range(rows):
            grad_ref[r, here, :] = sum(
                (gates[:, r * experts + e: r * experts + e + 1] * pooled[e] for e in range(experts)),
                grad_ref[r, here, :],
            )
        return 0

    lax.fori_loop(0, places // sub, spread, 0, unroll=8)

    for r in range(rows):
        grads = grad_ref[r].astype(BF16).astype(F32)
        hat, inverse = normalise(hidden_ref[r])
        sums_ref[0:1] += jnp.sum(grads * hat, axis=0, keepdims=True)
        sums_ref[1:2] += jnp.sum(grads, axis=0, keepdims=True)
        total = cotangent_ref[r].astype(F32) + pull_norm(grads * gains_ref[2:3], hat, inverse)
        out_ref[r] = total
        total = total.astype(BF16)
        project_ref[...] += dot_tn(attended_ref[r], total)
        low_ref[r] = dot_nt(total, weight_ref[...]).astype(BF16)


def pull_slots(found, slots, gates, change, mixed, hidden, cotangent, attended, router, gains, packed, held):
    rows, span, width = mixed.shape
    parts = list(found.values())
    experts, depth, _ = parts[0].shape
    places = span // slots.shape[0]
    at = slot_of(found)
    block = pl.BlockSpec((rows, places, width), lambda i, slots: (0, at(i, slots), 0))
    columns = gates.shape[1]
    sums = [(experts, width), (width, width), (8, width)]
    ins = [
        pl.BlockSpec((places, columns), lambda i, slots: (at(i, slots), 0)),
        pl.BlockSpec((1, places, columns), lambda i, slots: (i, 0, 0)),
        block,
        block,
        block,
        block,
        constant_spec(router.shape),
        constant_spec(gains.shape),
        constant_spec((width, width), 0, 3),
    ] + [constant_spec(part.shape) for part in parts]
    aliases = {}
    if held is not None:
        aliases = {len(ins) + 1: 0, len(ins) + 2: 1}
        ins += [pl.BlockSpec(memory_space=pltpu.HBM)] * 2 + [constant_spec(shape) for shape in sums]
    return pl.pallas_call(
        functools.partial(pull_kernel, held is None, len(parts)),
        grid_spec=pltpu.PrefetchScalarGridSpec(
            num_scalar_prefetch=1,
            grid=(len(parts),),
            in_specs=ins,
            out_specs=[block, block] + [constant_spec(shape) for shape in sums],
            scratch_shapes=[
                pltpu.VMEM(parts[0].shape, BF16),
                pltpu.VMEM((places, columns), F32),
                pltpu.VMEM((rows, places, width), F32),
            ],
        ),
        out_shape=[jax.ShapeDtypeStruct((rows, span, width), F32), jax.ShapeDtypeStruct((rows, span, width), BF16)]
        + [jax.ShapeDtypeStruct(shape, F32) for shape in sums],
        input_output_aliases=aliases,
        compiler_params=pltpu.CompilerParams(vmem_limit_bytes=58 << 20),
        cost_estimate=pl.CostEstimate(
            flops=len(parts) * rows * places * width * width * 20,
            bytes_accessed=rows * places * width * 20,
            transcendentals=0,
        ),
        name="pull_slots",
    )(slots, gates, change, mixed, hidden, cotangent, attended, router, gains, packed, *parts, *(held or ()))


def project_kernel(grads_ref, tokens_ref, product_ref, sums_ref):
    @pl.when((pl.program_id(0) == 0) & (pl.program_id(1) == 0))
    def _():
        product_ref[...] = jnp.zeros_like(product_ref)
        sums_ref[...] = jnp.zeros_like(sums_ref)

    hat = normalise(tokens_ref[0].astype(F32))[0].astype(BF16)
    ones = jnp.ones((hat.shape[0], 8), BF16)
    product_ref[...] += dot_tn(hat, grads_ref[0])
    sums_ref[...] += dot_tn(ones, grads_ref[0])


def project_grads(grads, tokens, tile=1024):
    rows, length, width = tokens.shape
    shapes = [(width, 3 * width), (8, 3 * width)]
    return pl.pallas_call(
        project_kernel,
        grid=(rows, length // tile),
        in_specs=[
            pl.BlockSpec((1, tile, 3 * width), lambda r, t: (r, t, 0)),
            pl.BlockSpec((1, tile, width), lambda r, t: (r, t, 0)),
        ],
        out_specs=[constant_spec(shape) for shape in shapes],
        out_shape=[jax.ShapeDtypeStruct(shape, F32) for shape in shapes],
        compiler_params=pltpu.CompilerParams(vmem_limit_bytes=40 << 20),
        cost_estimate=pl.CostEstimate(
            flops=rows, bytes_accessed=rows, transcendentals=0
        ),
        name="project_grads",
    )(grads, tokens)


def tokens_kernel(grads_ref, tokens_ref, hidden_ref, gains_ref, weight_ref, *rest):
    out_ref = rest[-1]
    for at in pieces(tokens_ref.shape[1]):
        hat, inverse = normalise(tokens_ref[0, at].astype(F32))
        grads = dot_nt(grads_ref[0, at], weight_ref[...])
        out_ref[0, at] = hidden_ref[0, at] + pull_norm(grads * gains_ref[0:1], hat, inverse)


def pull_tokens(grads, tokens, hidden, gains, packed, row_from, row_to, held=None, tile=1024):
    rows, length, width = tokens.shape
    block = pl.BlockSpec((1, tile, width), lambda r, t: (r + row_from, t, 0))
    aliased = [] if held is None else [held]
    return pl.pallas_call(
        tokens_kernel,
        grid=(row_to - row_from, length // tile),
        in_specs=[
            pl.BlockSpec((1, tile, 3 * width), lambda r, t: (r + row_from, t, 0)),
            block,
            block,
            constant_spec(gains.shape),
            constant_spec((width, 3 * width)),
        ]
        + [pl.BlockSpec(memory_space=pltpu.HBM) for _ in aliased],
        out_specs=block,
        out_shape=jax.ShapeDtypeStruct((rows, length, width), F32),
        input_output_aliases={5: 0} if aliased else {},
        compiler_params=pltpu.CompilerParams(vmem_limit_bytes=58 << 20),
        cost_estimate=pl.CostEstimate(
            flops=(row_to - row_from) * length * width * width * 20,
            bytes_accessed=(row_to - row_from) * length * width * 16,
            transcendentals=0,
        ),
        name="pull_tokens",
    )(grads, tokens, hidden, gains, packed, *aliased)


def ring_order(size):
    inner = 2 if size % 2 == 0 and size > 2 else 1
    outer = size // inner
    up = [z * inner for z in range(outer)]
    if inner == 1:
        return up
    return up + [z * inner + 1 for z in reversed(range(outer))]


def shift(value, order, step):
    count = len(order)
    return lax.ppermute(value, "dp", [(order[i], order[(i + step) % count]) for i in range(count)])


def flip(value, bit, axis="fsdp"):
    count = lax.axis_size(axis)
    return lax.ppermute(value, axis, [(i, i ^ bit) for i in range(count)])


def turn(value, step, axis="dp"):
    count = lax.axis_size(axis)
    return lax.ppermute(value, axis, [(i, (i + step) % count) for i in range(count)])


def take(values, index):
    starts = (index,) + (jnp.uint32(0),) * (values.ndim - 1)
    return lax.dynamic_slice(values, starts, (1,) + values.shape[1:])[0]


def put(values, value, index):
    return lax.dynamic_update_slice(values, value[None], (index,) + (jnp.uint32(0),) * value.ndim)


def add(a, b):
    return (a.astype(F32) + b.astype(F32)).astype(BF16)


def together(*values):
    return lax.optimization_barrier(values)


class Ring:
    def __init__(self, value, order):
        self.order, self.done = order, 0
        self.ahead = self.behind = value

    def left(self):
        return self.done < len(self.order) // 2

    def after(self, *values):
        self.ahead, self.behind, *_ = together(self.ahead, self.behind, *values)

    def step(self, *beside):
        count = len(self.order)
        self.done += 1
        slot = count - self.done
        ahead, behind = self.ahead, self.behind
        middle = 2 * self.done == count and ahead.shape[0] % 2 == 0
        if middle:
            half = ahead.shape[0] // 2
            ahead, behind = ahead[:half], behind[half:]
        ahead = shift(ahead, self.order, 1)
        if 2 * self.done < count or middle:
            behind = shift(behind, self.order, -1)
        ahead, behind, *beside = together(ahead, behind, *beside)
        self.ahead, self.behind = ahead, behind
        if middle:
            return {slot: jnp.concatenate([ahead, behind], axis=0)}, beside
        return {slot: ahead, self.done: behind} if 2 * self.done < count else {slot: ahead}, beside


def gather_all(value, steps, *beside):
    pair = pair_of(lax.axis_size("dp"))
    lines = lax.axis_size("dp") // pair
    size = lax.axis_size("fsdp")
    here = lax.axis_index("fsdp")

    def both(value, bit, axis, index):
        other = flip(value, bit, axis)
        upper = (index & bit) != 0
        return jnp.stack([jnp.where(upper, other, value), jnp.where(upper, value, other)])

    whole = put(jnp.zeros((lines,) + value.shape, value.dtype), value, steps[0])
    for k in range(1, lines):
        whole = put(whole, turn(value, -k * pair), steps[k])
    if beside:
        whole, *beside = together(whole, *beside)
    whole = both(whole, 1, "dp", lax.axis_index("dp")) if pair == 2 else whole[None]
    whole = jnp.moveaxis(whole, 0, 1)
    whole = whole.reshape((lines * pair, 1) + value.shape)
    bit = size // 2
    while bit:
        whole = both(whole, bit, "fsdp", here)
        whole = jnp.moveaxis(whole, 0, 2)
        whole = whole.reshape((lines * pair, -1) + value.shape)
        bit //= 2
    return whole, beside


def scatter_all(values, steps, work):
    owners, size = lax.axis_size("dp"), lax.axis_size("fsdp")
    bits = size.bit_length() - 1
    here = lax.axis_index("fsdp")
    width = values.shape[1]
    pair = pair_of(owners)
    work = list(work)

    def half(held, axis, upper, bit, name):
        low, high = (lax.index_in_dim(held, i, axis, keepdims=False) for i in (0, 1))
        came = flip(jnp.where(upper, low, high), bit, name)
        if work:
            came, = work.pop(0)(came)
        return add(jnp.where(upper, high, low), came)

    held = values.reshape((owners // pair, pair) + (2,) * bits + (-1, width))
    for level in range(bits):
        held = half(held, bits + 1 - level, ((here >> level) & 1) != 0, 1 << level, "fsdp")
    held = half(held, 1, (lax.axis_index("dp") & 1) != 0, 1, "dp") if pair == 2 else held[:, 0]
    came = [turn(take(held, steps[k]), k * pair) for k in range(1, owners // pair)]
    while work:
        came = work.pop(0)(*came)
    return sum((value.astype(F32) for value in came), take(held, steps[0]).astype(F32))


def pair_of(owners):
    return 2 if owners % 2 == 0 else 1


def exchange(values):
    return jnp.stack([values[0]] + [flip(values[k], k) for k in range(1, values.shape[0])])


def per_device(
    tokens,
    segment_ids,
    pad_tokens,
    cotangent,
    project_in,
    project_out,
    router_weight,
    expert_in,
    expert_out,
    first_gain,
    first_bias,
    second_gain,
    second_bias,
):
    blocks_here, rows, length, width = tokens.shape
    tokens = tokens.reshape(rows, length, width)
    cotangent = cotangent.reshape(rows, length, width)
    segments = segment_ids.reshape(rows, length)
    group = pad_tokens.shape[1]
    owners = lax.axis_size("dp")
    experts = router_weight.shape[1]
    order = ring_order(owners)
    data_index = lax.axis_index("dp")
    expert_index = lax.axis_index("fsdp")
    places = length // owners

    pair = pair_of(owners)
    lines = owners // pair
    ring = np.array([[order[(order.index(d) + k) % owners] for k in range(owners)] for d in range(owners)], np.int32)
    place = np.array(
        [[(o % pair ^ d % pair) * lines + (o // pair - d // pair) % lines for o in ring[d]] for d in range(owners)],
        np.int32,
    )
    line = np.array([[(d // pair + k) % lines for k in range(lines)] for d in range(owners)], np.int32)
    tables = np.concatenate([ring, place, line], axis=1)
    tables = lax.dynamic_slice(
        jnp.asarray(tables), (data_index.astype(jnp.uint32), jnp.uint32(0)), (1, tables.shape[1])
    )[0]
    slots, shares = tables[:owners], tables[owners: 2 * owners]
    spots = [tables[k].astype(jnp.uint32) for k in range(owners)]
    steps = [tables[2 * owners + k].astype(jnp.uint32) for k in range(lines)]

    vectors = jnp.stack([first_gain, first_bias, second_gain, second_bias], axis=1)
    small = jnp.concatenate([router_weight, vectors], axis=1)
    small = jnp.pad(small, ((0, 0), (0, 128 - small.shape[1])))
    packed = jnp.concatenate([project_in, project_out, small], axis=1)
    packed, (expert_in, expert_out) = gather_all(packed, steps, expert_in, expert_out)
    weights = jnp.stack([expert_in[0], expert_out[0].T])
    packed = packed.reshape(width, packed.shape[-1])
    packed, weights = together(packed, weights)
    kept = {0: weights}
    weights = Ring(weights, order)
    small = packed[:, 4 * width:].T
    mine = (jnp.arange(experts)[:, None] ^ jnp.arange(experts)[None, :]) == expert_index
    router = jnp.sum(jnp.where(mine[:, :, None], small[None, :experts], 0), axis=1).astype(BF16)
    spread_router = jnp.stack(
        [jnp.pad(router, ((r * experts, (rows - 1 - r) * experts), (0, 0))) for r in range(rows)]
    )
    gains = jnp.pad(small[experts: experts + 4].astype(F32), ((0, 4), (0, 0)))

    own_pads = lax.dynamic_slice_in_dim(pad_tokens[0], data_index * rows, rows, 0)
    vlens = (length - own_pads).astype(jnp.int32)
    starts = jnp.zeros_like(segments)
    for doc in range(1, 4):
        before = jnp.sum((segments < doc).astype(jnp.int32), axis=1, keepdims=True)
        starts = jnp.where(segments == doc, before, starts)
    starts = starts.reshape(rows, length // QB, QB)
    lows = starts[:, :, 0] // QB

    def meanwhile(value):
        if not weights.left():
            return value
        found, (value,) = weights.step(value)
        kept.update(found)
        return value

    joined = meanwhile(join_tokens(tokens, gains, packed))
    attended, logs = attn_fwd(joined, starts, lows, vlens, 1)
    attended = meanwhile(attended)
    hidden, mixed, logits = mix_tokens(
        attended, tokens, gains, packed, jnp.pad(router, ((0, 16 - experts), (0, 0))), 0
    )
    logits = meanwhile(logits)[:, :experts]
    valid = (jnp.arange(length)[None, :] < vlens[:, None])[:, None, :]
    highest = jnp.max(jnp.where(valid, logits, NEGATIVE), axis=0)
    total = jnp.sum(jnp.where(valid, jnp.exp(logits - highest), 0.0), axis=0)
    stats = jnp.stack([highest, total])[None]
    if pair == 2:
        stats = jnp.concatenate([stats, flip(stats, 1, "dp")])
    stats = jnp.concatenate([stats] + [turn(stats, k * pair) for k in range(1, lines)])
    tops = jnp.max(stats[:, 0], axis=0)
    total = jnp.sum(stats[:, 1] * jnp.exp(stats[:, 0] - tops), axis=0)
    gates = jnp.where(valid, jnp.exp(jnp.where(valid, logits - tops, NEGATIVE)) / total, 0.0)
    gates = gates.reshape(rows * experts, length).T
    pooled = meanwhile(pool_tokens(slots, gates, mixed, experts, 1.0))
    while weights.left():
        kept.update(weights.step()[0])
    weights = jnp.stack([kept[k] for k in range(owners)])
    grads = pool_tokens(slots, gates, cotangent, experts, float(group))

    half = experts // 2
    first = [(pooled[:, :half], 1), (pooled[:, half:], -1)]
    second = [(grads[:, :half], 1), (grads[:, half:], -1)]
    held = [part[-way % owners] for part, way in first]
    later = [part[-way % owners] for part, way in second]
    for step in range(owners - 1):
        came = [shift(value, order, way) for value, (_, way) in zip(held, first)]
        *came, one, two = together(*came, *later)
        later = [one, two]
        held = [add(value, part[-way * (2 + step) % owners]) for value, (part, way) in zip(came, first)]
        came = [shift(value, order, way) for value, (_, way) in zip(later, second)]
        later = [add(value, part[-way * (2 + step) % owners]) for value, (part, way) in zip(came, second)]
    pooled = exchange(jnp.concatenate(held, axis=0))
    result, act, slope = run_experts(pooled, weights)
    grads = exchange(jnp.concatenate(later, axis=0))
    grad_pooled, grad_weights = pull_experts(shares, pooled, grads, result, act, slope, weights)

    result = exchange(result)
    back = exchange(grad_pooled)

    def pull(found, change, out):
        return pull_slots(
            found, slots, gates, change, mixed, hidden, cotangent, attended, spread_router, gains, packed, out
        )

    def spread(found, out):
        return spread_tokens(found, slots, gates, cotangent, hidden, group, out)

    turns = owners // 2
    first, second = Ring(result, order), Ring(back, order)
    found, (grad_weights,) = first.step(grad_weights)
    groups, arrived = [{0: result}, found], [{0: back}]
    out, pulled, changes = None, None, []
    for step in range(turns + 1):
        work = []
        for k in [step] if step < turns - 1 else [turns - 1, turns] if step == turns - 1 else []:
            out, change = spread(groups[k], out)
            changes.append(change)
            work = [out]
        if 0 < step < turns - 1 or step == turns:
            k = step - 1 if step < turns else turns - 2
            pulled = pull(arrived[k], changes[k], pulled)
            work += pulled
        if step > 0:
            second.after(*groups[min(step + 1, turns)].values())
        if first.left():
            found, work = first.step(*work)
            groups.append(found)
        if second.left() and step > 0:
            found, work = second.step(*work)
            arrived.append(found)
        if step < turns:
            out, *work = work
        pulled = work or pulled
    pulled = pull(arrived[turns - 1], changes[turns - 1], pulled)
    layer_out = out
    pulled = pull(arrived[turns], changes[turns], pulled)
    grad_hidden, grad_attended, router_grad, grad_proj_out, sums_two = pulled
    grad_attended, grad_weights = together(grad_attended, grad_weights)
    split = rows - max(1, rows // 4)
    if pair == 2:
        came = flip(grad_weights[lines:], 1, "dp")
    grads = attn_bwd(joined, grad_attended, attended, logs, starts, lows, vlens, 0, split)
    grad_weights = grad_weights[:lines]
    if pair == 2:
        came, grads = together(came, grads)
        grad_weights = add(grad_weights, came)
    grad_parts = [turn(grad_weights[k], k * pair) for k in range(1, lines)]
    grads = attn_bwd(joined, grad_attended, attended, logs, starts, lows, vlens, split, rows, grads)
    product, sums_one = project_grads(grads, tokens)
    product, *grad_parts = together(product, *grad_parts)
    full_in = packed[:, : 3 * width].astype(F32)
    sums_one = sums_one[:1]
    grad_proj_in = gains[0][:, None] * product + gains[1][:, None] * sums_one
    sums_one = jnp.stack([jnp.sum(full_in * product, axis=1), jnp.sum(full_in * sums_one, axis=1)])
    router_grad = jnp.sum(jnp.where(mine[:, :, None], router_grad[None], 0.0), axis=1)

    late = jnp.concatenate([router_grad, sums_one, sums_two[:2]], axis=0).T
    late = jnp.pad(late, ((0, 0), (0, 128 - late.shape[1])))
    reduced = jnp.concatenate([grad_proj_in, grad_proj_out, late], axis=1).astype(BF16)
    made = []

    def tokens_beside(*came):
        *came, grad = together(*came, pull_tokens(grads, tokens, grad_hidden, gains, packed, 0, rows))
        made.append(grad)
        return came

    def weights_beside(*came):
        value, *parts = together(*came, *grad_parts)
        made.append(sum((part.astype(F32) for part in parts), grad_weights[0].astype(F32)))
        return [value]

    reduced = scatter_all(reduced, steps, [lambda *came: came, tokens_beside, weights_beside])
    tokens_grad, grad_weights = made
    late = reduced[:, 4 * width:]
    return (
        layer_out[None],
        tokens_grad[None],
        reduced[:, : 3 * width],
        reduced[:, 3 * width: 4 * width],
        late[:, :experts],
        grad_weights[0][None],
        grad_weights[1].T[None],
        late[:, experts],
        late[:, experts + 1],
        late[:, experts + 2],
        late[:, experts + 3],
    )


def solution(mesh):
    in_specs = (
        P("fsdp", "dp", None, None),
        P("fsdp", "dp", None),
        P("fsdp", None),
        P("fsdp", "dp", None, None),
        P(("dp", "fsdp"), None),
        P(("dp", "fsdp"), None),
        P(("dp", "fsdp"), None),
        P("fsdp", None, "dp"),
        P("fsdp", "dp", None),
        P(("dp", "fsdp")),
        P(("dp", "fsdp")),
        P(("dp", "fsdp")),
        P(("dp", "fsdp")),
    )
    out_specs = (
        P("fsdp", "dp", None, None),
        P("fsdp", "dp", None, None),
        P(("dp", "fsdp"), None),
        P(("dp", "fsdp"), None),
        P(("dp", "fsdp"), None),
        P("fsdp", None, "dp"),
        P("fsdp", "dp", None),
        P(("dp", "fsdp")),
        P(("dp", "fsdp")),
        P(("dp", "fsdp")),
        P(("dp", "fsdp")),
    )
    return jax.shard_map(
        per_device, mesh=mesh, in_specs=in_specs, out_specs=out_specs, check_vma=False
    )
```

```python
import functools, math
import jax
import jax.numpy as jnp
import numpy as np
from jax import lax
from jax.experimental import pallas as pl
from jax.experimental.pallas import tpu as pltpu
from jax.sharding import PartitionSpec as P

NEGATIVE = -1e30
QB = 128
F32 = jnp.float32
BF16 = jnp.bfloat16
NT = (((1,), (1,)), ((), ()))
TN = (((0,), (0,)), ((), ()))


def dot(a, b):
    return jnp.dot(a, b, preferred_element_type=F32)


def dot_nt(a, b):
    return lax.dot_general(a, b, NT, preferred_element_type=F32)


def dot_tn(a, b):
    return lax.dot_general(a, b, TN, preferred_element_type=F32)


def iota(shape, axis):
    return lax.broadcasted_iota(jnp.int32, shape, axis)


def split_heads(x):
    low = iota(x.shape, 1) < 64
    zero = jnp.zeros_like(x)
    return jnp.concatenate([jnp.where(low, x, zero), jnp.where(low, zero, x)], axis=0)


def join_heads(x):
    half = x.shape[0] // 2
    low = iota((half, x.shape[1]), 1) < 64
    return jnp.where(low, x[:half], x[half:])


def attn_fwd_kernel(width, batch, count, lo_ref, vlen_ref, start_ref, joined_ref, out_ref, log_ref, bias_ref):
    row = pl.program_id(0) * batch

    def block(qb, _):
        lo = functools.reduce(jnp.minimum, [lo_ref[row + r, qb] for r in range(batch)])
        base = pl.multiple_of(qb * QB, QB)
        first = pl.multiple_of(lo * QB, QB)
        own = pl.ds(base, QB)

        def variant(blocks):
            span = blocks * QB
            keys = pl.ds(first, span)
            i = base + iota((QB, QB), 0)
            bias = []
            for r in range(batch):
                begins = jnp.broadcast_to(start_ref[r, pl.ds(qb, 1), :], (QB, QB)).T
                for b in range(blocks):
                    j = first + b * QB + iota((QB, QB), 1)
                    ok = ((j >= begins) & (j <= i) & (j < vlen_ref[row + r])) | (j == i)
                    bias_ref[r, :, b * QB:(b + 1) * QB] = jnp.where(ok, 0.0, NEGATIVE)
                bias.append(jnp.concatenate([bias_ref[r, :, :span]] * 2, axis=0))
            work = [(r, lane) for r in range(batch) for lane in range(0, width, 128)]
            query = [split_heads(joined_ref[r, own, pl.ds(at, 128)] * jnp.asarray(0.125, BF16)) for r, at in work]
            scores = [dot_nt(q, joined_ref[r, keys, pl.ds(width + at, 128)]) for q, (r, at) in zip(query, work)]
            scores = [s + bias[r] for s, (r, _) in zip(scores, work)]
            tops = [jnp.max(s, axis=1, keepdims=True) for s in scores]
            raised = [jnp.exp(s - top) for s, top in zip(scores, tops)]
            totals = [jnp.sum(p, axis=1, keepdims=True) for p in raised]
            out = [
                dot(p.astype(BF16), joined_ref[r, keys, pl.ds(2 * width + at, 128)]) for p, (r, at) in zip(raised, work)
            ]
            for o, total, (r, at) in zip(out, totals, work):
                out_ref[r, own, pl.ds(at, 128)] = join_heads(o * (1.0 / total)).astype(BF16)
            lane = iota((QB, QB), 1)
            for r in range(batch):
                tile = jnp.zeros((QB, QB), F32)
                for top, total, (other, at) in zip(tops, totals, work):
                    if other == r:
                        log = top + jnp.log(total)
                        tile = jnp.where(lane == at // 64, log[:QB], tile)
                        tile = jnp.where(lane == at // 64 + 1, log[QB:], tile)
                log_ref[r, pl.ds(qb, 1)] = tile.T[None, : log_ref.shape[2]]

        for blocks in range(1, 6):
            pl.when(qb - lo + 1 == blocks)(functools.partial(variant, blocks))
        return 0

    lax.fori_loop(0, count, block, 0)


def attn_fwd(joined, starts, lows, vlens, batch=2):
    rows, length, triple = joined.shape
    width = triple // 3
    count = length // QB
    return pl.pallas_call(
        functools.partial(attn_fwd_kernel, width, batch, count),
        grid_spec=pltpu.PrefetchScalarGridSpec(
            num_scalar_prefetch=2,
            grid=(rows // batch,),
            in_specs=[
                pl.BlockSpec((batch, count, QB), lambda r, *_: (r, 0, 0)),
                pl.BlockSpec((batch, length, triple), lambda r, *_: (r, 0, 0)),
            ],
            out_specs=[
                pl.BlockSpec((batch, length, width), lambda r, *_: (r, 0, 0)),
                pl.BlockSpec((batch, count, width // 64, QB), lambda r, *_: (r, 0, 0, 0)),
            ],
            scratch_shapes=[pltpu.VMEM((batch, QB, 5 * QB), F32)],
        ),
        out_shape=[
            jax.ShapeDtypeStruct((rows, length, width), BF16),
            jax.ShapeDtypeStruct((rows, count, width // 64, QB), F32),
        ],
        compiler_params=pltpu.CompilerParams(vmem_limit_bytes=48 << 20),
        cost_estimate=pl.CostEstimate(
            flops=rows * length * 400 * 8 * 256 * 4, bytes_accessed=rows * length * triple * 2, transcendentals=0
        ),
        name="attend",
    )(lows, vlens, starts, joined)


def attn_bwd_kernel(width, row_from, batch, count, lo_ref, vlen_ref, start_ref, joined_ref, grad_ref, attended_ref, log_ref, *rest):
    out_ref, dk_ref, dv_ref, bias_ref = rest[-4:]
    row = pl.program_id(0) * batch + row_from
    dk_ref[...] = jnp.zeros_like(dk_ref)
    dv_ref[...] = jnp.zeros_like(dv_ref)

    def block(qb, _):
        lo = functools.reduce(jnp.minimum, [lo_ref[row + r, qb] for r in range(batch)])
        base = pl.multiple_of(qb * QB, QB)
        first = pl.multiple_of(lo * QB, QB)
        own = pl.ds(base, QB)

        def variant(blocks):
            span = blocks * QB
            keys = pl.ds(first, span)
            i = base + iota((QB, QB), 1)
            pick = jnp.where(iota((16, width), 1) // 64 == iota((16, width), 0), 1.0, 0.0).astype(BF16)
            bias, sums = [], []
            for r in range(batch):
                begins = start_ref[r, pl.ds(qb, 1), :]
                for b in range(blocks):
                    j = first + b * QB + iota((QB, QB), 0)
                    ok = ((j >= begins) & (j <= i) & (j < vlen_ref[row + r])) | (j == i)
                    bias_ref[r, b * QB:(b + 1) * QB, :] = jnp.where(ok, 0.0, NEGATIVE)
                bias.append(jnp.concatenate([bias_ref[r, :span, :]] * 2, axis=1))
                product = grad_ref[r, own, :].astype(F32) * attended_ref[r, own, :].astype(F32)
                high = product.astype(BF16)
                sums.append(dot_nt(pick, high) + dot_nt(pick, (product - high.astype(F32)).astype(BF16)))
            work = [(r, lane) for r in range(batch) for lane in range(0, width, 128)]
            query = [split_heads(joined_ref[r, own, pl.ds(at, 128)] * jnp.asarray(0.125, BF16)) for r, at in work]
            grads = [split_heads(grad_ref[r, own, pl.ds(at, 128)]) for r, at in work]
            prob, moved = [], []
            for q, g, (r, at) in zip(query, grads, work):
                head = at // 64
                log = log_ref[r, qb]
                log = jnp.concatenate([log[head: head + 1], log[head + 1: head + 2]], axis=1)
                total = jnp.concatenate([sums[r][head: head + 1], sums[r][head + 1: head + 2]], axis=1)
                scores = dot_nt(joined_ref[r, keys, pl.ds(width + at, 128)], q)
                change = dot_nt(joined_ref[r, keys, pl.ds(2 * width + at, 128)], g)
                p = jnp.exp(scores + bias[r] - log)
                prob.append(p.astype(BF16))
                moved.append((p * (change - total)).astype(BF16))
            for p, g, (r, at) in zip(prob, grads, work):
                dv_ref[r, keys, pl.ds(at, 128)] += dot(p, g)
            for m, q, (r, at) in zip(moved, query, work):
                dk_ref[r, keys, pl.ds(at, 128)] += dot(m, q)
            back = [dot_tn(m, joined_ref[r, keys, pl.ds(width + at, 128)]) for m, (r, at) in zip(moved, work)]
            for b, (r, at) in zip(back, work):
                out_ref[r, own, pl.ds(at, 128)] = (join_heads(b) * 0.125).astype(BF16)

        for blocks in range(1, 6):
            pl.when(qb - lo + 1 == blocks)(functools.partial(variant, blocks))
        return 0

    lax.fori_loop(0, count, block, 0)
    out_ref[:, :, width: 2 * width] = dk_ref[...].astype(BF16)
    out_ref[:, :, 2 * width:] = dv_ref[...].astype(BF16)


def attn_bwd(joined, grads, attended, logs, starts, lows, vlens, row_from, row_to, held=None, batch=1):
    rows, length, triple = joined.shape
    width = triple // 3
    count = length // QB
    aliased = [] if held is None else [held]
    skip = row_from // batch
    wide = pl.BlockSpec((batch, length, triple), lambda r, *_: (r + skip, 0, 0))
    slim = pl.BlockSpec((batch, length, width), lambda r, *_: (r + skip, 0, 0))
    return pl.pallas_call(
        functools.partial(attn_bwd_kernel, width, row_from, batch, count),
        grid_spec=pltpu.PrefetchScalarGridSpec(
            num_scalar_prefetch=2,
            grid=((row_to - row_from) // batch,),
            in_specs=[
                pl.BlockSpec((batch, count, QB), lambda r, *_: (r + skip, 0, 0)),
                wide,
                slim,
                slim,
                pl.BlockSpec((batch,) + logs.shape[1:], lambda r, *_: (r + skip, 0, 0, 0)),
            ]
            + [pl.BlockSpec(memory_space=pltpu.HBM) for _ in aliased],
            out_specs=wide,
            scratch_shapes=[
                pltpu.VMEM((batch, length, width), F32),
                pltpu.VMEM((batch, length, width), F32),
                pltpu.VMEM((batch, 5 * QB, QB), F32),
            ],
        ),
        out_shape=jax.ShapeDtypeStruct(joined.shape, BF16),
        input_output_aliases={7: 0} if aliased else {},
        compiler_params=pltpu.CompilerParams(vmem_limit_bytes=48 << 20),
        cost_estimate=pl.CostEstimate(
            flops=row_to * length * 400 * 8 * 256 * 20 if aliased else rows,
            bytes_accessed=rows * length,
            transcendentals=0,
        ),
        name="attend_back",
    )(lows, vlens, starts, joined, grads, attended, logs, *aliased)


def normalise(values):
    centred = values - jnp.mean(values, axis=-1, keepdims=True)
    inverse = lax.rsqrt(jnp.mean(centred * centred, axis=-1, keepdims=True) + 1e-05)
    return centred * inverse, inverse


def pull_norm(scaled, hat, inverse):
    return inverse * (
        scaled
        - jnp.mean(scaled, axis=-1, keepdims=True)
        - hat * jnp.mean(scaled * hat, axis=-1, keepdims=True)
    )


PIECE = 256


def pieces(count):
    return [slice(at, min(at + PIECE, count)) for at in range(0, count, PIECE)]


def constant_spec(shape, *where):
    where = where or (0,) * len(shape)
    return pl.BlockSpec(shape, lambda *_: where)


def join_kernel(tokens_ref, gains_ref, weight_ref, joined_ref):
    for at in pieces(tokens_ref.shape[1]):
        hat, _ = normalise(tokens_ref[0, at].astype(F32))
        normed = (hat * gains_ref[0:1] + gains_ref[1:2]).astype(BF16)
        joined_ref[0, at] = dot(normed, weight_ref[...]).astype(BF16)


def join_tokens(tokens, gains, packed, tile=1024):
    rows, length, width = tokens.shape
    return pl.pallas_call(
        join_kernel,
        grid=(rows, length // tile),
        in_specs=[
            pl.BlockSpec((1, tile, width), lambda r, t: (r, t, 0)),
            constant_spec(gains.shape),
            constant_spec((width, 3 * width)),
        ],
        out_specs=pl.BlockSpec((1, tile, 3 * width), lambda r, t: (r, t, 0)),
        out_shape=jax.ShapeDtypeStruct((rows, length, 3 * width), BF16),
        compiler_params=pltpu.CompilerParams(vmem_limit_bytes=40 << 20),
        cost_estimate=pl.CostEstimate(
            flops=rows * length * width * width * 6, bytes_accessed=rows * length * width * 8, transcendentals=0
        ),
        name="join",
    )(tokens, gains, packed)


def mixed_kernel(attended_ref, tokens_ref, gains_ref, weight_ref, router_ref, hidden_ref, mixed_ref, logits_ref):
    hidden = tokens_ref[0].astype(F32) + dot(attended_ref[0], weight_ref[...])
    hidden_ref[0] = hidden
    hat, _ = normalise(hidden)
    mixed = (hat * gains_ref[2:3] + gains_ref[3:4]).astype(BF16)
    mixed_ref[0] = mixed
    logits_ref[0] = dot_nt(router_ref[...], mixed)


def mix_tokens(attended, tokens, gains, packed, router, offset, tile=1024):
    rows, span, width = attended.shape
    block = pl.BlockSpec((1, tile, width), lambda r, t: (r, t, 0))
    return pl.pallas_call(
        mixed_kernel,
        grid=(rows, span // tile),
        in_specs=[
            block,
            pl.BlockSpec((1, tile, width), lambda r, t: (r, t + offset // tile, 0)),
            constant_spec(gains.shape),
            constant_spec((width, width), 0, 3),
            constant_spec(router.shape),
        ],
        out_specs=[block, block, pl.BlockSpec((1, router.shape[0], tile), lambda r, t: (r, 0, t))],
        out_shape=[
            jax.ShapeDtypeStruct((rows, span, width), F32),
            jax.ShapeDtypeStruct((rows, span, width), BF16),
            jax.ShapeDtypeStruct((rows, router.shape[0], span), F32),
        ],
        compiler_params=pltpu.CompilerParams(vmem_limit_bytes=40 << 20),
        cost_estimate=pl.CostEstimate(
            flops=rows * span * width * width * 2, bytes_accessed=rows * span * width * 10, transcendentals=0
        ),
        name="mix",
    )(attended, tokens, gains, packed, router)


def pool_kernel(experts, scale, slots_ref, gates_ref, values_ref, out_ref):
    rows, places = values_ref.shape[0], values_ref.shape[1]
    sub = 16

    def step(s, _):
        here = pl.ds(pl.multiple_of(s * sub, sub), sub)
        gates = gates_ref[here, :].astype(BF16).astype(F32)
        values = [values_ref[r, here, :].astype(F32) for r in range(rows)]
        for e in range(experts):
            total = sum(gates[:, r * experts + e: r * experts + e + 1] * values[r] for r in range(rows))
            out_ref[0, e, here, :] = (scale * total).astype(BF16)
        return 0

    lax.fori_loop(0, places // sub, step, 0, unroll=8)


def pool_tokens(slots, gates, values, experts, scale):
    rows, span, width = values.shape
    owners = slots.shape[0]
    places = span // owners
    return pl.pallas_call(
        functools.partial(pool_kernel, experts, scale),
        grid_spec=pltpu.PrefetchScalarGridSpec(
            num_scalar_prefetch=1,
            grid=(owners,),
            in_specs=[
                pl.BlockSpec((places, gates.shape[1]), lambda i, slots: (slots[i], 0)),
                pl.BlockSpec((rows, places, width), lambda i, slots: (0, slots[i], 0)),
            ],
            out_specs=pl.BlockSpec((1, experts, places, width), lambda i, slots: (i, 0, 0, 0)),
        ),
        out_shape=jax.ShapeDtypeStruct((owners, experts, places, width), BF16),
        compiler_params=pltpu.CompilerParams(vmem_limit_bytes=40 << 20),
        cost_estimate=pl.CostEstimate(
            flops=rows * span * width * 1000, bytes_accessed=rows * span * width * 8, transcendentals=0
        ),
        name="pool",
    )(slots, gates, values)


CUBIC = 0.044715
SLOPE = math.sqrt(2.0 / math.pi)


def expert_kernel(steps, pooled_ref, weights_ref, result_ref, act_ref, slope_ref, total_ref):
    step = pl.program_id(0)
    blocks, places, width = pooled_ref.shape
    pooled = pooled_ref[...].reshape(blocks * places, width)
    pre = dot(pooled, weights_ref[0, 0])
    square = pre * pre
    bent = jnp.tanh(SLOPE * pre * (1.0 + CUBIC * square))
    half = 0.5 * (1.0 + bent)
    act = (pre * half).astype(BF16)
    act_ref[0] = act
    slope_ref[0] = half + 0.5 * pre * (1.0 - bent * bent) * (SLOPE * (1.0 + 3.0 * CUBIC * square))
    result = dot_nt(act, weights_ref[0, 1])

    @pl.when(step == 0)
    def _():
        total_ref[...] = result

    @pl.when(step > 0)
    def _():
        total_ref[...] += result

    @pl.when(step == steps - 1)
    def _():
        result_ref[...] = total_ref[...].astype(BF16).reshape(blocks, places, width)


def run_experts(pooled, weights):
    blocks, places, width = pooled.shape
    steps, _, _, tile = weights.shape
    count = blocks * places
    return pl.pallas_call(
        functools.partial(expert_kernel, steps),
        grid=(steps,),
        in_specs=[constant_spec(pooled.shape), pl.BlockSpec((1, 2, width, tile), lambda i: (i, 0, 0, 0))],
        out_specs=[
            constant_spec(pooled.shape),
            pl.BlockSpec((1, count, tile), lambda i: (i, 0, 0)),
            pl.BlockSpec((1, count, tile), lambda i: (i, 0, 0)),
        ],
        out_shape=[
            jax.ShapeDtypeStruct(pooled.shape, BF16),
            jax.ShapeDtypeStruct((steps, count, tile), BF16),
            jax.ShapeDtypeStruct((steps, count, tile), F32),
        ],
        scratch_shapes=[pltpu.VMEM((count, width), F32)],
        compiler_params=pltpu.CompilerParams(vmem_limit_bytes=40 << 20),
        cost_estimate=pl.CostEstimate(
            flops=count * width * tile * steps * 8, bytes_accessed=width * tile * steps * 8, transcendentals=0
        ),
        name="experts",
    )(pooled, weights)


def expert_back_kernel(steps, slots_ref, pooled_ref, grads_ref, result_ref, act_ref, slope_ref, weights_ref, back_ref, grad_ref, total_ref):
    step = pl.program_id(0)
    blocks, places, width = pooled_ref.shape
    count = blocks * places
    pooled = pooled_ref[...].reshape(count, width)
    grads = grads_ref[...].reshape(count, width)
    act = act_ref[0]
    grad_pre = (dot(grads, weights_ref[0, 1]) * slope_ref[0]).astype(BF16)
    grad_ref[0, 0] = dot_tn(pooled, grad_pre).astype(BF16)
    grad_ref[0, 1] = dot_tn(grads, act).astype(BF16)
    part = dot_nt(grad_pre, weights_ref[0, 0])

    @pl.when(step == 0)
    def _():
        total_ref[...] = part

    @pl.when(step > 0)
    def _():
        total_ref[...] += part

    @pl.when(step == steps - 1)
    def _():
        grad_pooled = total_ref[...].astype(BF16)
        back_ref[:, :places] = grad_pooled.reshape(blocks, places, width)
        result = result_ref[...].reshape(count, width)
        product = result.astype(F32) * grads.astype(F32) + grad_pooled.astype(F32) * pooled.astype(F32)
        high = product.astype(BF16)
        rest = (product - high.astype(F32)).astype(BF16)
        ones = jnp.ones((16, width), BF16)
        sums = dot_nt(ones, high) + dot_nt(ones, rest)
        top = sums.astype(BF16)
        low = (sums - top.astype(F32)).astype(BF16)
        for b in range(blocks):
            here = slice(b * places, b * places + places)
            fill = jnp.zeros((16, width - 2 * places), BF16)
            back_ref[b, places:] = jnp.concatenate([top[:, here], low[:, here], fill], axis=1)


def pull_experts(slots, pooled, grads, result, act, slope, weights):
    blocks, places, width = pooled.shape
    steps, _, _, tile = weights.shape
    count = blocks * places
    return pl.pallas_call(
        functools.partial(expert_back_kernel, steps),
        grid_spec=pltpu.PrefetchScalarGridSpec(
            num_scalar_prefetch=1,
            grid=(steps,),
            in_specs=[constant_spec(pooled.shape)] * 3
            + [pl.BlockSpec((1, count, tile), lambda i, slots: (i, 0, 0))] * 2
            + [pl.BlockSpec((1, 2, width, tile), lambda i, slots: (i, 0, 0, 0))],
            out_specs=[
                constant_spec((blocks, places + 16, width)),
                pl.BlockSpec((1, 2, width, tile), lambda i, slots: (slots[i], 0, 0, 0)),
            ],
            scratch_shapes=[pltpu.VMEM((count, width), F32)],
        ),
        out_shape=[
            jax.ShapeDtypeStruct((blocks, places + 16, width), BF16),
            jax.ShapeDtypeStruct(weights.shape, BF16),
        ],
        compiler_params=pltpu.CompilerParams(vmem_limit_bytes=40 << 20),
        cost_estimate=pl.CostEstimate(
            flops=count * width * tile * steps * 12, bytes_accessed=width * tile * steps * 8, transcendentals=0
        ),
        name="pull_experts",
    )(slots, pooled, grads, result, act, slope, weights)


def spread_kernel(group, count, slots_ref, gates_ref, grads_ref, hidden_ref, *rest):
    parts, (out_ref, change_ref, result_ref) = rest[:count], rest[-3:]
    for k in range(count):
        @pl.when(pl.program_id(0) == k)
        def _():
            result_ref[...] = parts[k][...]

    rows, places = grads_ref.shape[0], grads_ref.shape[1]
    experts = result_ref.shape[0]
    sub = 16
    columns = gates_ref.shape[1]

    def step(s, _):
        here = pl.ds(pl.multiple_of(s * sub, sub), sub)
        results = [result_ref[e, here, :].astype(F32) * group for e in range(experts)]
        gates = gates_ref[here, :].astype(BF16).astype(F32)
        lane = iota((sub, columns), 1)
        changes = jnp.zeros((sub, columns), F32)
        for r in range(rows):
            grads = grads_ref[r, here, :].astype(F32)
            for e in range(experts):
                both = jnp.sum(grads * results[e], axis=1, keepdims=True)
                changes = jnp.where(lane == r * experts + e, both, changes)
            total = sum(gates[:, r * experts + e: r * experts + e + 1] * results[e] for e in range(experts))
            out_ref[r, here, :] = (hidden_ref[r, here, :] + total.astype(BF16).astype(F32)).astype(BF16)
        change_ref[0, here, :] = changes
        return 0

    lax.fori_loop(0, places // sub, step, 0, unroll=8)


def slot_of(found):
    found = list(found)
    step = found[-1] - found[0]
    return lambda i, slots: slots[found[0] + i * step]


def spread_tokens(found, slots, gates, cotangent, hidden, group, held):
    rows, span, width = hidden.shape
    parts = list(found.values())
    experts, places, _ = parts[0].shape
    at = slot_of(found)
    block = pl.BlockSpec((rows, places, width), lambda i, slots: (0, at(i, slots), 0))
    columns = gates.shape[1]
    aliased = [] if held is None else [held]
    return pl.pallas_call(
        functools.partial(spread_kernel, group, len(parts)),
        grid_spec=pltpu.PrefetchScalarGridSpec(
            num_scalar_prefetch=1,
            grid=(len(parts),),
            in_specs=[pl.BlockSpec((places, columns), lambda i, slots: (at(i, slots), 0)), block, block]
            + [constant_spec(part.shape) for part in parts]
            + [pl.BlockSpec(memory_space=pltpu.HBM) for _ in aliased],
            out_specs=[block, pl.BlockSpec((1, places, columns), lambda i, slots: (i, 0, 0))],
            scratch_shapes=[pltpu.VMEM(parts[0].shape, BF16)],
        ),
        out_shape=[
            jax.ShapeDtypeStruct((rows, span, width), BF16),
            jax.ShapeDtypeStruct((len(parts), places, columns), F32),
        ],
        input_output_aliases={4 + len(parts): 0} if aliased else {},
        compiler_params=pltpu.CompilerParams(vmem_limit_bytes=58 << 20),
        cost_estimate=pl.CostEstimate(
            flops=len(parts) * rows * places * width * 5000, bytes_accessed=rows * places * width * 10, transcendentals=0
        ),
        name="spread",
    )(slots, gates, cotangent, hidden, *parts, *aliased)


def pull_kernel(first, count, slots_ref, gates_ref, change_ref, mixed_ref, hidden_ref, cotangent_ref, attended_ref, router_ref, gains_ref, weight_ref, *rest):
    parts, rest = rest[:count], rest[count:]
    out_ref, low_ref, router_grad_ref, project_ref, sums_ref, pooled_ref, logits_ref, grad_ref = rest[-8:]

    @pl.when(pl.program_id(0) == 0)
    def _():
        if first:
            router_grad_ref[...] = jnp.zeros_like(router_grad_ref)
            project_ref[...] = jnp.zeros_like(project_ref)
            sums_ref[...] = jnp.zeros_like(sums_ref)
        else:
            router_grad_ref[...] = rest[2][...]
            project_ref[...] = rest[3][...]
            sums_ref[...] = rest[4][...]

    for k in range(count):
        @pl.when(pl.program_id(0) == k)
        def _():
            pooled_ref[...] = parts[k][...]

    rows, places, width = mixed_ref.shape
    experts = pooled_ref.shape[0]
    sub = 16
    columns = gates_ref.shape[1]
    inner = jnp.zeros((places, columns), F32)
    for e in range(experts):
        pick = (iota((16, columns), 0) == 0) & (iota((16, columns), 1) % experts == e)
        pick = jnp.where(pick, 1.0, 0.0).astype(BF16)
        inner += dot_tn(pooled_ref[e, places:, :places], pick) + dot_tn(pooled_ref[e, places:, places: 2 * places], pick)

    def change(s, _):
        here = pl.ds(pl.multiple_of(s * sub, sub), sub)
        pooled = [pooled_ref[e, here, :].astype(F32) for e in range(experts)]
        lane = iota((sub, columns), 1)
        changes = jnp.zeros((sub, columns), F32)
        for r in range(rows):
            mixed = mixed_ref[r, here, :].astype(F32)
            for e in range(experts):
                both = jnp.sum(pooled[e] * mixed, axis=1, keepdims=True)
                changes = jnp.where(lane == r * experts + e, both, changes)
        logits_ref[here, :] = changes
        return 0

    lax.fori_loop(0, places // sub, change, 0, unroll=8)
    changes = (logits_ref[...] + change_ref[0]).astype(BF16).astype(F32)
    low = (gates_ref[...] * (changes - inner)).astype(BF16)
    for r in range(rows):
        grad_ref[r] = dot(low, router_ref[r])
        router_grad_ref[...] += dot_tn(low, mixed_ref[r])[r * experts: r * experts + experts]

    def spread(s, _):
        here = pl.ds(pl.multiple_of(s * sub, sub), sub)
        pooled = [pooled_ref[e, here, :].astype(F32) for e in range(experts)]
        gates = gates_ref[here, :].astype(BF16).astype(F32)
        for r in range(rows):
            grad_ref[r, here, :] = sum(
                (gates[:, r * experts + e: r * experts + e + 1] * pooled[e] for e in range(experts)),
                grad_ref[r, here, :],
            )
        return 0

    lax.fori_loop(0, places // sub, spread, 0, unroll=8)

    for r in range(rows):
        grads = grad_ref[r].astype(BF16).astype(F32)
        hat, inverse = normalise(hidden_ref[r])
        sums_ref[0:1] += jnp.sum(grads * hat, axis=0, keepdims=True)
        sums_ref[1:2] += jnp.sum(grads, axis=0, keepdims=True)
        total = cotangent_ref[r].astype(F32) + pull_norm(grads * gains_ref[2:3], hat, inverse)
        out_ref[r] = total
        total = total.astype(BF16)
        project_ref[...] += dot_tn(attended_ref[r], total)
        low_ref[r] = dot_nt(total, weight_ref[...]).astype(BF16)


def pull_slots(found, slots, gates, change, mixed, hidden, cotangent, attended, router, gains, packed, held, weight=20):
    rows, span, width = mixed.shape
    parts = list(found.values())
    experts, depth, _ = parts[0].shape
    places = span // slots.shape[0]
    at = slot_of(found)
    block = pl.BlockSpec((rows, places, width), lambda i, slots: (0, at(i, slots), 0))
    columns = gates.shape[1]
    sums = [(experts, width), (width, width), (8, width)]
    ins = [
        pl.BlockSpec((places, columns), lambda i, slots: (at(i, slots), 0)),
        pl.BlockSpec((1, places, columns), lambda i, slots: (i, 0, 0)),
        block,
        block,
        block,
        block,
        constant_spec(router.shape),
        constant_spec(gains.shape),
        constant_spec((width, width), 0, 3),
    ] + [constant_spec(part.shape) for part in parts]
    aliases = {}
    if held is not None:
        aliases = {len(ins) + 1: 0, len(ins) + 2: 1}
        ins += [pl.BlockSpec(memory_space=pltpu.HBM)] * 2 + [constant_spec(shape) for shape in sums]
    return pl.pallas_call(
        functools.partial(pull_kernel, held is None, len(parts)),
        grid_spec=pltpu.PrefetchScalarGridSpec(
            num_scalar_prefetch=1,
            grid=(len(parts),),
            in_specs=ins,
            out_specs=[block, block] + [constant_spec(shape) for shape in sums],
            scratch_shapes=[
                pltpu.VMEM(parts[0].shape, BF16),
                pltpu.VMEM((places, columns), F32),
                pltpu.VMEM((rows, places, width), F32),
            ],
        ),
        out_shape=[jax.ShapeDtypeStruct((rows, span, width), F32), jax.ShapeDtypeStruct((rows, span, width), BF16)]
        + [jax.ShapeDtypeStruct(shape, F32) for shape in sums],
        input_output_aliases=aliases,
        compiler_params=pltpu.CompilerParams(vmem_limit_bytes=58 << 20),
        cost_estimate=pl.CostEstimate(
            flops=len(parts) * rows * places * width * width * weight,
            bytes_accessed=rows * places * weight,
            transcendentals=0,
        ),
        name="pull_slots",
    )(slots, gates, change, mixed, hidden, cotangent, attended, router, gains, packed, *parts, *(held or ()))


def project_kernel(experts, grads_ref, tokens_ref, gains_ref, weight_ref, project_ref, late_ref, out_ref, product_ref, sums_ref):
    width, wide = product_ref.shape
    steps = pl.num_programs(0) * pl.num_programs(1)
    step = pl.program_id(0) * pl.num_programs(1) + pl.program_id(1)

    @pl.when(step == 0)
    def _():
        product_ref[...] = jnp.zeros_like(product_ref)
        sums_ref[...] = jnp.zeros_like(sums_ref)

    hat = normalise(tokens_ref[0].astype(F32))[0].astype(BF16)
    ones = jnp.ones((hat.shape[0], 8), BF16)
    product_ref[...] += dot_tn(hat, grads_ref[0])
    sums_ref[...] += dot_tn(ones, grads_ref[0])

    @pl.when(step == steps - 1)
    def _():
        sums = sums_ref[0:1, :]
        for at in range(0, width, 64):
            here = slice(at, at + 64)
            product = product_ref[here, :]
            weights = weight_ref[here, :].astype(F32)
            out_ref[here, :wide] = (gains_ref[here, 0:1] * product + gains_ref[here, 1:2] * sums).astype(BF16)
            out_ref[here, wide: wide + width] = project_ref[here, :].astype(BF16)
            late = late_ref[here, :]
            lane = iota(late.shape, 1)
            late = jnp.where(lane == experts, jnp.sum(weights * product, axis=1, keepdims=True), late)
            late = jnp.where(lane == experts + 1, jnp.sum(weights * sums, axis=1, keepdims=True), late)
            out_ref[here, wide + width:] = late.astype(BF16)


def project_grads(grads, tokens, gains, packed, project, late, experts, tile=1024):
    rows, length, width = tokens.shape
    wide = 3 * width
    return pl.pallas_call(
        functools.partial(project_kernel, experts),
        grid=(rows, length // tile),
        in_specs=[
            pl.BlockSpec((1, tile, wide), lambda r, t: (r, t, 0)),
            pl.BlockSpec((1, tile, width), lambda r, t: (r, t, 0)),
            constant_spec(gains.shape),
            constant_spec((width, wide)),
            constant_spec(project.shape),
            constant_spec(late.shape),
        ],
        out_specs=constant_spec(packed.shape),
        out_shape=jax.ShapeDtypeStruct(packed.shape, BF16),
        scratch_shapes=[pltpu.VMEM((width, wide), F32), pltpu.VMEM((8, wide), F32)],
        compiler_params=pltpu.CompilerParams(vmem_limit_bytes=48 << 20),
        cost_estimate=pl.CostEstimate(flops=rows, bytes_accessed=rows, transcendentals=0),
        name="project_grads",
    )(grads, tokens, gains, packed, project, late)


def tokens_kernel(grads_ref, tokens_ref, hidden_ref, gains_ref, weight_ref, *rest):
    out_ref = rest[-1]
    for at in pieces(tokens_ref.shape[1]):
        hat, inverse = normalise(tokens_ref[0, at].astype(F32))
        grads = dot_nt(grads_ref[0, at], weight_ref[...])
        out_ref[0, at] = hidden_ref[0, at] + pull_norm(grads * gains_ref[0:1], hat, inverse)


def pull_tokens(grads, tokens, hidden, gains, packed, row_from, row_to, held=None, tile=1024):
    rows, length, width = tokens.shape
    block = pl.BlockSpec((1, tile, width), lambda r, t: (r + row_from, t, 0))
    aliased = [] if held is None else [held]
    return pl.pallas_call(
        tokens_kernel,
        grid=(row_to - row_from, length // tile),
        in_specs=[
            pl.BlockSpec((1, tile, 3 * width), lambda r, t: (r + row_from, t, 0)),
            block,
            block,
            constant_spec(gains.shape),
            constant_spec((width, 3 * width)),
        ]
        + [pl.BlockSpec(memory_space=pltpu.HBM) for _ in aliased],
        out_specs=block,
        out_shape=jax.ShapeDtypeStruct((rows, length, width), F32),
        input_output_aliases={5: 0} if aliased else {},
        compiler_params=pltpu.CompilerParams(vmem_limit_bytes=58 << 20),
        cost_estimate=pl.CostEstimate(
            flops=(row_to - row_from) * length * width * width * 20,
            bytes_accessed=(row_to - row_from) * length * width * 16,
            transcendentals=0,
        ),
        name="pull_tokens",
    )(grads, tokens, hidden, gains, packed, *aliased)


def ring_order(size):
    inner = 2 if size % 2 == 0 and size > 2 else 1
    outer = size // inner
    up = [z * inner for z in range(outer)]
    if inner == 1:
        return up
    return up + [z * inner + 1 for z in reversed(range(outer))]


def shift(value, order, step):
    count = len(order)
    return lax.ppermute(value, "dp", [(order[i], order[(i + step) % count]) for i in range(count)])


def flip(value, bit, axis="fsdp"):
    count = lax.axis_size(axis)
    return lax.ppermute(value, axis, [(i, i ^ bit) for i in range(count)])


def turn(value, step, axis="dp"):
    count = lax.axis_size(axis)
    return lax.ppermute(value, axis, [(i, (i + step) % count) for i in range(count)])


def take(values, index):
    starts = (index,) + (jnp.uint32(0),) * (values.ndim - 1)
    return lax.dynamic_slice(values, starts, (1,) + values.shape[1:])[0]


def put(values, value, index):
    return lax.dynamic_update_slice(values, value[None], (index,) + (jnp.uint32(0),) * value.ndim)


def add(a, b):
    return (a.astype(F32) + b.astype(F32)).astype(BF16)


def together(*values):
    return lax.optimization_barrier(values)


class Ring:
    def __init__(self, value, order):
        self.order, self.done = order, 0
        self.ahead = self.behind = value

    def left(self):
        return self.done < len(self.order) // 2

    def after(self, *values):
        self.ahead, self.behind, *_ = together(self.ahead, self.behind, *values)

    def step(self, *beside):
        count = len(self.order)
        self.done += 1
        slot = count - self.done
        ahead, behind = self.ahead, self.behind
        middle = 2 * self.done == count and ahead.shape[0] % 2 == 0
        if middle:
            half = ahead.shape[0] // 2
            ahead, behind = ahead[:half], behind[half:]
        ahead = shift(ahead, self.order, 1)
        if 2 * self.done < count or middle:
            behind = shift(behind, self.order, -1)
        ahead, behind, *beside = together(ahead, behind, *beside)
        self.ahead, self.behind = ahead, behind
        if middle:
            return {slot: jnp.concatenate([ahead, behind], axis=0)}, beside
        return {slot: ahead, self.done: behind} if 2 * self.done < count else {slot: ahead}, beside


def gather_all(value, steps, *beside):
    pair = pair_of(lax.axis_size("dp"))
    lines = lax.axis_size("dp") // pair
    size = lax.axis_size("fsdp")
    here = lax.axis_index("fsdp")

    def both(value, bit, axis, index):
        other = flip(value, bit, axis)
        upper = (index & bit) != 0
        return jnp.stack([jnp.where(upper, other, value), jnp.where(upper, value, other)])

    whole = put(jnp.zeros((lines,) + value.shape, value.dtype), value, steps[0])
    for k in range(1, lines):
        whole = put(whole, turn(value, -k * pair), steps[k])
    if beside:
        whole, *beside = together(whole, *beside)
    whole = both(whole, 1, "dp", lax.axis_index("dp")) if pair == 2 else whole[None]
    whole = jnp.moveaxis(whole, 0, 1)
    whole = whole.reshape((lines * pair, 1) + value.shape)
    bit = size // 2
    while bit:
        whole = both(whole, bit, "fsdp", here)
        whole = jnp.moveaxis(whole, 0, 2)
        whole = whole.reshape((lines * pair, -1) + value.shape)
        bit //= 2
    return whole, beside


def scatter_all(values, steps, work):
    owners, size = lax.axis_size("dp"), lax.axis_size("fsdp")
    bits = size.bit_length() - 1
    here = lax.axis_index("fsdp")
    width = values.shape[1]
    pair = pair_of(owners)
    work = list(work)

    def half(held, axis, upper, bit, name):
        low, high = (lax.index_in_dim(held, i, axis, keepdims=False) for i in (0, 1))
        came = flip(jnp.where(upper, low, high), bit, name)
        if work:
            came, = work.pop(0)(came)
        return add(jnp.where(upper, high, low), came)

    held = values.reshape((owners // pair, pair) + (2,) * bits + (-1, width))
    for level in range(bits):
        held = half(held, bits + 1 - level, ((here >> level) & 1) != 0, 1 << level, "fsdp")
    held = half(held, 1, (lax.axis_index("dp") & 1) != 0, 1, "dp") if pair == 2 else held[:, 0]
    came = [turn(take(held, steps[k]), k * pair) for k in range(1, owners // pair)]
    while work:
        came = work.pop(0)(*came)
    return sum((value.astype(F32) for value in came), take(held, steps[0]).astype(F32))


def pair_of(owners):
    return 2 if owners % 2 == 0 else 1


def exchange(values):
    return jnp.stack([values[0]] + [flip(values[k], k) for k in range(1, values.shape[0])])


def per_device(
    tokens,
    segment_ids,
    pad_tokens,
    cotangent,
    project_in,
    project_out,
    router_weight,
    expert_in,
    expert_out,
    first_gain,
    first_bias,
    second_gain,
    second_bias,
):
    blocks_here, rows, length, width = tokens.shape
    tokens = tokens.reshape(rows, length, width)
    cotangent = cotangent.reshape(rows, length, width)
    segments = segment_ids.reshape(rows, length)
    group = pad_tokens.shape[1]
    owners = lax.axis_size("dp")
    experts = router_weight.shape[1]
    order = ring_order(owners)
    data_index = lax.axis_index("dp")
    expert_index = lax.axis_index("fsdp")
    places = length // owners

    pair = pair_of(owners)
    lines = owners // pair
    ring = np.array([[order[(order.index(d) + k) % owners] for k in range(owners)] for d in range(owners)], np.int32)
    place = np.array(
        [[(o % pair ^ d % pair) * lines + (o // pair - d // pair) % lines for o in ring[d]] for d in range(owners)],
        np.int32,
    )
    line = np.array([[(d // pair + k) % lines for k in range(lines)] for d in range(owners)], np.int32)
    tables = np.concatenate([ring, place, line], axis=1)
    tables = lax.dynamic_slice(
        jnp.asarray(tables), (data_index.astype(jnp.uint32), jnp.uint32(0)), (1, tables.shape[1])
    )[0]
    slots, shares = tables[:owners], tables[owners: 2 * owners]
    spots = [tables[k].astype(jnp.uint32) for k in range(owners)]
    steps = [tables[2 * owners + k].astype(jnp.uint32) for k in range(lines)]

    vectors = jnp.stack([first_gain, first_bias, second_gain, second_bias], axis=1)
    small = jnp.concatenate([router_weight, vectors], axis=1)
    small = jnp.pad(small, ((0, 0), (0, 128 - small.shape[1])))
    packed = jnp.concatenate([project_in, project_out, small], axis=1)
    packed, (expert_in, expert_out) = gather_all(packed, steps, expert_in, expert_out)
    weights = jnp.stack([expert_in[0], expert_out[0].T])
    packed = packed.reshape(width, packed.shape[-1])
    packed, weights = together(packed, weights)
    kept = {0: weights}
    weights = Ring(weights, order)
    small = packed[:, 4 * width:].T
    mine = (jnp.arange(experts)[:, None] ^ jnp.arange(experts)[None, :]) == expert_index
    router = jnp.sum(jnp.where(mine[:, :, None], small[None, :experts], 0), axis=1).astype(BF16)
    spread_router = jnp.stack(
        [jnp.pad(router, ((r * experts, (rows - 1 - r) * experts), (0, 0))) for r in range(rows)]
    )
    gains = jnp.pad(small[experts: experts + 4].astype(F32), ((0, 4), (0, 0)))

    own_pads = lax.dynamic_slice_in_dim(pad_tokens[0], data_index * rows, rows, 0)
    vlens = (length - own_pads).astype(jnp.int32)
    starts = jnp.zeros_like(segments)
    for doc in range(1, 4):
        before = jnp.sum((segments < doc).astype(jnp.int32), axis=1, keepdims=True)
        starts = jnp.where(segments == doc, before, starts)
    starts = starts.reshape(rows, length // QB, QB)
    lows = starts[:, :, 0] // QB

    def meanwhile(value):
        if not weights.left():
            return value
        found, (value,) = weights.step(value)
        kept.update(found)
        return value

    joined = meanwhile(join_tokens(tokens, gains, packed))
    attended, logs = attn_fwd(joined, starts, lows, vlens, 1)
    attended = meanwhile(attended)
    hidden, mixed, logits = mix_tokens(
        attended, tokens, gains, packed, jnp.pad(router, ((0, 16 - experts), (0, 0))), 0
    )
    logits = meanwhile(logits)[:, :experts]
    valid = (jnp.arange(length)[None, :] < vlens[:, None])[:, None, :]
    highest = jnp.max(jnp.where(valid, logits, NEGATIVE), axis=0)
    total = jnp.sum(jnp.where(valid, jnp.exp(logits - highest), 0.0), axis=0)
    stats = jnp.stack([highest, total])[None]
    if pair == 2:
        stats = jnp.concatenate([stats, flip(stats, 1, "dp")])
    stats = jnp.concatenate([stats] + [turn(stats, k * pair) for k in range(1, lines)])
    tops = jnp.max(stats[:, 0], axis=0)
    total = jnp.sum(stats[:, 1] * jnp.exp(stats[:, 0] - tops), axis=0)
    gates = jnp.where(valid, jnp.exp(jnp.where(valid, logits - tops, NEGATIVE)) / total, 0.0)
    gates = gates.reshape(rows * experts, length).T
    pooled = meanwhile(pool_tokens(slots, gates, mixed, experts, 1.0))
    while weights.left():
        kept.update(weights.step()[0])
    weights = jnp.stack([kept[k] for k in range(owners)])
    grads = pool_tokens(slots, gates, cotangent, experts, float(group))

    half = experts // 2
    first = [(pooled[:, :half], 1), (pooled[:, half:], -1)]
    second = [(grads[:, :half], 1), (grads[:, half:], -1)]
    held = [part[-way % owners] for part, way in first]
    later = [part[-way % owners] for part, way in second]
    for step in range(owners - 1):
        came = [shift(value, order, way) for value, (_, way) in zip(held, first)]
        *came, one, two = together(*came, *later)
        later = [one, two]
        held = [add(value, part[-way * (2 + step) % owners]) for value, (part, way) in zip(came, first)]
        came = [shift(value, order, way) for value, (_, way) in zip(later, second)]
        later = [add(value, part[-way * (2 + step) % owners]) for value, (part, way) in zip(came, second)]
    pooled = exchange(jnp.concatenate(held, axis=0))
    result, act, slope = run_experts(pooled, weights)
    grads = exchange(jnp.concatenate(later, axis=0))
    grad_pooled, grad_weights = pull_experts(shares, pooled, grads, result, act, slope, weights)

    result = exchange(result)
    back = exchange(grad_pooled)

    def pull(found, change, out, *weight):
        return pull_slots(
            found, slots, gates, change, mixed, hidden, cotangent, attended, spread_router, gains, packed, out, *weight
        )

    def spread(found, out):
        return spread_tokens(found, slots, gates, cotangent, hidden, group, out)

    turns = owners // 2
    first, second = Ring(result, order), Ring(back, order)
    found, (grad_weights,) = first.step(grad_weights)
    groups, arrived = [{0: result}, found], [{0: back}]
    out, pulled, changes = None, None, []
    for step in range(turns + 1):
        work = []
        for k in [step] if step < turns - 1 else [turns - 1, turns] if step == turns - 1 else []:
            out, change = spread(groups[k], out)
            changes.append(change)
            work = [out]
        if 0 < step < turns - 1 or step == turns:
            k = step - 1 if step < turns else turns - 2
            pulled = pull(arrived[k], changes[k], pulled)
            work += pulled
        if step > 0:
            second.after(*groups[min(step + 1, turns)].values())
        if first.left():
            found, work = first.step(*work)
            groups.append(found)
        if second.left() and step > 0:
            found, work = second.step(*work)
            arrived.append(found)
        if step < turns:
            out, *work = work
        pulled = work or pulled
    pulled = pull(arrived[turns - 1], changes[turns - 1], pulled)
    layer_out = out
    grad_weights, *_ = together(grad_weights, *arrived[turns].values())
    if pair == 2:
        came = flip(grad_weights[lines:], 1, "dp")
    pulled = pull(arrived[turns], changes[turns], pulled, 0)
    grad_hidden, grad_attended, router_grad, grad_proj_out, sums_two = pulled
    split = rows - max(1, rows // 2)
    grads = attn_bwd(joined, grad_attended, attended, logs, starts, lows, vlens, 0, split)
    grad_weights = grad_weights[:lines]
    if pair == 2:
        came, grads = together(came, grads)
        grad_weights = add(grad_weights, came)
    grad_parts = [turn(grad_weights[k], k * pair) for k in range(1, lines)]
    grads = attn_bwd(joined, grad_attended, attended, logs, starts, lows, vlens, split, rows, grads)
    router_grad = jnp.sum(jnp.where(mine[:, :, None], router_grad[None], 0.0), axis=1)
    late = jnp.concatenate([router_grad, jnp.zeros((2, width), F32), sums_two[:2]], axis=0).T
    late = jnp.pad(late, ((0, 0), (0, 128 - late.shape[1])))
    reduced = project_grads(grads, tokens, gains.T, packed, grad_proj_out, late, experts)
    reduced, *grad_parts = together(reduced, *grad_parts)
    made = []

    def tokens_beside(*came):
        *came, grad = together(*came, pull_tokens(grads, tokens, grad_hidden, gains, packed, 0, rows))
        made.append(grad)
        return came

    def weights_beside(*came):
        value, *parts = together(*came, *grad_parts)
        made.append(sum((part.astype(F32) for part in parts), grad_weights[0].astype(F32)))
        return [value]

    reduced = scatter_all(reduced, steps, [lambda *came: came, tokens_beside, weights_beside])
    tokens_grad, grad_weights = made
    late = reduced[:, 4 * width:]
    return (
        layer_out[None],
        tokens_grad[None],
        reduced[:, : 3 * width],
        reduced[:, 3 * width: 4 * width],
        late[:, :experts],
        grad_weights[0][None],
        grad_weights[1].T[None],
        late[:, experts],
        late[:, experts + 1],
        late[:, experts + 2],
        late[:, experts + 3],
    )


def solution(mesh):
    in_specs = (
        P("fsdp", "dp", None, None),
        P("fsdp", "dp", None),
        P("fsdp", None),
        P("fsdp", "dp", None, None),
        P(("dp", "fsdp"), None),
        P(("dp", "fsdp"), None),
        P(("dp", "fsdp"), None),
        P("fsdp", None, "dp"),
        P("fsdp", "dp", None),
        P(("dp", "fsdp")),
        P(("dp", "fsdp")),
        P(("dp", "fsdp")),
        P(("dp", "fsdp")),
    )
    out_specs = (
        P("fsdp", "dp", None, None),
        P("fsdp", "dp", None, None),
        P(("dp", "fsdp"), None),
        P(("dp", "fsdp"), None),
        P(("dp", "fsdp"), None),
        P("fsdp", None, "dp"),
        P("fsdp", "dp", None),
        P(("dp", "fsdp")),
        P(("dp", "fsdp")),
        P(("dp", "fsdp")),
        P(("dp", "fsdp")),
    )
    return jax.shard_map(
        per_device, mesh=mesh, in_specs=in_specs, out_specs=out_specs, check_vma=False
    )
```

```python
import functools, math
import jax
import jax.numpy as jnp
import numpy as np
from jax import lax
from jax.experimental import pallas as pl
from jax.experimental.pallas import tpu as pltpu
from jax.sharding import PartitionSpec as P

NEGATIVE = -1e30
QB = 128
F32 = jnp.float32
BF16 = jnp.bfloat16
NT = (((1,), (1,)), ((), ()))
TN = (((0,), (0,)), ((), ()))


def dot(a, b):
    return jnp.dot(a, b, preferred_element_type=F32)


def dot_nt(a, b):
    return lax.dot_general(a, b, NT, preferred_element_type=F32)


def dot_tn(a, b):
    return lax.dot_general(a, b, TN, preferred_element_type=F32)


def iota(shape, axis):
    return lax.broadcasted_iota(jnp.int32, shape, axis)


def split_heads(x):
    low = iota(x.shape, 1) < 64
    zero = jnp.zeros_like(x)
    return jnp.concatenate([jnp.where(low, x, zero), jnp.where(low, zero, x)], axis=0)


def join_heads(x):
    half = x.shape[0] // 2
    low = iota((half, x.shape[1]), 1) < 64
    return jnp.where(low, x[:half], x[half:])


def attn_fwd_kernel(width, batch, count, lo_ref, vlen_ref, start_ref, joined_ref, out_ref, log_ref, bias_ref):
    row = pl.program_id(0) * batch

    def block(qb, _):
        lo = functools.reduce(jnp.minimum, [lo_ref[row + r, qb] for r in range(batch)])
        base = pl.multiple_of(qb * QB, QB)
        first = pl.multiple_of(lo * QB, QB)
        own = pl.ds(base, QB)

        def variant(blocks):
            span = blocks * QB
            keys = pl.ds(first, span)
            i = base + iota((QB, QB), 0)
            bias = []
            for r in range(batch):
                begins = jnp.broadcast_to(start_ref[r, pl.ds(qb, 1), :], (QB, QB)).T
                for b in range(blocks):
                    j = first + b * QB + iota((QB, QB), 1)
                    ok = ((j >= begins) & (j <= i) & (j < vlen_ref[row + r])) | (j == i)
                    bias_ref[r, :, b * QB:(b + 1) * QB] = jnp.where(ok, 0.0, NEGATIVE)
                bias.append(jnp.concatenate([bias_ref[r, :, :span]] * 2, axis=0))
            work = [(r, lane) for r in range(batch) for lane in range(0, width, 128)]
            query = [split_heads(joined_ref[r, own, pl.ds(at, 128)] * jnp.asarray(0.125, BF16)) for r, at in work]
            scores = [dot_nt(q, joined_ref[r, keys, pl.ds(width + at, 128)]) for q, (r, at) in zip(query, work)]
            scores = [s + bias[r] for s, (r, _) in zip(scores, work)]
            tops = [jnp.max(s, axis=1, keepdims=True) for s in scores]
            raised = [jnp.exp(s - top) for s, top in zip(scores, tops)]
            totals = [jnp.sum(p, axis=1, keepdims=True) for p in raised]
            out = [
                dot(p.astype(BF16), joined_ref[r, keys, pl.ds(2 * width + at, 128)]) for p, (r, at) in zip(raised, work)
            ]
            for o, total, (r, at) in zip(out, totals, work):
                out_ref[r, own, pl.ds(at, 128)] = join_heads(o * (1.0 / total)).astype(BF16)
            lane = iota((QB, QB), 1)
            for r in range(batch):
                tile = jnp.zeros((QB, QB), F32)
                for top, total, (other, at) in zip(tops, totals, work):
                    if other == r:
                        log = top + jnp.log(total)
                        tile = jnp.where(lane == at // 64, log[:QB], tile)
                        tile = jnp.where(lane == at // 64 + 1, log[QB:], tile)
                log_ref[r, pl.ds(qb, 1)] = tile.T[None, : log_ref.shape[2]]

        for blocks in range(1, 6):
            pl.when(qb - lo + 1 == blocks)(functools.partial(variant, blocks))
        return 0

    lax.fori_loop(0, count, block, 0)


def attn_fwd(joined, starts, lows, vlens, batch=2):
    rows, length, triple = joined.shape
    width = triple // 3
    count = length // QB
    return pl.pallas_call(
        functools.partial(attn_fwd_kernel, width, batch, count),
        grid_spec=pltpu.PrefetchScalarGridSpec(
            num_scalar_prefetch=2,
            grid=(rows // batch,),
            in_specs=[
                pl.BlockSpec((batch, count, QB), lambda r, *_: (r, 0, 0)),
                pl.BlockSpec((batch, length, triple), lambda r, *_: (r, 0, 0)),
            ],
            out_specs=[
                pl.BlockSpec((batch, length, width), lambda r, *_: (r, 0, 0)),
                pl.BlockSpec((batch, count, width // 64, QB), lambda r, *_: (r, 0, 0, 0)),
            ],
            scratch_shapes=[pltpu.VMEM((batch, QB, 5 * QB), F32)],
        ),
        out_shape=[
            jax.ShapeDtypeStruct((rows, length, width), BF16),
            jax.ShapeDtypeStruct((rows, count, width // 64, QB), F32),
        ],
        compiler_params=pltpu.CompilerParams(vmem_limit_bytes=48 << 20),
        cost_estimate=pl.CostEstimate(
            flops=rows * length * 400 * 8 * 256 * 4, bytes_accessed=rows * length * triple * 2, transcendentals=0
        ),
        name="attend",
    )(lows, vlens, starts, joined)


def attn_bwd_kernel(width, row_from, batch, count, lo_ref, vlen_ref, start_ref, joined_ref, grad_ref, attended_ref, log_ref, *rest):
    out_ref, dk_ref, dv_ref, bias_ref = rest[-4:]
    row = pl.program_id(0) * batch + row_from
    dk_ref[...] = jnp.zeros_like(dk_ref)
    dv_ref[...] = jnp.zeros_like(dv_ref)

    def block(qb, _):
        lo = functools.reduce(jnp.minimum, [lo_ref[row + r, qb] for r in range(batch)])
        base = pl.multiple_of(qb * QB, QB)
        first = pl.multiple_of(lo * QB, QB)
        own = pl.ds(base, QB)

        def variant(blocks):
            span = blocks * QB
            keys = pl.ds(first, span)
            i = base + iota((QB, QB), 1)
            pick = jnp.where(iota((16, width), 1) // 64 == iota((16, width), 0), 1.0, 0.0).astype(BF16)
            bias, sums = [], []
            for r in range(batch):
                begins = start_ref[r, pl.ds(qb, 1), :]
                for b in range(blocks):
                    j = first + b * QB + iota((QB, QB), 0)
                    ok = ((j >= begins) & (j <= i) & (j < vlen_ref[row + r])) | (j == i)
                    bias_ref[r, b * QB:(b + 1) * QB, :] = jnp.where(ok, 0.0, NEGATIVE)
                bias.append(jnp.concatenate([bias_ref[r, :span, :]] * 2, axis=1))
                product = grad_ref[r, own, :].astype(F32) * attended_ref[r, own, :].astype(F32)
                high = product.astype(BF16)
                sums.append(dot_nt(pick, high) + dot_nt(pick, (product - high.astype(F32)).astype(BF16)))
            work = [(r, lane) for r in range(batch) for lane in range(0, width, 128)]
            query = [split_heads(joined_ref[r, own, pl.ds(at, 128)] * jnp.asarray(0.125, BF16)) for r, at in work]
            grads = [split_heads(grad_ref[r, own, pl.ds(at, 128)]) for r, at in work]
            prob, moved = [], []
            for q, g, (r, at) in zip(query, grads, work):
                head = at // 64
                log = log_ref[r, qb]
                log = jnp.concatenate([log[head: head + 1], log[head + 1: head + 2]], axis=1)
                total = jnp.concatenate([sums[r][head: head + 1], sums[r][head + 1: head + 2]], axis=1)
                scores = dot_nt(joined_ref[r, keys, pl.ds(width + at, 128)], q)
                change = dot_nt(joined_ref[r, keys, pl.ds(2 * width + at, 128)], g)
                p = jnp.exp(scores + bias[r] - log)
                prob.append(p.astype(BF16))
                moved.append((p * (change - total)).astype(BF16))
            for p, g, (r, at) in zip(prob, grads, work):
                dv_ref[r, keys, pl.ds(at, 128)] += dot(p, g)
            for m, q, (r, at) in zip(moved, query, work):
                dk_ref[r, keys, pl.ds(at, 128)] += dot(m, q)
            back = [dot_tn(m, joined_ref[r, keys, pl.ds(width + at, 128)]) for m, (r, at) in zip(moved, work)]
            for b, (r, at) in zip(back, work):
                out_ref[r, own, pl.ds(at, 128)] = (join_heads(b) * 0.125).astype(BF16)

        for blocks in range(1, 6):
            pl.when(qb - lo + 1 == blocks)(functools.partial(variant, blocks))
        return 0

    lax.fori_loop(0, count, block, 0)
    out_ref[:, :, width: 2 * width] = dk_ref[...].astype(BF16)
    out_ref[:, :, 2 * width:] = dv_ref[...].astype(BF16)


def attn_bwd(joined, grads, attended, logs, starts, lows, vlens, row_from, row_to, held=None, batch=1):
    rows, length, triple = joined.shape
    width = triple // 3
    count = length // QB
    aliased = [] if held is None else [held]
    skip = row_from // batch
    wide = pl.BlockSpec((batch, length, triple), lambda r, *_: (r + skip, 0, 0))
    slim = pl.BlockSpec((batch, length, width), lambda r, *_: (r + skip, 0, 0))
    return pl.pallas_call(
        functools.partial(attn_bwd_kernel, width, row_from, batch, count),
        grid_spec=pltpu.PrefetchScalarGridSpec(
            num_scalar_prefetch=2,
            grid=((row_to - row_from) // batch,),
            in_specs=[
                pl.BlockSpec((batch, count, QB), lambda r, *_: (r + skip, 0, 0)),
                wide,
                slim,
                slim,
                pl.BlockSpec((batch,) + logs.shape[1:], lambda r, *_: (r + skip, 0, 0, 0)),
            ]
            + [pl.BlockSpec(memory_space=pltpu.HBM) for _ in aliased],
            out_specs=wide,
            scratch_shapes=[
                pltpu.VMEM((batch, length, width), F32),
                pltpu.VMEM((batch, length, width), F32),
                pltpu.VMEM((batch, 5 * QB, QB), F32),
            ],
        ),
        out_shape=jax.ShapeDtypeStruct(joined.shape, BF16),
        input_output_aliases={7: 0} if aliased else {},
        compiler_params=pltpu.CompilerParams(vmem_limit_bytes=48 << 20),
        cost_estimate=pl.CostEstimate(
            flops=row_to * length * 400 * 8 * 256 * 20 if aliased else rows,
            bytes_accessed=rows * length,
            transcendentals=0,
        ),
        name="attend_back",
    )(lows, vlens, starts, joined, grads, attended, logs, *aliased)


def normalise(values):
    centred = values - jnp.mean(values, axis=-1, keepdims=True)
    inverse = lax.rsqrt(jnp.mean(centred * centred, axis=-1, keepdims=True) + 1e-05)
    return centred * inverse, inverse


def pull_norm(scaled, hat, inverse):
    return inverse * (
        scaled
        - jnp.mean(scaled, axis=-1, keepdims=True)
        - hat * jnp.mean(scaled * hat, axis=-1, keepdims=True)
    )


PIECE = 256


def pieces(count):
    return [slice(at, min(at + PIECE, count)) for at in range(0, count, PIECE)]


def constant_spec(shape, *where):
    where = where or (0,) * len(shape)
    return pl.BlockSpec(shape, lambda *_: where)


def join_kernel(tokens_ref, gains_ref, weight_ref, joined_ref):
    for at in pieces(tokens_ref.shape[1]):
        hat, _ = normalise(tokens_ref[0, at].astype(F32))
        normed = (hat * gains_ref[0:1] + gains_ref[1:2]).astype(BF16)
        joined_ref[0, at] = dot(normed, weight_ref[...]).astype(BF16)


def join_tokens(tokens, gains, packed, tile=1024):
    rows, length, width = tokens.shape
    return pl.pallas_call(
        join_kernel,
        grid=(rows, length // tile),
        in_specs=[
            pl.BlockSpec((1, tile, width), lambda r, t: (r, t, 0)),
            constant_spec(gains.shape),
            constant_spec((width, 3 * width)),
        ],
        out_specs=pl.BlockSpec((1, tile, 3 * width), lambda r, t: (r, t, 0)),
        out_shape=jax.ShapeDtypeStruct((rows, length, 3 * width), BF16),
        compiler_params=pltpu.CompilerParams(vmem_limit_bytes=40 << 20),
        cost_estimate=pl.CostEstimate(
            flops=rows * length * width * width * 6, bytes_accessed=rows * length * width * 8, transcendentals=0
        ),
        name="join",
    )(tokens, gains, packed)


def mixed_kernel(attended_ref, tokens_ref, gains_ref, weight_ref, router_ref, hidden_ref, mixed_ref, logits_ref):
    hidden = tokens_ref[0].astype(F32) + dot(attended_ref[0], weight_ref[...])
    hidden_ref[0] = hidden
    hat, _ = normalise(hidden)
    mixed = (hat * gains_ref[2:3] + gains_ref[3:4]).astype(BF16)
    mixed_ref[0] = mixed
    logits_ref[0] = dot_nt(router_ref[...], mixed)


def mix_tokens(attended, tokens, gains, packed, router, offset, tile=1024):
    rows, span, width = attended.shape
    block = pl.BlockSpec((1, tile, width), lambda r, t: (r, t, 0))
    return pl.pallas_call(
        mixed_kernel,
        grid=(rows, span // tile),
        in_specs=[
            block,
            pl.BlockSpec((1, tile, width), lambda r, t: (r, t + offset // tile, 0)),
            constant_spec(gains.shape),
            constant_spec((width, width), 0, 3),
            constant_spec(router.shape),
        ],
        out_specs=[block, block, pl.BlockSpec((1, router.shape[0], tile), lambda r, t: (r, 0, t))],
        out_shape=[
            jax.ShapeDtypeStruct((rows, span, width), F32),
            jax.ShapeDtypeStruct((rows, span, width), BF16),
            jax.ShapeDtypeStruct((rows, router.shape[0], span), F32),
        ],
        compiler_params=pltpu.CompilerParams(vmem_limit_bytes=40 << 20),
        cost_estimate=pl.CostEstimate(
            flops=rows * span * width * width * 2, bytes_accessed=rows * span * width * 10, transcendentals=0
        ),
        name="mix",
    )(attended, tokens, gains, packed, router)


def pool_kernel(experts, scale, slots_ref, gates_ref, values_ref, out_ref):
    rows, places = values_ref.shape[0], values_ref.shape[1]
    sub = 16

    def step(s, _):
        here = pl.ds(pl.multiple_of(s * sub, sub), sub)
        gates = gates_ref[here, :].astype(BF16).astype(F32)
        values = [values_ref[r, here, :].astype(F32) for r in range(rows)]
        for e in range(experts):
            total = sum(gates[:, r * experts + e: r * experts + e + 1] * values[r] for r in range(rows))
            out_ref[0, e, here, :] = (scale * total).astype(BF16)
        return 0

    lax.fori_loop(0, places // sub, step, 0, unroll=8)


def pool_tokens(slots, gates, values, experts, scale):
    rows, span, width = values.shape
    owners = slots.shape[0]
    places = span // owners
    return pl.pallas_call(
        functools.partial(pool_kernel, experts, scale),
        grid_spec=pltpu.PrefetchScalarGridSpec(
            num_scalar_prefetch=1,
            grid=(owners,),
            in_specs=[
                pl.BlockSpec((places, gates.shape[1]), lambda i, slots: (slots[i], 0)),
                pl.BlockSpec((rows, places, width), lambda i, slots: (0, slots[i], 0)),
            ],
            out_specs=pl.BlockSpec((1, experts, places, width), lambda i, slots: (i, 0, 0, 0)),
        ),
        out_shape=jax.ShapeDtypeStruct((owners, experts, places, width), BF16),
        compiler_params=pltpu.CompilerParams(vmem_limit_bytes=40 << 20),
        cost_estimate=pl.CostEstimate(
            flops=rows * span * width * 1000, bytes_accessed=rows * span * width * 8, transcendentals=0
        ),
        name="pool",
    )(slots, gates, values)


CUBIC = 0.044715
SLOPE = math.sqrt(2.0 / math.pi)


def expert_kernel(steps, pooled_ref, weights_ref, result_ref, act_ref, slope_ref, total_ref):
    step = pl.program_id(0)
    blocks, places, width = pooled_ref.shape
    pooled = pooled_ref[...].reshape(blocks * places, width)
    pre = dot(pooled, weights_ref[0, 0])
    square = pre * pre
    bent = jnp.tanh(SLOPE * pre * (1.0 + CUBIC * square))
    half = 0.5 * (1.0 + bent)
    act = (pre * half).astype(BF16)
    act_ref[0] = act
    slope_ref[0] = half + 0.5 * pre * (1.0 - bent * bent) * (SLOPE * (1.0 + 3.0 * CUBIC * square))
    result = dot_nt(act, weights_ref[0, 1])

    @pl.when(step == 0)
    def _():
        total_ref[...] = result

    @pl.when(step > 0)
    def _():
        total_ref[...] += result

    @pl.when(step == steps - 1)
    def _():
        result_ref[...] = total_ref[...].astype(BF16).reshape(blocks, places, width)


def run_experts(pooled, weights):
    blocks, places, width = pooled.shape
    steps, _, _, tile = weights.shape
    count = blocks * places
    return pl.pallas_call(
        functools.partial(expert_kernel, steps),
        grid=(steps,),
        in_specs=[constant_spec(pooled.shape), pl.BlockSpec((1, 2, width, tile), lambda i: (i, 0, 0, 0))],
        out_specs=[
            constant_spec(pooled.shape),
            pl.BlockSpec((1, count, tile), lambda i: (i, 0, 0)),
            pl.BlockSpec((1, count, tile), lambda i: (i, 0, 0)),
        ],
        out_shape=[
            jax.ShapeDtypeStruct(pooled.shape, BF16),
            jax.ShapeDtypeStruct((steps, count, tile), BF16),
            jax.ShapeDtypeStruct((steps, count, tile), F32),
        ],
        scratch_shapes=[pltpu.VMEM((count, width), F32)],
        compiler_params=pltpu.CompilerParams(vmem_limit_bytes=40 << 20),
        cost_estimate=pl.CostEstimate(
            flops=count * width * tile * steps * 8, bytes_accessed=width * tile * steps * 8, transcendentals=0
        ),
        name="experts",
    )(pooled, weights)


def expert_back_kernel(steps, slots_ref, pooled_ref, grads_ref, result_ref, act_ref, slope_ref, weights_ref, back_ref, grad_ref, total_ref):
    step = pl.program_id(0)
    blocks, places, width = pooled_ref.shape
    count = blocks * places
    pooled = pooled_ref[...].reshape(count, width)
    grads = grads_ref[...].reshape(count, width)
    act = act_ref[0]
    grad_pre = (dot(grads, weights_ref[0, 1]) * slope_ref[0]).astype(BF16)
    grad_ref[0, 0] = dot_tn(pooled, grad_pre).astype(BF16)
    grad_ref[0, 1] = dot_tn(grads, act).astype(BF16)
    part = dot_nt(grad_pre, weights_ref[0, 0])

    @pl.when(step == 0)
    def _():
        total_ref[...] = part

    @pl.when(step > 0)
    def _():
        total_ref[...] += part

    @pl.when(step == steps - 1)
    def _():
        grad_pooled = total_ref[...].astype(BF16)
        back_ref[:, :places] = grad_pooled.reshape(blocks, places, width)
        result = result_ref[...].reshape(count, width)
        product = result.astype(F32) * grads.astype(F32) + grad_pooled.astype(F32) * pooled.astype(F32)
        high = product.astype(BF16)
        rest = (product - high.astype(F32)).astype(BF16)
        ones = jnp.ones((16, width), BF16)
        sums = dot_nt(ones, high) + dot_nt(ones, rest)
        top = sums.astype(BF16)
        low = (sums - top.astype(F32)).astype(BF16)
        for b in range(blocks):
            here = slice(b * places, b * places + places)
            fill = jnp.zeros((16, width - 2 * places), BF16)
            back_ref[b, places:] = jnp.concatenate([top[:, here], low[:, here], fill], axis=1)


def pull_experts(slots, pooled, grads, result, act, slope, weights):
    blocks, places, width = pooled.shape
    steps, _, _, tile = weights.shape
    count = blocks * places
    return pl.pallas_call(
        functools.partial(expert_back_kernel, steps),
        grid_spec=pltpu.PrefetchScalarGridSpec(
            num_scalar_prefetch=1,
            grid=(steps,),
            in_specs=[constant_spec(pooled.shape)] * 3
            + [pl.BlockSpec((1, count, tile), lambda i, slots: (i, 0, 0))] * 2
            + [pl.BlockSpec((1, 2, width, tile), lambda i, slots: (i, 0, 0, 0))],
            out_specs=[
                constant_spec((blocks, places + 16, width)),
                pl.BlockSpec((1, 2, width, tile), lambda i, slots: (slots[i], 0, 0, 0)),
            ],
            scratch_shapes=[pltpu.VMEM((count, width), F32)],
        ),
        out_shape=[
            jax.ShapeDtypeStruct((blocks, places + 16, width), BF16),
            jax.ShapeDtypeStruct(weights.shape, BF16),
        ],
        compiler_params=pltpu.CompilerParams(vmem_limit_bytes=40 << 20),
        cost_estimate=pl.CostEstimate(
            flops=count * width * tile * steps * 12, bytes_accessed=width * tile * steps * 8, transcendentals=0
        ),
        name="pull_experts",
    )(slots, pooled, grads, result, act, slope, weights)


def spread_kernel(group, count, slots_ref, gates_ref, grads_ref, hidden_ref, *rest):
    parts, (out_ref, change_ref, result_ref) = rest[:count], rest[-3:]
    for k in range(count):
        @pl.when(pl.program_id(0) == k)
        def _():
            result_ref[...] = parts[k][...]

    rows, places = grads_ref.shape[0], grads_ref.shape[1]
    experts = result_ref.shape[0]
    sub = 16
    columns = gates_ref.shape[1]

    def step(s, _):
        here = pl.ds(pl.multiple_of(s * sub, sub), sub)
        results = [result_ref[e, here, :].astype(F32) * group for e in range(experts)]
        gates = gates_ref[here, :].astype(BF16).astype(F32)
        lane = iota((sub, columns), 1)
        changes = jnp.zeros((sub, columns), F32)
        for r in range(rows):
            grads = grads_ref[r, here, :].astype(F32)
            for e in range(experts):
                both = jnp.sum(grads * results[e], axis=1, keepdims=True)
                changes = jnp.where(lane == r * experts + e, both, changes)
            total = sum(gates[:, r * experts + e: r * experts + e + 1] * results[e] for e in range(experts))
            out_ref[r, here, :] = (hidden_ref[r, here, :] + total.astype(BF16).astype(F32)).astype(BF16)
        change_ref[0, here, :] = changes
        return 0

    lax.fori_loop(0, places // sub, step, 0, unroll=8)


def slot_of(found):
    found = list(found)
    step = found[-1] - found[0]
    return lambda i, slots: slots[found[0] + i * step]


def spread_tokens(found, slots, gates, cotangent, hidden, group, held):
    rows, span, width = hidden.shape
    parts = list(found.values())
    experts, places, _ = parts[0].shape
    at = slot_of(found)
    block = pl.BlockSpec((rows, places, width), lambda i, slots: (0, at(i, slots), 0))
    columns = gates.shape[1]
    aliased = [] if held is None else [held]
    return pl.pallas_call(
        functools.partial(spread_kernel, group, len(parts)),
        grid_spec=pltpu.PrefetchScalarGridSpec(
            num_scalar_prefetch=1,
            grid=(len(parts),),
            in_specs=[pl.BlockSpec((places, columns), lambda i, slots: (at(i, slots), 0)), block, block]
            + [constant_spec(part.shape) for part in parts]
            + [pl.BlockSpec(memory_space=pltpu.HBM) for _ in aliased],
            out_specs=[block, pl.BlockSpec((1, places, columns), lambda i, slots: (i, 0, 0))],
            scratch_shapes=[pltpu.VMEM(parts[0].shape, BF16)],
        ),
        out_shape=[
            jax.ShapeDtypeStruct((rows, span, width), BF16),
            jax.ShapeDtypeStruct((len(parts), places, columns), F32),
        ],
        input_output_aliases={4 + len(parts): 0} if aliased else {},
        compiler_params=pltpu.CompilerParams(vmem_limit_bytes=58 << 20),
        cost_estimate=pl.CostEstimate(
            flops=len(parts) * rows * places * width * 5000, bytes_accessed=rows * places * width * 10, transcendentals=0
        ),
        name="spread",
    )(slots, gates, cotangent, hidden, *parts, *aliased)


def pull_kernel(first, count, slots_ref, gates_ref, change_ref, mixed_ref, hidden_ref, cotangent_ref, attended_ref, router_ref, gains_ref, weight_ref, *rest):
    parts, rest = rest[:count], rest[count:]
    out_ref, low_ref, router_grad_ref, project_ref, sums_ref, pooled_ref, logits_ref, grad_ref = rest[-8:]

    @pl.when(pl.program_id(0) == 0)
    def _():
        if first:
            router_grad_ref[...] = jnp.zeros_like(router_grad_ref)
            project_ref[...] = jnp.zeros_like(project_ref)
            sums_ref[...] = jnp.zeros_like(sums_ref)
        else:
            router_grad_ref[...] = rest[2][...]
            project_ref[...] = rest[3][...]
            sums_ref[...] = rest[4][...]

    for k in range(count):
        @pl.when(pl.program_id(0) == k)
        def _():
            pooled_ref[...] = parts[k][...]

    rows, places, width = mixed_ref.shape
    experts = pooled_ref.shape[0]
    sub = 16
    columns = gates_ref.shape[1]
    inner = jnp.zeros((places, columns), F32)
    for e in range(experts):
        pick = (iota((16, columns), 0) == 0) & (iota((16, columns), 1) % experts == e)
        pick = jnp.where(pick, 1.0, 0.0).astype(BF16)
        inner += dot_tn(pooled_ref[e, places:, :places], pick) + dot_tn(pooled_ref[e, places:, places: 2 * places], pick)

    def change(s, _):
        here = pl.ds(pl.multiple_of(s * sub, sub), sub)
        pooled = [pooled_ref[e, here, :].astype(F32) for e in range(experts)]
        lane = iota((sub, columns), 1)
        changes = jnp.zeros((sub, columns), F32)
        for r in range(rows):
            mixed = mixed_ref[r, here, :].astype(F32)
            for e in range(experts):
                both = jnp.sum(pooled[e] * mixed, axis=1, keepdims=True)
                changes = jnp.where(lane == r * experts + e, both, changes)
        logits_ref[here, :] = changes
        return 0

    lax.fori_loop(0, places // sub, change, 0, unroll=8)
    changes = (logits_ref[...] + change_ref[0]).astype(BF16).astype(F32)
    low = (gates_ref[...] * (changes - inner)).astype(BF16)
    for r in range(rows):
        grad_ref[r] = dot(low, router_ref[r])
        router_grad_ref[...] += dot_tn(low, mixed_ref[r])[r * experts: r * experts + experts]

    def spread(s, _):
        here = pl.ds(pl.multiple_of(s * sub, sub), sub)
        pooled = [pooled_ref[e, here, :].astype(F32) for e in range(experts)]
        gates = gates_ref[here, :].astype(BF16).astype(F32)
        for r in range(rows):
            grad_ref[r, here, :] = sum(
                (gates[:, r * experts + e: r * experts + e + 1] * pooled[e] for e in range(experts)),
                grad_ref[r, here, :],
            )
        return 0

    lax.fori_loop(0, places // sub, spread, 0, unroll=8)

    for r in range(rows):
        grads = grad_ref[r].astype(BF16).astype(F32)
        hat, inverse = normalise(hidden_ref[r])
        sums_ref[0:1] += jnp.sum(grads * hat, axis=0, keepdims=True)
        sums_ref[1:2] += jnp.sum(grads, axis=0, keepdims=True)
        total = cotangent_ref[r].astype(F32) + pull_norm(grads * gains_ref[2:3], hat, inverse)
        out_ref[r] = total
        total = total.astype(BF16)
        project_ref[...] += dot_tn(attended_ref[r], total)
        low_ref[r] = dot_nt(total, weight_ref[...]).astype(BF16)


def pull_slots(found, slots, gates, change, mixed, hidden, cotangent, attended, router, gains, packed, held, weight=20):
    rows, span, width = mixed.shape
    parts = list(found.values())
    experts, depth, _ = parts[0].shape
    places = span // slots.shape[0]
    at = slot_of(found)
    block = pl.BlockSpec((rows, places, width), lambda i, slots: (0, at(i, slots), 0))
    columns = gates.shape[1]
    sums = [(experts, width), (width, width), (8, width)]
    ins = [
        pl.BlockSpec((places, columns), lambda i, slots: (at(i, slots), 0)),
        pl.BlockSpec((1, places, columns), lambda i, slots: (i, 0, 0)),
        block,
        block,
        block,
        block,
        constant_spec(router.shape),
        constant_spec(gains.shape),
        constant_spec((width, width), 0, 3),
    ] + [constant_spec(part.shape) for part in parts]
    aliases = {}
    if held is not None:
        aliases = {len(ins) + 1: 0, len(ins) + 2: 1}
        ins += [pl.BlockSpec(memory_space=pltpu.HBM)] * 2 + [constant_spec(shape) for shape in sums]
    return pl.pallas_call(
        functools.partial(pull_kernel, held is None, len(parts)),
        grid_spec=pltpu.PrefetchScalarGridSpec(
            num_scalar_prefetch=1,
            grid=(len(parts),),
            in_specs=ins,
            out_specs=[block, block] + [constant_spec(shape) for shape in sums],
            scratch_shapes=[
                pltpu.VMEM(parts[0].shape, BF16),
                pltpu.VMEM((places, columns), F32),
                pltpu.VMEM((rows, places, width), F32),
            ],
        ),
        out_shape=[jax.ShapeDtypeStruct((rows, span, width), F32), jax.ShapeDtypeStruct((rows, span, width), BF16)]
        + [jax.ShapeDtypeStruct(shape, F32) for shape in sums],
        input_output_aliases=aliases,
        compiler_params=pltpu.CompilerParams(vmem_limit_bytes=58 << 20),
        cost_estimate=pl.CostEstimate(
            flops=len(parts) * rows * places * width * width * weight,
            bytes_accessed=rows * places * weight,
            transcendentals=0,
        ),
        name="pull_slots",
    )(slots, gates, change, mixed, hidden, cotangent, attended, router, gains, packed, *parts, *(held or ()))


def project_kernel(experts, grads_ref, tokens_ref, gains_ref, weight_ref, project_ref, late_ref, out_ref, product_ref, sums_ref):
    width, wide = product_ref.shape
    steps = pl.num_programs(0) * pl.num_programs(1)
    step = pl.program_id(0) * pl.num_programs(1) + pl.program_id(1)

    @pl.when(step == 0)
    def _():
        product_ref[...] = jnp.zeros_like(product_ref)
        sums_ref[...] = jnp.zeros_like(sums_ref)

    hat = normalise(tokens_ref[0].astype(F32))[0].astype(BF16)
    ones = jnp.ones((hat.shape[0], 8), BF16)
    product_ref[...] += dot_tn(hat, grads_ref[0])
    sums_ref[...] += dot_tn(ones, grads_ref[0])

    @pl.when(step == steps - 1)
    def _():
        sums = sums_ref[0:1, :]
        for at in range(0, width, 64):
            here = slice(at, at + 64)
            product = product_ref[here, :]
            weights = weight_ref[here, :].astype(F32)
            out_ref[here, :wide] = (gains_ref[here, 0:1] * product + gains_ref[here, 1:2] * sums).astype(BF16)
            out_ref[here, wide: wide + width] = project_ref[here, :].astype(BF16)
            late = late_ref[here, :]
            lane = iota(late.shape, 1)
            late = jnp.where(lane == experts, jnp.sum(weights * product, axis=1, keepdims=True), late)
            late = jnp.where(lane == experts + 1, jnp.sum(weights * sums, axis=1, keepdims=True), late)
            out_ref[here, wide + width:] = late.astype(BF16)


def project_grads(grads, tokens, gains, packed, project, late, experts, tile=1024):
    rows, length, width = tokens.shape
    wide = 3 * width
    return pl.pallas_call(
        functools.partial(project_kernel, experts),
        grid=(rows, length // tile),
        in_specs=[
            pl.BlockSpec((1, tile, wide), lambda r, t: (r, t, 0)),
            pl.BlockSpec((1, tile, width), lambda r, t: (r, t, 0)),
            constant_spec(gains.shape),
            constant_spec((width, wide)),
            constant_spec(project.shape),
            constant_spec(late.shape),
        ],
        out_specs=constant_spec(packed.shape),
        out_shape=jax.ShapeDtypeStruct(packed.shape, BF16),
        scratch_shapes=[pltpu.VMEM((width, wide), F32), pltpu.VMEM((8, wide), F32)],
        compiler_params=pltpu.CompilerParams(vmem_limit_bytes=48 << 20),
        cost_estimate=pl.CostEstimate(flops=rows, bytes_accessed=rows, transcendentals=0),
        name="project_grads",
    )(grads, tokens, gains, packed, project, late)


def tokens_kernel(grads_ref, tokens_ref, hidden_ref, gains_ref, weight_ref, *rest):
    out_ref = rest[-1]
    for at in pieces(tokens_ref.shape[1]):
        hat, inverse = normalise(tokens_ref[0, at].astype(F32))
        grads = dot_nt(grads_ref[0, at], weight_ref[...])
        out_ref[0, at] = hidden_ref[0, at] + pull_norm(grads * gains_ref[0:1], hat, inverse)


def pull_tokens(grads, tokens, hidden, gains, packed, row_from, row_to, held=None, tile=1024):
    rows, length, width = tokens.shape
    block = pl.BlockSpec((1, tile, width), lambda r, t: (r + row_from, t, 0))
    aliased = [] if held is None else [held]
    return pl.pallas_call(
        tokens_kernel,
        grid=(row_to - row_from, length // tile),
        in_specs=[
            pl.BlockSpec((1, tile, 3 * width), lambda r, t: (r + row_from, t, 0)),
            block,
            block,
            constant_spec(gains.shape),
            constant_spec((width, 3 * width)),
        ]
        + [pl.BlockSpec(memory_space=pltpu.HBM) for _ in aliased],
        out_specs=block,
        out_shape=jax.ShapeDtypeStruct((rows, length, width), F32),
        input_output_aliases={5: 0} if aliased else {},
        compiler_params=pltpu.CompilerParams(vmem_limit_bytes=58 << 20),
        cost_estimate=pl.CostEstimate(
            flops=(row_to - row_from) * length * width * width * 20,
            bytes_accessed=(row_to - row_from) * length * width * 16,
            transcendentals=0,
        ),
        name="pull_tokens",
    )(grads, tokens, hidden, gains, packed, *aliased)


def ring_order(size):
    inner = 2 if size % 2 == 0 and size > 2 else 1
    outer = size // inner
    up = [z * inner for z in range(outer)]
    if inner == 1:
        return up
    return up + [z * inner + 1 for z in reversed(range(outer))]


def shift(value, order, step):
    count = len(order)
    return lax.ppermute(value, "dp", [(order[i], order[(i + step) % count]) for i in range(count)])


def flip(value, bit, axis="fsdp"):
    count = lax.axis_size(axis)
    return lax.ppermute(value, axis, [(i, i ^ bit) for i in range(count)])


def turn(value, step, axis="dp"):
    count = lax.axis_size(axis)
    return lax.ppermute(value, axis, [(i, (i + step) % count) for i in range(count)])


def take(values, index):
    starts = (index,) + (jnp.uint32(0),) * (values.ndim - 1)
    return lax.dynamic_slice(values, starts, (1,) + values.shape[1:])[0]


def put(values, value, index):
    return lax.dynamic_update_slice(values, value[None], (index,) + (jnp.uint32(0),) * value.ndim)


def add(a, b):
    return (a.astype(F32) + b.astype(F32)).astype(BF16)


def together(*values):
    return lax.optimization_barrier(values)


class Ring:
    def __init__(self, value, order):
        self.order, self.done = order, 0
        self.ahead = self.behind = value

    def left(self):
        return self.done < len(self.order) // 2

    def after(self, *values):
        self.ahead, self.behind, *_ = together(self.ahead, self.behind, *values)

    def step(self, *beside):
        count = len(self.order)
        self.done += 1
        slot = count - self.done
        ahead, behind = self.ahead, self.behind
        middle = 2 * self.done == count and ahead.shape[0] % 2 == 0
        if middle:
            half = ahead.shape[0] // 2
            ahead, behind = ahead[:half], behind[half:]
        ahead = shift(ahead, self.order, 1)
        if 2 * self.done < count or middle:
            behind = shift(behind, self.order, -1)
        ahead, behind, *beside = together(ahead, behind, *beside)
        self.ahead, self.behind = ahead, behind
        if middle:
            return {slot: jnp.concatenate([ahead, behind], axis=0)}, beside
        return {slot: ahead, self.done: behind} if 2 * self.done < count else {slot: ahead}, beside


def gather_all(value, steps, *beside):
    pair = pair_of(lax.axis_size("dp"))
    lines = lax.axis_size("dp") // pair
    size = lax.axis_size("fsdp")
    here = lax.axis_index("fsdp")

    def both(value, bit, axis, index):
        other = flip(value, bit, axis)
        upper = (index & bit) != 0
        return jnp.stack([jnp.where(upper, other, value), jnp.where(upper, value, other)])

    whole = put(jnp.zeros((lines,) + value.shape, value.dtype), value, steps[0])
    for k in range(1, lines):
        whole = put(whole, turn(value, -k * pair), steps[k])
    if beside:
        whole, *beside = together(whole, *beside)
    whole = both(whole, 1, "dp", lax.axis_index("dp")) if pair == 2 else whole[None]
    whole = jnp.moveaxis(whole, 0, 1)
    whole = whole.reshape((lines * pair, 1) + value.shape)
    bit = size // 2
    while bit:
        whole = both(whole, bit, "fsdp", here)
        whole = jnp.moveaxis(whole, 0, 2)
        whole = whole.reshape((lines * pair, -1) + value.shape)
        bit //= 2
    return whole, beside


def scatter_all(values, steps, work):
    owners, size = lax.axis_size("dp"), lax.axis_size("fsdp")
    bits = size.bit_length() - 1
    here = lax.axis_index("fsdp")
    width = values.shape[1]
    pair = pair_of(owners)
    work = list(work)

    def half(held, axis, upper, bit, name):
        low, high = (lax.index_in_dim(held, i, axis, keepdims=False) for i in (0, 1))
        came = flip(jnp.where(upper, low, high), bit, name)
        if work:
            came, = work.pop(0)(came)
        return add(jnp.where(upper, high, low), came)

    held = values.reshape((owners // pair, pair) + (2,) * bits + (-1, width))
    for level in range(bits):
        held = half(held, bits + 1 - level, ((here >> level) & 1) != 0, 1 << level, "fsdp")
    held = half(held, 1, (lax.axis_index("dp") & 1) != 0, 1, "dp") if pair == 2 else held[:, 0]
    came = [turn(take(held, steps[k]), k * pair) for k in range(1, owners // pair)]
    while work:
        came = work.pop(0)(*came)
    return sum((value.astype(F32) for value in came), take(held, steps[0]).astype(F32))


def pair_of(owners):
    return 2 if owners % 2 == 0 else 1


def exchange(values):
    return jnp.stack([values[0]] + [flip(values[k], k) for k in range(1, values.shape[0])])


def per_device(
    tokens,
    segment_ids,
    pad_tokens,
    cotangent,
    project_in,
    project_out,
    router_weight,
    expert_in,
    expert_out,
    first_gain,
    first_bias,
    second_gain,
    second_bias,
):
    blocks_here, rows, length, width = tokens.shape
    tokens = tokens.reshape(rows, length, width)
    cotangent = cotangent.reshape(rows, length, width)
    segments = segment_ids.reshape(rows, length)
    group = pad_tokens.shape[1]
    owners = lax.axis_size("dp")
    experts = router_weight.shape[1]
    order = ring_order(owners)
    data_index = lax.axis_index("dp")
    expert_index = lax.axis_index("fsdp")
    places = length // owners

    pair = pair_of(owners)
    lines = owners // pair
    ring = np.array([[order[(order.index(d) + k) % owners] for k in range(owners)] for d in range(owners)], np.int32)
    place = np.array(
        [[(o % pair ^ d % pair) * lines + (o // pair - d // pair) % lines for o in ring[d]] for d in range(owners)],
        np.int32,
    )
    line = np.array([[(d // pair + k) % lines for k in range(lines)] for d in range(owners)], np.int32)
    tables = np.concatenate([ring, place, line], axis=1)
    tables = lax.dynamic_slice(
        jnp.asarray(tables), (data_index.astype(jnp.uint32), jnp.uint32(0)), (1, tables.shape[1])
    )[0]
    slots, shares = tables[:owners], tables[owners: 2 * owners]
    spots = [tables[k].astype(jnp.uint32) for k in range(owners)]
    steps = [tables[2 * owners + k].astype(jnp.uint32) for k in range(lines)]

    vectors = jnp.stack([first_gain, first_bias, second_gain, second_bias], axis=1)
    small = jnp.concatenate([router_weight, vectors], axis=1)
    small = jnp.pad(small, ((0, 0), (0, 128 - small.shape[1])))
    packed = jnp.concatenate([project_in, project_out, small], axis=1)
    packed, (expert_in, expert_out) = gather_all(packed, steps, expert_in, expert_out)
    weights = jnp.stack([expert_in[0], expert_out[0].T])
    packed = packed.reshape(width, packed.shape[-1])
    packed, weights = together(packed, weights)
    kept = {0: weights}
    weights = Ring(weights, order)
    small = packed[:, 4 * width:].T
    mine = (jnp.arange(experts)[:, None] ^ jnp.arange(experts)[None, :]) == expert_index
    router = jnp.sum(jnp.where(mine[:, :, None], small[None, :experts], 0), axis=1).astype(BF16)
    spread_router = jnp.stack(
        [jnp.pad(router, ((r * experts, (rows - 1 - r) * experts), (0, 0))) for r in range(rows)]
    )
    gains = jnp.pad(small[experts: experts + 4].astype(F32), ((0, 4), (0, 0)))

    own_pads = lax.dynamic_slice_in_dim(pad_tokens[0], data_index * rows, rows, 0)
    vlens = (length - own_pads).astype(jnp.int32)
    starts = jnp.zeros_like(segments)
    for doc in range(1, 4):
        before = jnp.sum((segments < doc).astype(jnp.int32), axis=1, keepdims=True)
        starts = jnp.where(segments == doc, before, starts)
    starts = starts.reshape(rows, length // QB, QB)
    lows = starts[:, :, 0] // QB

    def meanwhile(value):
        if not weights.left():
            return value
        found, (value,) = weights.step(value)
        kept.update(found)
        return value

    joined = meanwhile(join_tokens(tokens, gains, packed))
    attended, logs = attn_fwd(joined, starts, lows, vlens, 1)
    attended = meanwhile(attended)
    hidden, mixed, logits = mix_tokens(
        attended, tokens, gains, packed, jnp.pad(router, ((0, 16 - experts), (0, 0))), 0
    )
    logits = meanwhile(logits)[:, :experts]
    valid = (jnp.arange(length)[None, :] < vlens[:, None])[:, None, :]
    highest = jnp.max(jnp.where(valid, logits, NEGATIVE), axis=0)
    total = jnp.sum(jnp.where(valid, jnp.exp(logits - highest), 0.0), axis=0)
    stats = jnp.stack([highest, total])[None]
    if pair == 2:
        stats = jnp.concatenate([stats, flip(stats, 1, "dp")])
    stats = jnp.concatenate([stats] + [turn(stats, k * pair) for k in range(1, lines)])
    tops = jnp.max(stats[:, 0], axis=0)
    total = jnp.sum(stats[:, 1] * jnp.exp(stats[:, 0] - tops), axis=0)
    gates = jnp.where(valid, jnp.exp(jnp.where(valid, logits - tops, NEGATIVE)) / total, 0.0)
    gates = gates.reshape(rows * experts, length).T
    pooled = meanwhile(pool_tokens(slots, gates, mixed, experts, 1.0))
    while weights.left():
        kept.update(weights.step()[0])
    weights = jnp.stack([kept[k] for k in range(owners)])
    grads = pool_tokens(slots, gates, cotangent, experts, float(group))

    half = experts // 2
    first = [(pooled[:, :half], 1), (pooled[:, half:], -1)]
    second = [(grads[:, :half], 1), (grads[:, half:], -1)]
    held = [part[-way % owners] for part, way in first]
    later = [part[-way % owners] for part, way in second]
    for step in range(owners - 1):
        came = [shift(value, order, way) for value, (_, way) in zip(held, first)]
        if step == 0:
            *came, one, two = together(*came, *later)
            later = [one, two]
        held = [add(value, part[-way * (2 + step) % owners]) for value, (part, way) in zip(came, first)]
        came = [shift(value, order, way) for value, (_, way) in zip(later, second)]
        later = [add(value, part[-way * (2 + step) % owners]) for value, (part, way) in zip(came, second)]
    pooled = exchange(jnp.concatenate(held, axis=0))
    result, act, slope = run_experts(pooled, weights)
    grads = exchange(jnp.concatenate(later, axis=0))
    grad_pooled, grad_weights = pull_experts(shares, pooled, grads, result, act, slope, weights)

    result = exchange(result)
    back = exchange(grad_pooled)

    def pull(found, change, out, *weight):
        return pull_slots(
            found, slots, gates, change, mixed, hidden, cotangent, attended, spread_router, gains, packed, out, *weight
        )

    def spread(found, out):
        return spread_tokens(found, slots, gates, cotangent, hidden, group, out)

    turns = owners // 2
    first, second = Ring(result, order), Ring(back, order)
    found, (grad_weights,) = first.step(grad_weights)
    groups, arrived = [{0: result}, found], [{0: back}]
    out, pulled, changes = None, None, []
    for step in range(turns + 1):
        work = []
        for k in [step] if step < turns - 1 else [turns - 1, turns] if step == turns - 1 else []:
            out, change = spread(groups[k], out)
            changes.append(change)
            work = [out]
        if 0 < step < turns - 1 or step == turns:
            k = step - 1 if step < turns else turns - 2
            pulled = pull(arrived[k], changes[k], pulled)
            work += pulled
        if step > 0:
            if step == 1:
                second.after(*groups[2].values())
        if first.left():
            found, work = first.step(*work)
            groups.append(found)
        if second.left() and step > 0:
            found, work = second.step(*work)
            arrived.append(found)
        if step < turns:
            out, *work = work
        pulled = work or pulled
    pulled = pull(arrived[turns - 1], changes[turns - 1], pulled)
    layer_out = out
    grad_weights, *_ = together(grad_weights, *arrived[turns].values())
    if pair == 2:
        came = flip(grad_weights[lines:], 1, "dp")
    pulled = pull(arrived[turns], changes[turns], pulled, 0)
    grad_hidden, grad_attended, router_grad, grad_proj_out, sums_two = pulled
    split = rows - max(1, rows // 2)
    grads = attn_bwd(joined, grad_attended, attended, logs, starts, lows, vlens, 0, split)
    grad_weights = grad_weights[:lines]
    if pair == 2:
        came, grads = together(came, grads)
        grad_weights = add(grad_weights, came)
    grad_parts = [turn(grad_weights[k], k * pair) for k in range(1, lines)]
    grads = attn_bwd(joined, grad_attended, attended, logs, starts, lows, vlens, split, rows, grads)
    router_grad = jnp.sum(jnp.where(mine[:, :, None], router_grad[None], 0.0), axis=1)
    late = jnp.concatenate([router_grad, jnp.zeros((2, width), F32), sums_two[:2]], axis=0).T
    late = jnp.pad(late, ((0, 0), (0, 128 - late.shape[1])))
    reduced = project_grads(grads, tokens, gains.T, packed, grad_proj_out, late, experts)
    reduced, *grad_parts = together(reduced, *grad_parts)
    made = []

    def tokens_beside(*came):
        *came, grad = together(*came, pull_tokens(grads, tokens, grad_hidden, gains, packed, 0, rows))
        made.append(grad)
        return came

    def weights_beside(*came):
        value, *parts = together(*came, *grad_parts)
        made.append(sum((part.astype(F32) for part in parts), grad_weights[0].astype(F32)))
        return [value]

    reduced = scatter_all(reduced, steps, [lambda *came: came, tokens_beside, weights_beside])
    tokens_grad, grad_weights = made
    late = reduced[:, 4 * width:]
    return (
        layer_out[None],
        tokens_grad[None],
        reduced[:, : 3 * width],
        reduced[:, 3 * width: 4 * width],
        late[:, :experts],
        grad_weights[0][None],
        grad_weights[1].T[None],
        late[:, experts],
        late[:, experts + 1],
        late[:, experts + 2],
        late[:, experts + 3],
    )


def solution(mesh):
    in_specs = (
        P("fsdp", "dp", None, None),
        P("fsdp", "dp", None),
        P("fsdp", None),
        P("fsdp", "dp", None, None),
        P(("dp", "fsdp"), None),
        P(("dp", "fsdp"), None),
        P(("dp", "fsdp"), None),
        P("fsdp", None, "dp"),
        P("fsdp", "dp", None),
        P(("dp", "fsdp")),
        P(("dp", "fsdp")),
        P(("dp", "fsdp")),
        P(("dp", "fsdp")),
    )
    out_specs = (
        P("fsdp", "dp", None, None),
        P("fsdp", "dp", None, None),
        P(("dp", "fsdp"), None),
        P(("dp", "fsdp"), None),
        P(("dp", "fsdp"), None),
        P("fsdp", None, "dp"),
        P("fsdp", "dp", None),
        P(("dp", "fsdp")),
        P(("dp", "fsdp")),
        P(("dp", "fsdp")),
        P(("dp", "fsdp")),
    )
    return jax.shard_map(
        per_device, mesh=mesh, in_specs=in_specs, out_specs=out_specs, check_vma=False
    )
```

```python
import functools, math
import jax
import jax.numpy as jnp
import numpy as np
from jax import lax
from jax.experimental import pallas as pl
from jax.experimental.pallas import tpu as pltpu
from jax.sharding import PartitionSpec as P

NEGATIVE = -1e30
QB = 128
F32 = jnp.float32
BF16 = jnp.bfloat16
NT = (((1,), (1,)), ((), ()))
TN = (((0,), (0,)), ((), ()))


def dot(a, b):
    return jnp.dot(a, b, preferred_element_type=F32)


def dot_nt(a, b):
    return lax.dot_general(a, b, NT, preferred_element_type=F32)


def dot_tn(a, b):
    return lax.dot_general(a, b, TN, preferred_element_type=F32)


def iota(shape, axis):
    return lax.broadcasted_iota(jnp.int32, shape, axis)


def split_heads(x):
    low = iota(x.shape, 1) < 64
    zero = jnp.zeros_like(x)
    return jnp.concatenate([jnp.where(low, x, zero), jnp.where(low, zero, x)], axis=0)


def join_heads(x):
    half = x.shape[0] // 2
    low = iota((half, x.shape[1]), 1) < 64
    return jnp.where(low, x[:half], x[half:])


def attn_fwd_kernel(width, batch, count, lo_ref, vlen_ref, start_ref, joined_ref, out_ref, log_ref, bias_ref):
    row = pl.program_id(0) * batch

    def block(qb, _):
        lo = functools.reduce(jnp.minimum, [lo_ref[row + r, qb] for r in range(batch)])
        base = pl.multiple_of(qb * QB, QB)
        first = pl.multiple_of(lo * QB, QB)
        own = pl.ds(base, QB)

        def variant(blocks):
            span = blocks * QB
            keys = pl.ds(first, span)
            i = base + iota((QB, QB), 0)
            bias = []
            for r in range(batch):
                begins = jnp.broadcast_to(start_ref[r, pl.ds(qb, 1), :], (QB, QB)).T
                for b in range(blocks):
                    j = first + b * QB + iota((QB, QB), 1)
                    ok = ((j >= begins) & (j <= i) & (j < vlen_ref[row + r])) | (j == i)
                    bias_ref[r, :, b * QB:(b + 1) * QB] = jnp.where(ok, 0.0, NEGATIVE)
                bias.append(jnp.concatenate([bias_ref[r, :, :span]] * 2, axis=0))
            work = [(r, lane) for r in range(batch) for lane in range(0, width, 128)]
            query = [split_heads(joined_ref[r, own, pl.ds(at, 128)] * jnp.asarray(0.125, BF16)) for r, at in work]
            scores = [dot_nt(q, joined_ref[r, keys, pl.ds(width + at, 128)]) for q, (r, at) in zip(query, work)]
            scores = [s + bias[r] for s, (r, _) in zip(scores, work)]
            tops = [jnp.max(s, axis=1, keepdims=True) for s in scores]
            raised = [jnp.exp(s - top) for s, top in zip(scores, tops)]
            totals = [jnp.sum(p, axis=1, keepdims=True) for p in raised]
            out = [
                dot(p.astype(BF16), joined_ref[r, keys, pl.ds(2 * width + at, 128)]) for p, (r, at) in zip(raised, work)
            ]
            for o, total, (r, at) in zip(out, totals, work):
                out_ref[r, own, pl.ds(at, 128)] = join_heads(o * (1.0 / total)).astype(BF16)
            lane = iota((QB, QB), 1)
            for r in range(batch):
                tile = jnp.zeros((QB, QB), F32)
                for top, total, (other, at) in zip(tops, totals, work):
                    if other == r:
                        log = top + jnp.log(total)
                        tile = jnp.where(lane == at // 64, log[:QB], tile)
                        tile = jnp.where(lane == at // 64 + 1, log[QB:], tile)
                log_ref[r, pl.ds(qb, 1)] = tile.T[None, : log_ref.shape[2]]

        for blocks in range(1, 6):
            pl.when(qb - lo + 1 == blocks)(functools.partial(variant, blocks))
        return 0

    lax.fori_loop(0, count, block, 0)


def attn_fwd(joined, starts, lows, vlens, batch=2):
    rows, length, triple = joined.shape
    width = triple // 3
    count = length // QB
    return pl.pallas_call(
        functools.partial(attn_fwd_kernel, width, batch, count),
        grid_spec=pltpu.PrefetchScalarGridSpec(
            num_scalar_prefetch=2,
            grid=(rows // batch,),
            in_specs=[
                pl.BlockSpec((batch, count, QB), lambda r, *_: (r, 0, 0)),
                pl.BlockSpec((batch, length, triple), lambda r, *_: (r, 0, 0)),
            ],
            out_specs=[
                pl.BlockSpec((batch, length, width), lambda r, *_: (r, 0, 0)),
                pl.BlockSpec((batch, count, width // 64, QB), lambda r, *_: (r, 0, 0, 0)),
            ],
            scratch_shapes=[pltpu.VMEM((batch, QB, 5 * QB), F32)],
        ),
        out_shape=[
            jax.ShapeDtypeStruct((rows, length, width), BF16),
            jax.ShapeDtypeStruct((rows, count, width // 64, QB), F32),
        ],
        compiler_params=pltpu.CompilerParams(vmem_limit_bytes=48 << 20),
        cost_estimate=pl.CostEstimate(
            flops=rows * length * 400 * 8 * 256 * 4, bytes_accessed=rows * length * triple * 2, transcendentals=0
        ),
        name="attend",
    )(lows, vlens, starts, joined)


def attn_bwd_kernel(width, row_from, batch, count, lo_ref, vlen_ref, start_ref, joined_ref, grad_ref, attended_ref, log_ref, *rest):
    out_ref, dk_ref, dv_ref, bias_ref = rest[-4:]
    row = pl.program_id(0) * batch + row_from
    dk_ref[...] = jnp.zeros_like(dk_ref)
    dv_ref[...] = jnp.zeros_like(dv_ref)

    def block(qb, _):
        lo = functools.reduce(jnp.minimum, [lo_ref[row + r, qb] for r in range(batch)])
        base = pl.multiple_of(qb * QB, QB)
        first = pl.multiple_of(lo * QB, QB)
        own = pl.ds(base, QB)

        def variant(blocks):
            span = blocks * QB
            keys = pl.ds(first, span)
            i = base + iota((QB, QB), 1)
            pick = jnp.where(iota((16, width), 1) // 64 == iota((16, width), 0), 1.0, 0.0).astype(BF16)
            bias, sums = [], []
            for r in range(batch):
                begins = start_ref[r, pl.ds(qb, 1), :]
                for b in range(blocks):
                    j = first + b * QB + iota((QB, QB), 0)
                    ok = ((j >= begins) & (j <= i) & (j < vlen_ref[row + r])) | (j == i)
                    bias_ref[r, b * QB:(b + 1) * QB, :] = jnp.where(ok, 0.0, NEGATIVE)
                bias.append(jnp.concatenate([bias_ref[r, :span, :]] * 2, axis=1))
                product = grad_ref[r, own, :].astype(F32) * attended_ref[r, own, :].astype(F32)
                high = product.astype(BF16)
                sums.append(dot_nt(pick, high) + dot_nt(pick, (product - high.astype(F32)).astype(BF16)))
            work = [(r, lane) for r in range(batch) for lane in range(0, width, 128)]
            query = [split_heads(joined_ref[r, own, pl.ds(at, 128)] * jnp.asarray(0.125, BF16)) for r, at in work]
            grads = [split_heads(grad_ref[r, own, pl.ds(at, 128)]) for r, at in work]
            prob, moved = [], []
            for q, g, (r, at) in zip(query, grads, work):
                head = at // 64
                log = log_ref[r, qb]
                log = jnp.concatenate([log[head: head + 1], log[head + 1: head + 2]], axis=1)
                total = jnp.concatenate([sums[r][head: head + 1], sums[r][head + 1: head + 2]], axis=1)
                scores = dot_nt(joined_ref[r, keys, pl.ds(width + at, 128)], q)
                change = dot_nt(joined_ref[r, keys, pl.ds(2 * width + at, 128)], g)
                p = jnp.exp(scores + bias[r] - log)
                prob.append(p.astype(BF16))
                moved.append((p * (change - total)).astype(BF16))
            for p, g, (r, at) in zip(prob, grads, work):
                dv_ref[r, keys, pl.ds(at, 128)] += dot(p, g)
            for m, q, (r, at) in zip(moved, query, work):
                dk_ref[r, keys, pl.ds(at, 128)] += dot(m, q)
            back = [dot_tn(m, joined_ref[r, keys, pl.ds(width + at, 128)]) for m, (r, at) in zip(moved, work)]
            for b, (r, at) in zip(back, work):
                out_ref[r, own, pl.ds(at, 128)] = (join_heads(b) * 0.125).astype(BF16)

        for blocks in range(1, 6):
            pl.when(qb - lo + 1 == blocks)(functools.partial(variant, blocks))
        return 0

    lax.fori_loop(0, count, block, 0)
    out_ref[:, :, width: 2 * width] = dk_ref[...].astype(BF16)
    out_ref[:, :, 2 * width:] = dv_ref[...].astype(BF16)


def attn_bwd(joined, grads, attended, logs, starts, lows, vlens, row_from, row_to, held=None, batch=1):
    rows, length, triple = joined.shape
    width = triple // 3
    count = length // QB
    aliased = [] if held is None else [held]
    skip = row_from // batch
    wide = pl.BlockSpec((batch, length, triple), lambda r, *_: (r + skip, 0, 0))
    slim = pl.BlockSpec((batch, length, width), lambda r, *_: (r + skip, 0, 0))
    return pl.pallas_call(
        functools.partial(attn_bwd_kernel, width, row_from, batch, count),
        grid_spec=pltpu.PrefetchScalarGridSpec(
            num_scalar_prefetch=2,
            grid=((row_to - row_from) // batch,),
            in_specs=[
                pl.BlockSpec((batch, count, QB), lambda r, *_: (r + skip, 0, 0)),
                wide,
                slim,
                slim,
                pl.BlockSpec((batch,) + logs.shape[1:], lambda r, *_: (r + skip, 0, 0, 0)),
            ]
            + [pl.BlockSpec(memory_space=pltpu.HBM) for _ in aliased],
            out_specs=wide,
            scratch_shapes=[
                pltpu.VMEM((batch, length, width), F32),
                pltpu.VMEM((batch, length, width), F32),
                pltpu.VMEM((batch, 5 * QB, QB), F32),
            ],
        ),
        out_shape=jax.ShapeDtypeStruct(joined.shape, BF16),
        input_output_aliases={7: 0} if aliased else {},
        compiler_params=pltpu.CompilerParams(vmem_limit_bytes=58 << 20),
        cost_estimate=pl.CostEstimate(
            flops=row_to * length * 400 * 8 * 256 * 20 if aliased else rows,
            bytes_accessed=rows * length,
            transcendentals=0,
        ),
        name="attend_back",
    )(lows, vlens, starts, joined, grads, attended, logs, *aliased)


def normalise(values):
    centred = values - jnp.mean(values, axis=-1, keepdims=True)
    inverse = lax.rsqrt(jnp.mean(centred * centred, axis=-1, keepdims=True) + 1e-05)
    return centred * inverse, inverse


def pull_norm(scaled, hat, inverse):
    return inverse * (
        scaled
        - jnp.mean(scaled, axis=-1, keepdims=True)
        - hat * jnp.mean(scaled * hat, axis=-1, keepdims=True)
    )


PIECE = 256


def pieces(count):
    return [slice(at, min(at + PIECE, count)) for at in range(0, count, PIECE)]


def constant_spec(shape, *where):
    where = where or (0,) * len(shape)
    return pl.BlockSpec(shape, lambda *_: where)


def join_kernel(tokens_ref, gains_ref, weight_ref, joined_ref):
    for at in pieces(tokens_ref.shape[1]):
        hat, _ = normalise(tokens_ref[0, at].astype(F32))
        normed = (hat * gains_ref[0:1] + gains_ref[1:2]).astype(BF16)
        joined_ref[0, at] = dot(normed, weight_ref[...]).astype(BF16)


def join_tokens(tokens, gains, packed, tile=1024):
    rows, length, width = tokens.shape
    return pl.pallas_call(
        join_kernel,
        grid=(rows, length // tile),
        in_specs=[
            pl.BlockSpec((1, tile, width), lambda r, t: (r, t, 0)),
            constant_spec(gains.shape),
            constant_spec((width, 3 * width)),
        ],
        out_specs=pl.BlockSpec((1, tile, 3 * width), lambda r, t: (r, t, 0)),
        out_shape=jax.ShapeDtypeStruct((rows, length, 3 * width), BF16),
        compiler_params=pltpu.CompilerParams(vmem_limit_bytes=40 << 20),
        cost_estimate=pl.CostEstimate(
            flops=rows * length * width * width * 6, bytes_accessed=rows * length * width * 8, transcendentals=0
        ),
        name="join",
    )(tokens, gains, packed)


def mixed_kernel(attended_ref, tokens_ref, gains_ref, weight_ref, router_ref, hidden_ref, mixed_ref, logits_ref):
    hidden = tokens_ref[0].astype(F32) + dot(attended_ref[0], weight_ref[...])
    hidden_ref[0] = hidden
    hat, _ = normalise(hidden)
    mixed = (hat * gains_ref[2:3] + gains_ref[3:4]).astype(BF16)
    mixed_ref[0] = mixed
    logits_ref[0] = dot_nt(router_ref[...], mixed)


def mix_tokens(attended, tokens, gains, packed, router, offset, tile=1024):
    rows, span, width = attended.shape
    block = pl.BlockSpec((1, tile, width), lambda r, t: (r, t, 0))
    return pl.pallas_call(
        mixed_kernel,
        grid=(rows, span // tile),
        in_specs=[
            block,
            pl.BlockSpec((1, tile, width), lambda r, t: (r, t + offset // tile, 0)),
            constant_spec(gains.shape),
            constant_spec((width, width), 0, 3),
            constant_spec(router.shape),
        ],
        out_specs=[block, block, pl.BlockSpec((1, router.shape[0], tile), lambda r, t: (r, 0, t))],
        out_shape=[
            jax.ShapeDtypeStruct((rows, span, width), F32),
            jax.ShapeDtypeStruct((rows, span, width), BF16),
            jax.ShapeDtypeStruct((rows, router.shape[0], span), F32),
        ],
        compiler_params=pltpu.CompilerParams(vmem_limit_bytes=40 << 20),
        cost_estimate=pl.CostEstimate(
            flops=rows * span * width * width * 2, bytes_accessed=rows * span * width * 10, transcendentals=0
        ),
        name="mix",
    )(attended, tokens, gains, packed, router)


def pool_kernel(experts, scale, slots_ref, gates_ref, values_ref, out_ref):
    rows, places = values_ref.shape[0], values_ref.shape[1]
    sub = 16

    def step(s, _):
        here = pl.ds(pl.multiple_of(s * sub, sub), sub)
        gates = gates_ref[here, :].astype(BF16).astype(F32)
        values = [values_ref[r, here, :].astype(F32) for r in range(rows)]
        for e in range(experts):
            total = sum(gates[:, r * experts + e: r * experts + e + 1] * values[r] for r in range(rows))
            out_ref[0, e, here, :] = (scale * total).astype(BF16)
        return 0

    lax.fori_loop(0, places // sub, step, 0, unroll=8)


def pool_tokens(slots, gates, values, experts, scale):
    rows, span, width = values.shape
    owners = slots.shape[0]
    places = span // owners
    return pl.pallas_call(
        functools.partial(pool_kernel, experts, scale),
        grid_spec=pltpu.PrefetchScalarGridSpec(
            num_scalar_prefetch=1,
            grid=(owners,),
            in_specs=[
                pl.BlockSpec((places, gates.shape[1]), lambda i, slots: (slots[i], 0)),
                pl.BlockSpec((rows, places, width), lambda i, slots: (0, slots[i], 0)),
            ],
            out_specs=pl.BlockSpec((1, experts, places, width), lambda i, slots: (i, 0, 0, 0)),
        ),
        out_shape=jax.ShapeDtypeStruct((owners, experts, places, width), BF16),
        compiler_params=pltpu.CompilerParams(vmem_limit_bytes=40 << 20),
        cost_estimate=pl.CostEstimate(
            flops=rows * span * width * 1000, bytes_accessed=rows * span * width * 8, transcendentals=0
        ),
        name="pool",
    )(slots, gates, values)


CUBIC = 0.044715
SLOPE = math.sqrt(2.0 / math.pi)


def expert_kernel(steps, pooled_ref, weights_ref, result_ref, act_ref, slope_ref, total_ref):
    step = pl.program_id(0)
    blocks, places, width = pooled_ref.shape
    pooled = pooled_ref[...].reshape(blocks * places, width)
    pre = dot(pooled, weights_ref[0, 0])
    square = pre * pre
    bent = jnp.tanh(SLOPE * pre * (1.0 + CUBIC * square))
    half = 0.5 * (1.0 + bent)
    act = (pre * half).astype(BF16)
    act_ref[0] = act
    slope_ref[0] = half + 0.5 * pre * (1.0 - bent * bent) * (SLOPE * (1.0 + 3.0 * CUBIC * square))
    result = dot_nt(act, weights_ref[0, 1])

    @pl.when(step == 0)
    def _():
        total_ref[...] = result

    @pl.when(step > 0)
    def _():
        total_ref[...] += result

    @pl.when(step == steps - 1)
    def _():
        result_ref[...] = total_ref[...].astype(BF16).reshape(blocks, places, width)


def run_experts(pooled, weights):
    blocks, places, width = pooled.shape
    steps, _, _, tile = weights.shape
    count = blocks * places
    return pl.pallas_call(
        functools.partial(expert_kernel, steps),
        grid=(steps,),
        in_specs=[constant_spec(pooled.shape), pl.BlockSpec((1, 2, width, tile), lambda i: (i, 0, 0, 0))],
        out_specs=[
            constant_spec(pooled.shape),
            pl.BlockSpec((1, count, tile), lambda i: (i, 0, 0)),
            pl.BlockSpec((1, count, tile), lambda i: (i, 0, 0)),
        ],
        out_shape=[
            jax.ShapeDtypeStruct(pooled.shape, BF16),
            jax.ShapeDtypeStruct((steps, count, tile), BF16),
            jax.ShapeDtypeStruct((steps, count, tile), F32),
        ],
        scratch_shapes=[pltpu.VMEM((count, width), F32)],
        compiler_params=pltpu.CompilerParams(vmem_limit_bytes=40 << 20),
        cost_estimate=pl.CostEstimate(
            flops=count * width * tile * steps * 8, bytes_accessed=width * tile * steps * 8, transcendentals=0
        ),
        name="experts",
    )(pooled, weights)


def expert_back_kernel(steps, slots_ref, pooled_ref, grads_ref, result_ref, act_ref, slope_ref, weights_ref, back_ref, grad_ref, total_ref):
    step = pl.program_id(0)
    blocks, places, width = pooled_ref.shape
    count = blocks * places
    pooled = pooled_ref[...].reshape(count, width)
    grads = grads_ref[...].reshape(count, width)
    act = act_ref[0]
    grad_pre = (dot(grads, weights_ref[0, 1]) * slope_ref[0]).astype(BF16)
    grad_ref[0, 0] = dot_tn(pooled, grad_pre).astype(BF16)
    grad_ref[0, 1] = dot_tn(grads, act).astype(BF16)
    part = dot_nt(grad_pre, weights_ref[0, 0])

    @pl.when(step == 0)
    def _():
        total_ref[...] = part

    @pl.when(step > 0)
    def _():
        total_ref[...] += part

    @pl.when(step == steps - 1)
    def _():
        grad_pooled = total_ref[...].astype(BF16)
        back_ref[:, :places] = grad_pooled.reshape(blocks, places, width)
        result = result_ref[...].reshape(count, width)
        product = result.astype(F32) * grads.astype(F32) + grad_pooled.astype(F32) * pooled.astype(F32)
        high = product.astype(BF16)
        rest = (product - high.astype(F32)).astype(BF16)
        ones = jnp.ones((16, width), BF16)
        sums = dot_nt(ones, high) + dot_nt(ones, rest)
        top = sums.astype(BF16)
        low = (sums - top.astype(F32)).astype(BF16)
        for b in range(blocks):
            here = slice(b * places, b * places + places)
            fill = jnp.zeros((16, width - 2 * places), BF16)
            back_ref[b, places:] = jnp.concatenate([top[:, here], low[:, here], fill], axis=1)


def pull_experts(slots, pooled, grads, result, act, slope, weights):
    blocks, places, width = pooled.shape
    steps, _, _, tile = weights.shape
    count = blocks * places
    return pl.pallas_call(
        functools.partial(expert_back_kernel, steps),
        grid_spec=pltpu.PrefetchScalarGridSpec(
            num_scalar_prefetch=1,
            grid=(steps,),
            in_specs=[constant_spec(pooled.shape)] * 3
            + [pl.BlockSpec((1, count, tile), lambda i, slots: (i, 0, 0))] * 2
            + [pl.BlockSpec((1, 2, width, tile), lambda i, slots: (i, 0, 0, 0))],
            out_specs=[
                constant_spec((blocks, places + 16, width)),
                pl.BlockSpec((1, 2, width, tile), lambda i, slots: (slots[i], 0, 0, 0)),
            ],
            scratch_shapes=[pltpu.VMEM((count, width), F32)],
        ),
        out_shape=[
            jax.ShapeDtypeStruct((blocks, places + 16, width), BF16),
            jax.ShapeDtypeStruct(weights.shape, BF16),
        ],
        compiler_params=pltpu.CompilerParams(vmem_limit_bytes=40 << 20),
        cost_estimate=pl.CostEstimate(
            flops=count * width * tile * steps * 12, bytes_accessed=width * tile * steps * 8, transcendentals=0
        ),
        name="pull_experts",
    )(slots, pooled, grads, result, act, slope, weights)


def spread_kernel(group, count, slots_ref, gates_ref, grads_ref, hidden_ref, *rest):
    parts, (out_ref, change_ref, result_ref) = rest[:count], rest[-3:]
    for k in range(count):
        @pl.when(pl.program_id(0) == k)
        def _():
            result_ref[...] = parts[k][...]

    rows, places = grads_ref.shape[0], grads_ref.shape[1]
    experts = result_ref.shape[0]
    sub = 16
    columns = gates_ref.shape[1]

    def step(s, _):
        here = pl.ds(pl.multiple_of(s * sub, sub), sub)
        results = [result_ref[e, here, :].astype(F32) * group for e in range(experts)]
        gates = gates_ref[here, :].astype(BF16).astype(F32)
        lane = iota((sub, columns), 1)
        changes = jnp.zeros((sub, columns), F32)
        for r in range(rows):
            grads = grads_ref[r, here, :].astype(F32)
            for e in range(experts):
                both = jnp.sum(grads * results[e], axis=1, keepdims=True)
                changes = jnp.where(lane == r * experts + e, both, changes)
            total = sum(gates[:, r * experts + e: r * experts + e + 1] * results[e] for e in range(experts))
            out_ref[r, here, :] = (hidden_ref[r, here, :] + total.astype(BF16).astype(F32)).astype(BF16)
        change_ref[0, here, :] = changes
        return 0

    lax.fori_loop(0, places // sub, step, 0, unroll=8)


def slot_of(found):
    found = list(found)
    step = found[-1] - found[0]
    return lambda i, slots: slots[found[0] + i * step]


def spread_tokens(found, slots, gates, cotangent, hidden, group, held):
    rows, span, width = hidden.shape
    parts = list(found.values())
    experts, places, _ = parts[0].shape
    at = slot_of(found)
    block = pl.BlockSpec((rows, places, width), lambda i, slots: (0, at(i, slots), 0))
    columns = gates.shape[1]
    aliased = [] if held is None else [held]
    return pl.pallas_call(
        functools.partial(spread_kernel, group, len(parts)),
        grid_spec=pltpu.PrefetchScalarGridSpec(
            num_scalar_prefetch=1,
            grid=(len(parts),),
            in_specs=[pl.BlockSpec((places, columns), lambda i, slots: (at(i, slots), 0)), block, block]
            + [constant_spec(part.shape) for part in parts]
            + [pl.BlockSpec(memory_space=pltpu.HBM) for _ in aliased],
            out_specs=[block, pl.BlockSpec((1, places, columns), lambda i, slots: (i, 0, 0))],
            scratch_shapes=[pltpu.VMEM(parts[0].shape, BF16)],
        ),
        out_shape=[
            jax.ShapeDtypeStruct((rows, span, width), BF16),
            jax.ShapeDtypeStruct((len(parts), places, columns), F32),
        ],
        input_output_aliases={4 + len(parts): 0} if aliased else {},
        compiler_params=pltpu.CompilerParams(vmem_limit_bytes=58 << 20),
        cost_estimate=pl.CostEstimate(
            flops=len(parts) * rows * places * width * 5000, bytes_accessed=rows * places * width * 10, transcendentals=0
        ),
        name="spread",
    )(slots, gates, cotangent, hidden, *parts, *aliased)


def pull_kernel(first, count, slots_ref, gates_ref, change_ref, mixed_ref, hidden_ref, cotangent_ref, attended_ref, router_ref, gains_ref, weight_ref, *rest):
    parts, rest = rest[:count], rest[count:]
    out_ref, low_ref, router_grad_ref, project_ref, sums_ref, pooled_ref, logits_ref, grad_ref = rest[-8:]

    @pl.when(pl.program_id(0) == 0)
    def _():
        if first:
            router_grad_ref[...] = jnp.zeros_like(router_grad_ref)
            project_ref[...] = jnp.zeros_like(project_ref)
            sums_ref[...] = jnp.zeros_like(sums_ref)
        else:
            router_grad_ref[...] = rest[2][...]
            project_ref[...] = rest[3][...]
            sums_ref[...] = rest[4][...]

    for k in range(count):
        @pl.when(pl.program_id(0) == k)
        def _():
            pooled_ref[...] = parts[k][...]

    rows, places, width = mixed_ref.shape
    experts = pooled_ref.shape[0]
    sub = 16
    columns = gates_ref.shape[1]
    inner = jnp.zeros((places, columns), F32)
    for e in range(experts):
        pick = (iota((16, columns), 0) == 0) & (iota((16, columns), 1) % experts == e)
        pick = jnp.where(pick, 1.0, 0.0).astype(BF16)
        inner += dot_tn(pooled_ref[e, places:, :places], pick) + dot_tn(pooled_ref[e, places:, places: 2 * places], pick)

    def change(s, _):
        here = pl.ds(pl.multiple_of(s * sub, sub), sub)
        pooled = [pooled_ref[e, here, :].astype(F32) for e in range(experts)]
        lane = iota((sub, columns), 1)
        changes = jnp.zeros((sub, columns), F32)
        for r in range(rows):
            mixed = mixed_ref[r, here, :].astype(F32)
            for e in range(experts):
                both = jnp.sum(pooled[e] * mixed, axis=1, keepdims=True)
                changes = jnp.where(lane == r * experts + e, both, changes)
        logits_ref[here, :] = changes
        return 0

    lax.fori_loop(0, places // sub, change, 0, unroll=8)
    changes = (logits_ref[...] + change_ref[0]).astype(BF16).astype(F32)
    low = (gates_ref[...] * (changes - inner)).astype(BF16)
    for r in range(rows):
        grad_ref[r] = dot(low, router_ref[r])
        router_grad_ref[...] += dot_tn(low, mixed_ref[r])[r * experts: r * experts + experts]

    def spread(s, _):
        here = pl.ds(pl.multiple_of(s * sub, sub), sub)
        pooled = [pooled_ref[e, here, :].astype(F32) for e in range(experts)]
        gates = gates_ref[here, :].astype(BF16).astype(F32)
        for r in range(rows):
            grad_ref[r, here, :] = sum(
                (gates[:, r * experts + e: r * experts + e + 1] * pooled[e] for e in range(experts)),
                grad_ref[r, here, :],
            )
        return 0

    lax.fori_loop(0, places // sub, spread, 0, unroll=8)

    for r in range(rows):
        grads = grad_ref[r].astype(BF16).astype(F32)
        hat, inverse = normalise(hidden_ref[r])
        sums_ref[0:1] += jnp.sum(grads * hat, axis=0, keepdims=True)
        sums_ref[1:2] += jnp.sum(grads, axis=0, keepdims=True)
        total = cotangent_ref[r].astype(F32) + pull_norm(grads * gains_ref[2:3], hat, inverse)
        out_ref[r] = total
        total = total.astype(BF16)
        project_ref[...] += dot_tn(attended_ref[r], total)
        low_ref[r] = dot_nt(total, weight_ref[...]).astype(BF16)


def pull_slots(found, slots, gates, change, mixed, hidden, cotangent, attended, router, gains, packed, held, weight=20):
    rows, span, width = mixed.shape
    parts = list(found.values())
    experts, depth, _ = parts[0].shape
    places = span // slots.shape[0]
    at = slot_of(found)
    block = pl.BlockSpec((rows, places, width), lambda i, slots: (0, at(i, slots), 0))
    columns = gates.shape[1]
    sums = [(experts, width), (width, width), (8, width)]
    ins = [
        pl.BlockSpec((places, columns), lambda i, slots: (at(i, slots), 0)),
        pl.BlockSpec((1, places, columns), lambda i, slots: (i, 0, 0)),
        block,
        block,
        block,
        block,
        constant_spec(router.shape),
        constant_spec(gains.shape),
        constant_spec((width, width), 0, 3),
    ] + [constant_spec(part.shape) for part in parts]
    aliases = {}
    if held is not None:
        aliases = {len(ins) + 1: 0, len(ins) + 2: 1}
        ins += [pl.BlockSpec(memory_space=pltpu.HBM)] * 2 + [constant_spec(shape) for shape in sums]
    return pl.pallas_call(
        functools.partial(pull_kernel, held is None, len(parts)),
        grid_spec=pltpu.PrefetchScalarGridSpec(
            num_scalar_prefetch=1,
            grid=(len(parts),),
            in_specs=ins,
            out_specs=[block, block] + [constant_spec(shape) for shape in sums],
            scratch_shapes=[
                pltpu.VMEM(parts[0].shape, BF16),
                pltpu.VMEM((places, columns), F32),
                pltpu.VMEM((rows, places, width), F32),
            ],
        ),
        out_shape=[jax.ShapeDtypeStruct((rows, span, width), F32), jax.ShapeDtypeStruct((rows, span, width), BF16)]
        + [jax.ShapeDtypeStruct(shape, F32) for shape in sums],
        input_output_aliases=aliases,
        compiler_params=pltpu.CompilerParams(vmem_limit_bytes=58 << 20),
        cost_estimate=pl.CostEstimate(
            flops=len(parts) * rows * places * width * width * weight,
            bytes_accessed=rows * places * weight,
            transcendentals=0,
        ),
        name="pull_slots",
    )(slots, gates, change, mixed, hidden, cotangent, attended, router, gains, packed, *parts, *(held or ()))


def project_kernel(experts, grads_ref, tokens_ref, gains_ref, weight_ref, project_ref, late_ref, out_ref, product_ref, sums_ref):
    width, wide = product_ref.shape
    steps = pl.num_programs(0) * pl.num_programs(1)
    step = pl.program_id(0) * pl.num_programs(1) + pl.program_id(1)

    @pl.when(step == 0)
    def _():
        product_ref[...] = jnp.zeros_like(product_ref)
        sums_ref[...] = jnp.zeros_like(sums_ref)

    hat = normalise(tokens_ref[0].astype(F32))[0].astype(BF16)
    ones = jnp.ones((hat.shape[0], 8), BF16)
    product_ref[...] += dot_tn(hat, grads_ref[0])
    sums_ref[...] += dot_tn(ones, grads_ref[0])

    @pl.when(step == steps - 1)
    def _():
        sums = sums_ref[0:1, :]
        for at in range(0, width, 64):
            here = slice(at, at + 64)
            product = product_ref[here, :]
            weights = weight_ref[here, :].astype(F32)
            out_ref[here, :wide] = (gains_ref[here, 0:1] * product + gains_ref[here, 1:2] * sums).astype(BF16)
            out_ref[here, wide: wide + width] = project_ref[here, :].astype(BF16)
            late = late_ref[here, :]
            lane = iota(late.shape, 1)
            late = jnp.where(lane == experts, jnp.sum(weights * product, axis=1, keepdims=True), late)
            late = jnp.where(lane == experts + 1, jnp.sum(weights * sums, axis=1, keepdims=True), late)
            out_ref[here, wide + width:] = late.astype(BF16)


def project_grads(grads, tokens, gains, packed, project, late, experts, tile=1024):
    rows, length, width = tokens.shape
    wide = 3 * width
    return pl.pallas_call(
        functools.partial(project_kernel, experts),
        grid=(rows, length // tile),
        in_specs=[
            pl.BlockSpec((1, tile, wide), lambda r, t: (r, t, 0)),
            pl.BlockSpec((1, tile, width), lambda r, t: (r, t, 0)),
            constant_spec(gains.shape),
            constant_spec((width, wide)),
            constant_spec(project.shape),
            constant_spec(late.shape),
        ],
        out_specs=constant_spec(packed.shape),
        out_shape=jax.ShapeDtypeStruct(packed.shape, BF16),
        scratch_shapes=[pltpu.VMEM((width, wide), F32), pltpu.VMEM((8, wide), F32)],
        compiler_params=pltpu.CompilerParams(vmem_limit_bytes=58 << 20),
        cost_estimate=pl.CostEstimate(flops=rows, bytes_accessed=rows, transcendentals=0),
        name="project_grads",
    )(grads, tokens, gains, packed, project, late)


def tokens_kernel(grads_ref, tokens_ref, hidden_ref, gains_ref, weight_ref, *rest):
    out_ref = rest[-1]
    for at in pieces(tokens_ref.shape[1]):
        hat, inverse = normalise(tokens_ref[0, at].astype(F32))
        grads = dot_nt(grads_ref[0, at], weight_ref[...])
        out_ref[0, at] = hidden_ref[0, at] + pull_norm(grads * gains_ref[0:1], hat, inverse)


def pull_tokens(grads, tokens, hidden, gains, packed, row_from, row_to, held=None, tile=1024):
    rows, length, width = tokens.shape
    block = pl.BlockSpec((1, tile, width), lambda r, t: (r + row_from, t, 0))
    aliased = [] if held is None else [held]
    return pl.pallas_call(
        tokens_kernel,
        grid=(row_to - row_from, length // tile),
        in_specs=[
            pl.BlockSpec((1, tile, 3 * width), lambda r, t: (r + row_from, t, 0)),
            block,
            block,
            constant_spec(gains.shape),
            constant_spec((width, 3 * width)),
        ]
        + [pl.BlockSpec(memory_space=pltpu.HBM) for _ in aliased],
        out_specs=block,
        out_shape=jax.ShapeDtypeStruct((rows, length, width), F32),
        input_output_aliases={5: 0} if aliased else {},
        compiler_params=pltpu.CompilerParams(vmem_limit_bytes=58 << 20),
        cost_estimate=pl.CostEstimate(
            flops=(row_to - row_from) * length * width * width * 20,
            bytes_accessed=(row_to - row_from) * length * width * 16,
            transcendentals=0,
        ),
        name="pull_tokens",
    )(grads, tokens, hidden, gains, packed, *aliased)


def ring_order(size):
    inner = 2 if size % 2 == 0 and size > 2 else 1
    outer = size // inner
    up = [z * inner for z in range(outer)]
    if inner == 1:
        return up
    return up + [z * inner + 1 for z in reversed(range(outer))]


def shift(value, order, step):
    count = len(order)
    return lax.ppermute(value, "dp", [(order[i], order[(i + step) % count]) for i in range(count)])


def flip(value, bit, axis="fsdp"):
    count = lax.axis_size(axis)
    return lax.ppermute(value, axis, [(i, i ^ bit) for i in range(count)])


def turn(value, step, axis="dp"):
    count = lax.axis_size(axis)
    return lax.ppermute(value, axis, [(i, (i + step) % count) for i in range(count)])


def take(values, index):
    starts = (index,) + (jnp.uint32(0),) * (values.ndim - 1)
    return lax.dynamic_slice(values, starts, (1,) + values.shape[1:])[0]


def put(values, value, index):
    return lax.dynamic_update_slice(values, value[None], (index,) + (jnp.uint32(0),) * value.ndim)


def add(a, b):
    return (a.astype(F32) + b.astype(F32)).astype(BF16)


def together(*values):
    return lax.optimization_barrier(values)


class Ring:
    def __init__(self, value, order):
        self.order, self.done = order, 0
        self.ahead = self.behind = value

    def left(self):
        return self.done < len(self.order) // 2

    def after(self, *values):
        self.ahead, self.behind, *_ = together(self.ahead, self.behind, *values)

    def step(self, *beside):
        count = len(self.order)
        self.done += 1
        slot = count - self.done
        ahead, behind = self.ahead, self.behind
        middle = 2 * self.done == count and ahead.shape[0] % 2 == 0
        if middle:
            half = ahead.shape[0] // 2
            ahead, behind = ahead[:half], behind[half:]
        ahead = shift(ahead, self.order, 1)
        if 2 * self.done < count or middle:
            behind = shift(behind, self.order, -1)
        ahead, behind, *beside = together(ahead, behind, *beside)
        self.ahead, self.behind = ahead, behind
        if middle:
            return {slot: jnp.concatenate([ahead, behind], axis=0)}, beside
        return {slot: ahead, self.done: behind} if 2 * self.done < count else {slot: ahead}, beside


def gather_all(value, steps, *beside):
    pair = pair_of(lax.axis_size("dp"))
    lines = lax.axis_size("dp") // pair
    size = lax.axis_size("fsdp")
    here = lax.axis_index("fsdp")

    def both(value, bit, axis, index):
        other = flip(value, bit, axis)
        upper = (index & bit) != 0
        return jnp.stack([jnp.where(upper, other, value), jnp.where(upper, value, other)])

    whole = put(jnp.zeros((lines,) + value.shape, value.dtype), value, steps[0])
    for k in range(1, lines):
        whole = put(whole, turn(value, -k * pair), steps[k])
    if beside:
        whole, *beside = together(whole, *beside)
    whole = both(whole, 1, "dp", lax.axis_index("dp")) if pair == 2 else whole[None]
    whole = jnp.moveaxis(whole, 0, 1)
    whole = whole.reshape((lines * pair, 1) + value.shape)
    bit = size // 2
    while bit:
        whole = both(whole, bit, "fsdp", here)
        whole = jnp.moveaxis(whole, 0, 2)
        whole = whole.reshape((lines * pair, -1) + value.shape)
        bit //= 2
    return whole, beside


def scatter_all(values, steps, work):
    owners, size = lax.axis_size("dp"), lax.axis_size("fsdp")
    bits = size.bit_length() - 1
    here = lax.axis_index("fsdp")
    width = values.shape[1]
    pair = pair_of(owners)
    work = list(work)

    def half(held, axis, upper, bit, name):
        low, high = (lax.index_in_dim(held, i, axis, keepdims=False) for i in (0, 1))
        came = flip(jnp.where(upper, low, high), bit, name)
        if work:
            came, = work.pop(0)(came)
        return add(jnp.where(upper, high, low), came)

    held = values.reshape((owners // pair, pair) + (2,) * bits + (-1, width))
    for level in range(bits):
        held = half(held, bits + 1 - level, ((here >> level) & 1) != 0, 1 << level, "fsdp")
    held = half(held, 1, (lax.axis_index("dp") & 1) != 0, 1, "dp") if pair == 2 else held[:, 0]
    came = [turn(take(held, steps[k]), k * pair) for k in range(1, owners // pair)]
    while work:
        came = work.pop(0)(*came)
    return sum((value.astype(F32) for value in came), take(held, steps[0]).astype(F32))


def pair_of(owners):
    return 2 if owners % 2 == 0 else 1


def exchange(values):
    return jnp.stack([values[0]] + [flip(values[k], k) for k in range(1, values.shape[0])])


def per_device(
    tokens,
    segment_ids,
    pad_tokens,
    cotangent,
    project_in,
    project_out,
    router_weight,
    expert_in,
    expert_out,
    first_gain,
    first_bias,
    second_gain,
    second_bias,
):
    blocks_here, rows, length, width = tokens.shape
    tokens = tokens.reshape(rows, length, width)
    cotangent = cotangent.reshape(rows, length, width)
    segments = segment_ids.reshape(rows, length)
    group = pad_tokens.shape[1]
    owners = lax.axis_size("dp")
    experts = router_weight.shape[1]
    order = ring_order(owners)
    data_index = lax.axis_index("dp")
    expert_index = lax.axis_index("fsdp")
    places = length // owners

    pair = pair_of(owners)
    lines = owners // pair
    ring = np.array([[order[(order.index(d) + k) % owners] for k in range(owners)] for d in range(owners)], np.int32)
    place = np.array(
        [[(o % pair ^ d % pair) * lines + (o // pair - d // pair) % lines for o in ring[d]] for d in range(owners)],
        np.int32,
    )
    line = np.array([[(d // pair + k) % lines for k in range(lines)] for d in range(owners)], np.int32)
    tables = np.concatenate([ring, place, line], axis=1)
    tables = lax.dynamic_slice(
        jnp.asarray(tables), (data_index.astype(jnp.uint32), jnp.uint32(0)), (1, tables.shape[1])
    )[0]
    slots, shares = tables[:owners], tables[owners: 2 * owners]
    spots = [tables[k].astype(jnp.uint32) for k in range(owners)]
    steps = [tables[2 * owners + k].astype(jnp.uint32) for k in range(lines)]

    vectors = jnp.stack([first_gain, first_bias, second_gain, second_bias], axis=1)
    small = jnp.concatenate([router_weight, vectors], axis=1)
    small = jnp.pad(small, ((0, 0), (0, 128 - small.shape[1])))
    packed = jnp.concatenate([project_in, project_out, small], axis=1)
    packed, (expert_in, expert_out) = gather_all(packed, steps, expert_in, expert_out)
    weights = jnp.stack([expert_in[0], expert_out[0].T])
    packed = packed.reshape(width, packed.shape[-1])
    packed, weights = together(packed, weights)
    kept = {0: weights}
    weights = Ring(weights, order)
    small = packed[:, 4 * width:].T
    mine = (jnp.arange(experts)[:, None] ^ jnp.arange(experts)[None, :]) == expert_index
    router = jnp.sum(jnp.where(mine[:, :, None], small[None, :experts], 0), axis=1).astype(BF16)
    spread_router = jnp.stack(
        [jnp.pad(router, ((r * experts, (rows - 1 - r) * experts), (0, 0))) for r in range(rows)]
    )
    gains = jnp.pad(small[experts: experts + 4].astype(F32), ((0, 4), (0, 0)))

    own_pads = lax.dynamic_slice_in_dim(pad_tokens[0], data_index * rows, rows, 0)
    vlens = (length - own_pads).astype(jnp.int32)
    starts = jnp.zeros_like(segments)
    for doc in range(1, 4):
        before = jnp.sum((segments < doc).astype(jnp.int32), axis=1, keepdims=True)
        starts = jnp.where(segments == doc, before, starts)
    starts = starts.reshape(rows, length // QB, QB)
    lows = starts[:, :, 0] // QB

    def meanwhile(value):
        if not weights.left():
            return value
        found, (value,) = weights.step(value)
        kept.update(found)
        return value

    joined = meanwhile(join_tokens(tokens, gains, packed))
    attended, logs = attn_fwd(joined, starts, lows, vlens, 1)
    attended = meanwhile(attended)
    hidden, mixed, logits = mix_tokens(
        attended, tokens, gains, packed, jnp.pad(router, ((0, 16 - experts), (0, 0))), 0
    )
    logits = meanwhile(logits)[:, :experts]
    valid = (jnp.arange(length)[None, :] < vlens[:, None])[:, None, :]
    highest = jnp.max(jnp.where(valid, logits, NEGATIVE), axis=0)
    total = jnp.sum(jnp.where(valid, jnp.exp(logits - highest), 0.0), axis=0)
    stats = jnp.stack([highest, total])[None]
    if pair == 2:
        stats = jnp.concatenate([stats, flip(stats, 1, "dp")])
    stats = jnp.concatenate([stats] + [turn(stats, k * pair) for k in range(1, lines)])
    tops = jnp.max(stats[:, 0], axis=0)
    total = jnp.sum(stats[:, 1] * jnp.exp(stats[:, 0] - tops), axis=0)
    gates = jnp.where(valid, jnp.exp(jnp.where(valid, logits - tops, NEGATIVE)) / total, 0.0)
    gates = gates.reshape(rows * experts, length).T
    pooled = meanwhile(pool_tokens(slots, gates, mixed, experts, 1.0))
    while weights.left():
        kept.update(weights.step()[0])
    weights = jnp.stack([kept[k] for k in range(owners)])
    grads = pool_tokens(slots, gates, cotangent, experts, float(group))

    half = experts // 2
    first = [(pooled[:, :half], 1), (pooled[:, half:], -1)]
    second = [(grads[:, :half], 1), (grads[:, half:], -1)]
    held = [part[-way % owners] for part, way in first]
    later = [part[-way % owners] for part, way in second]
    for step in range(owners - 1):
        came = [shift(value, order, way) for value, (_, way) in zip(held, first)]
        if step == 0:
            *came, one, two = together(*came, *later)
            later = [one, two]
        held = [add(value, part[-way * (2 + step) % owners]) for value, (part, way) in zip(came, first)]
        came = [shift(value, order, way) for value, (_, way) in zip(later, second)]
        later = [add(value, part[-way * (2 + step) % owners]) for value, (part, way) in zip(came, second)]
    pooled = exchange(jnp.concatenate(held, axis=0))
    result, act, slope = run_experts(pooled, weights)
    grads = exchange(jnp.concatenate(later, axis=0))
    grad_pooled, grad_weights = pull_experts(shares, pooled, grads, result, act, slope, weights)

    result = exchange(result)
    back = exchange(grad_pooled)

    def pull(found, change, out, *weight):
        return pull_slots(
            found, slots, gates, change, mixed, hidden, cotangent, attended, spread_router, gains, packed, out, *weight
        )

    def spread(found, out):
        return spread_tokens(found, slots, gates, cotangent, hidden, group, out)

    turns = owners // 2
    first, second = Ring(result, order), Ring(back, order)
    found, (grad_weights,) = first.step(grad_weights)
    groups, arrived = [{0: result}, found], [{0: back}]
    out, pulled, changes = None, None, []
    for step in range(turns + 1):
        work = []
        for k in [step] if step < turns - 1 else [turns - 1, turns] if step == turns - 1 else []:
            out, change = spread(groups[k], out)
            changes.append(change)
            work = [out]
        if 0 < step < turns - 1 or step == turns:
            k = step - 1 if step < turns else turns - 2
            pulled = pull(arrived[k], changes[k], pulled)
            work += pulled
        if step > 0:
            if step == 1:
                second.after(*groups[2].values())
        if first.left():
            found, _ = first.step()
            groups.append(found)
        if second.left() and step > 0:
            found, work = second.step(*work)
            arrived.append(found)
        if step < turns:
            out, *work = work
        pulled = work or pulled
    grad_weights, *_ = together(grad_weights, *arrived[turns].values())
    if pair == 2:
        came = flip(grad_weights[lines:], 1, "dp")
    pulled = pull(arrived[turns - 1], changes[turns - 1], pulled, 0)
    layer_out = out
    pulled = pull(arrived[turns], changes[turns], pulled, 0)
    grad_hidden, grad_attended, router_grad, grad_proj_out, sums_two = pulled
    split = rows - max(1, rows // 2)
    grads = attn_bwd(joined, grad_attended, attended, logs, starts, lows, vlens, 0, split)
    grad_weights = grad_weights[:lines]
    if pair == 2:
        came, grads = together(came, grads)
        grad_weights = add(grad_weights, came)
    grad_parts = [turn(grad_weights[k], k * pair) for k in range(1, lines)]
    grads = attn_bwd(joined, grad_attended, attended, logs, starts, lows, vlens, split, rows, grads)
    router_grad = jnp.sum(jnp.where(mine[:, :, None], router_grad[None], 0.0), axis=1)
    late = jnp.concatenate([router_grad, jnp.zeros((2, width), F32), sums_two[:2]], axis=0).T
    late = jnp.pad(late, ((0, 0), (0, 128 - late.shape[1])))
    reduced = project_grads(grads, tokens, gains.T, packed, grad_proj_out, late, experts)
    reduced, *grad_parts = together(reduced, *grad_parts)
    made = []

    def tokens_beside(*came):
        *came, grad = together(*came, pull_tokens(grads, tokens, grad_hidden, gains, packed, 0, rows))
        made.append(grad)
        return came

    def weights_beside(*came):
        value, *parts = together(*came, *grad_parts)
        made.append(sum((part.astype(F32) for part in parts), grad_weights[0].astype(F32)))
        return [value]

    reduced = scatter_all(reduced, steps, [lambda *came: came, tokens_beside, weights_beside])
    tokens_grad, grad_weights = made
    late = reduced[:, 4 * width:]
    return (
        layer_out[None],
        tokens_grad[None],
        reduced[:, : 3 * width],
        reduced[:, 3 * width: 4 * width],
        late[:, :experts],
        grad_weights[0][None],
        grad_weights[1].T[None],
        late[:, experts],
        late[:, experts + 1],
        late[:, experts + 2],
        late[:, experts + 3],
    )


def solution(mesh):
    in_specs = (
        P("fsdp", "dp", None, None),
        P("fsdp", "dp", None),
        P("fsdp", None),
        P("fsdp", "dp", None, None),
        P(("dp", "fsdp"), None),
        P(("dp", "fsdp"), None),
        P(("dp", "fsdp"), None),
        P("fsdp", None, "dp"),
        P("fsdp", "dp", None),
        P(("dp", "fsdp")),
        P(("dp", "fsdp")),
        P(("dp", "fsdp")),
        P(("dp", "fsdp")),
    )
    out_specs = (
        P("fsdp", "dp", None, None),
        P("fsdp", "dp", None, None),
        P(("dp", "fsdp"), None),
        P(("dp", "fsdp"), None),
        P(("dp", "fsdp"), None),
        P("fsdp", None, "dp"),
        P("fsdp", "dp", None),
        P(("dp", "fsdp")),
        P(("dp", "fsdp")),
        P(("dp", "fsdp")),
        P(("dp", "fsdp")),
    )
    return jax.shard_map(
        per_device, mesh=mesh, in_specs=in_specs, out_specs=out_specs, check_vma=False
    )
```

```python
import functools, math
import jax
import jax.numpy as jnp
import numpy as np
from jax import lax
from jax.experimental import pallas as pl
from jax.experimental.pallas import tpu as pltpu
from jax.sharding import PartitionSpec as P

NEGATIVE = -1e30
QB = 128
F32 = jnp.float32
BF16 = jnp.bfloat16
NT = (((1,), (1,)), ((), ()))
TN = (((0,), (0,)), ((), ()))


def dot(a, b):
    return jnp.dot(a, b, preferred_element_type=F32)


def dot_nt(a, b):
    return lax.dot_general(a, b, NT, preferred_element_type=F32)


def dot_tn(a, b):
    return lax.dot_general(a, b, TN, preferred_element_type=F32)


def iota(shape, axis):
    return lax.broadcasted_iota(jnp.int32, shape, axis)


def split_heads(x):
    low = iota(x.shape, 1) < 64
    zero = jnp.zeros_like(x)
    return jnp.concatenate([jnp.where(low, x, zero), jnp.where(low, zero, x)], axis=0)


def join_heads(x):
    half = x.shape[0] // 2
    low = iota((half, x.shape[1]), 1) < 64
    return jnp.where(low, x[:half], x[half:])


def attn_fwd_kernel(width, batch, count, lo_ref, vlen_ref, start_ref, joined_ref, out_ref, log_ref, bias_ref):
    row = pl.program_id(0) * batch

    def block(qb, _):
        lo = functools.reduce(jnp.minimum, [lo_ref[row + r, qb] for r in range(batch)])
        base = pl.multiple_of(qb * QB, QB)
        first = pl.multiple_of(lo * QB, QB)
        own = pl.ds(base, QB)

        def variant(blocks):
            span = blocks * QB
            keys = pl.ds(first, span)
            i = base + iota((QB, QB), 0)
            bias = []
            for r in range(batch):
                begins = jnp.broadcast_to(start_ref[r, pl.ds(qb, 1), :], (QB, QB)).T
                for b in range(blocks):
                    j = first + b * QB + iota((QB, QB), 1)
                    ok = ((j >= begins) & (j <= i) & (j < vlen_ref[row + r])) | (j == i)
                    bias_ref[r, :, b * QB:(b + 1) * QB] = jnp.where(ok, 0.0, NEGATIVE)
                bias.append(jnp.concatenate([bias_ref[r, :, :span]] * 2, axis=0))
            work = [(r, lane) for r in range(batch) for lane in range(0, width, 128)]
            query = [split_heads(joined_ref[r, own, pl.ds(at, 128)] * jnp.asarray(0.125, BF16)) for r, at in work]
            scores = [dot_nt(q, joined_ref[r, keys, pl.ds(width + at, 128)]) for q, (r, at) in zip(query, work)]
            scores = [s + bias[r] for s, (r, _) in zip(scores, work)]
            tops = [jnp.max(s, axis=1, keepdims=True) for s in scores]
            raised = [jnp.exp(s - top) for s, top in zip(scores, tops)]
            totals = [jnp.sum(p, axis=1, keepdims=True) for p in raised]
            out = [
                dot(p.astype(BF16), joined_ref[r, keys, pl.ds(2 * width + at, 128)]) for p, (r, at) in zip(raised, work)
            ]
            for o, total, (r, at) in zip(out, totals, work):
                out_ref[r, own, pl.ds(at, 128)] = join_heads(o * (1.0 / total)).astype(BF16)
            lane = iota((QB, QB), 1)
            for r in range(batch):
                tile = jnp.zeros((QB, QB), F32)
                for top, total, (other, at) in zip(tops, totals, work):
                    if other == r:
                        log = top + jnp.log(total)
                        tile = jnp.where(lane == at // 64, log[:QB], tile)
                        tile = jnp.where(lane == at // 64 + 1, log[QB:], tile)
                log_ref[r, pl.ds(qb, 1)] = tile.T[None, : log_ref.shape[2]]

        for blocks in range(1, 6):
            pl.when(qb - lo + 1 == blocks)(functools.partial(variant, blocks))
        return 0

    lax.fori_loop(0, count, block, 0)


def attn_fwd(joined, starts, lows, vlens, batch=2):
    rows, length, triple = joined.shape
    width = triple // 3
    count = length // QB
    return pl.pallas_call(
        functools.partial(attn_fwd_kernel, width, batch, count),
        grid_spec=pltpu.PrefetchScalarGridSpec(
            num_scalar_prefetch=2,
            grid=(rows // batch,),
            in_specs=[
                pl.BlockSpec((batch, count, QB), lambda r, *_: (r, 0, 0)),
                pl.BlockSpec((batch, length, triple), lambda r, *_: (r, 0, 0)),
            ],
            out_specs=[
                pl.BlockSpec((batch, length, width), lambda r, *_: (r, 0, 0)),
                pl.BlockSpec((batch, count, width // 64, QB), lambda r, *_: (r, 0, 0, 0)),
            ],
            scratch_shapes=[pltpu.VMEM((batch, QB, 5 * QB), F32)],
        ),
        out_shape=[
            jax.ShapeDtypeStruct((rows, length, width), BF16),
            jax.ShapeDtypeStruct((rows, count, width // 64, QB), F32),
        ],
        compiler_params=pltpu.CompilerParams(vmem_limit_bytes=48 << 20),
        cost_estimate=pl.CostEstimate(
            flops=rows * length * 400 * 8 * 256 * 4, bytes_accessed=rows * length * triple * 2, transcendentals=0
        ),
        name="attend",
    )(lows, vlens, starts, joined)


def attn_bwd_kernel(width, row_from, batch, count, lo_ref, vlen_ref, start_ref, joined_ref, grad_ref, attended_ref, log_ref, *rest):
    out_ref, dk_ref, dv_ref, bias_ref = rest[-4:]
    row = pl.program_id(0) * batch + row_from
    dk_ref[...] = jnp.zeros_like(dk_ref)
    dv_ref[...] = jnp.zeros_like(dv_ref)

    def block(qb, _):
        lo = functools.reduce(jnp.minimum, [lo_ref[row + r, qb] for r in range(batch)])
        base = pl.multiple_of(qb * QB, QB)
        first = pl.multiple_of(lo * QB, QB)
        own = pl.ds(base, QB)

        def variant(blocks):
            span = blocks * QB
            keys = pl.ds(first, span)
            i = base + iota((QB, QB), 1)
            pick = jnp.where(iota((16, width), 1) // 64 == iota((16, width), 0), 1.0, 0.0).astype(BF16)
            bias, sums = [], []
            for r in range(batch):
                begins = start_ref[r, pl.ds(qb, 1), :]
                for b in range(blocks):
                    j = first + b * QB + iota((QB, QB), 0)
                    ok = ((j >= begins) & (j <= i) & (j < vlen_ref[row + r])) | (j == i)
                    bias_ref[r, b * QB:(b + 1) * QB, :] = jnp.where(ok, 0.0, NEGATIVE)
                bias.append(jnp.concatenate([bias_ref[r, :span, :]] * 2, axis=1))
                product = grad_ref[r, own, :].astype(F32) * attended_ref[r, own, :].astype(F32)
                high = product.astype(BF16)
                sums.append(dot_nt(pick, high) + dot_nt(pick, (product - high.astype(F32)).astype(BF16)))
            work = [(r, lane) for r in range(batch) for lane in range(0, width, 128)]
            query = [split_heads(joined_ref[r, own, pl.ds(at, 128)] * jnp.asarray(0.125, BF16)) for r, at in work]
            grads = [split_heads(grad_ref[r, own, pl.ds(at, 128)]) for r, at in work]
            prob, moved = [], []
            for q, g, (r, at) in zip(query, grads, work):
                head = at // 64
                log = log_ref[r, qb]
                log = jnp.concatenate([log[head: head + 1], log[head + 1: head + 2]], axis=1)
                total = jnp.concatenate([sums[r][head: head + 1], sums[r][head + 1: head + 2]], axis=1)
                scores = dot_nt(joined_ref[r, keys, pl.ds(width + at, 128)], q)
                change = dot_nt(joined_ref[r, keys, pl.ds(2 * width + at, 128)], g)
                p = jnp.exp(scores + bias[r] - log)
                prob.append(p.astype(BF16))
                moved.append((p * (change - total)).astype(BF16))
            for p, g, (r, at) in zip(prob, grads, work):
                dv_ref[r, keys, pl.ds(at, 128)] += dot(p, g)
            for m, q, (r, at) in zip(moved, query, work):
                dk_ref[r, keys, pl.ds(at, 128)] += dot(m, q)
            back = [dot_tn(m, joined_ref[r, keys, pl.ds(width + at, 128)]) for m, (r, at) in zip(moved, work)]
            for b, (r, at) in zip(back, work):
                out_ref[r, own, pl.ds(at, 128)] = (join_heads(b) * 0.125).astype(BF16)

        for blocks in range(1, 6):
            pl.when(qb - lo + 1 == blocks)(functools.partial(variant, blocks))
        return 0

    lax.fori_loop(0, count, block, 0)
    out_ref[:, :, width: 2 * width] = dk_ref[...].astype(BF16)
    out_ref[:, :, 2 * width:] = dv_ref[...].astype(BF16)


def attn_bwd(joined, grads, attended, logs, starts, lows, vlens, row_from, row_to, held=None, batch=1):
    rows, length, triple = joined.shape
    width = triple // 3
    count = length // QB
    aliased = [] if held is None else [held]
    skip = row_from // batch
    wide = pl.BlockSpec((batch, length, triple), lambda r, *_: (r + skip, 0, 0))
    slim = pl.BlockSpec((batch, length, width), lambda r, *_: (r + skip, 0, 0))
    return pl.pallas_call(
        functools.partial(attn_bwd_kernel, width, row_from, batch, count),
        grid_spec=pltpu.PrefetchScalarGridSpec(
            num_scalar_prefetch=2,
            grid=((row_to - row_from) // batch,),
            in_specs=[
                pl.BlockSpec((batch, count, QB), lambda r, *_: (r + skip, 0, 0)),
                wide,
                slim,
                slim,
                pl.BlockSpec((batch,) + logs.shape[1:], lambda r, *_: (r + skip, 0, 0, 0)),
            ]
            + [pl.BlockSpec(memory_space=pltpu.HBM) for _ in aliased],
            out_specs=wide,
            scratch_shapes=[
                pltpu.VMEM((batch, length, width), F32),
                pltpu.VMEM((batch, length, width), F32),
                pltpu.VMEM((batch, 5 * QB, QB), F32),
            ],
        ),
        out_shape=jax.ShapeDtypeStruct(joined.shape, BF16),
        input_output_aliases={7: 0} if aliased else {},
        compiler_params=pltpu.CompilerParams(vmem_limit_bytes=58 << 20),
        cost_estimate=pl.CostEstimate(
            flops=row_to * length * 400 * 8 * 256 * 20 if aliased else rows,
            bytes_accessed=rows * length,
            transcendentals=0,
        ),
        name="attend_back",
    )(lows, vlens, starts, joined, grads, attended, logs, *aliased)


def normalise(values):
    centred = values - jnp.mean(values, axis=-1, keepdims=True)
    inverse = lax.rsqrt(jnp.mean(centred * centred, axis=-1, keepdims=True) + 1e-05)
    return centred * inverse, inverse


def pull_norm(scaled, hat, inverse):
    return inverse * (
        scaled
        - jnp.mean(scaled, axis=-1, keepdims=True)
        - hat * jnp.mean(scaled * hat, axis=-1, keepdims=True)
    )


PIECE = 256


def pieces(count):
    return [slice(at, min(at + PIECE, count)) for at in range(0, count, PIECE)]


def constant_spec(shape, *where):
    where = where or (0,) * len(shape)
    return pl.BlockSpec(shape, lambda *_: where)


def join_kernel(tokens_ref, gains_ref, weight_ref, joined_ref):
    for at in pieces(tokens_ref.shape[1]):
        hat, _ = normalise(tokens_ref[0, at].astype(F32))
        normed = (hat * gains_ref[0:1] + gains_ref[1:2]).astype(BF16)
        joined_ref[0, at] = dot(normed, weight_ref[...]).astype(BF16)


def join_tokens(tokens, gains, packed, tile=1024):
    rows, length, width = tokens.shape
    return pl.pallas_call(
        join_kernel,
        grid=(rows, length // tile),
        in_specs=[
            pl.BlockSpec((1, tile, width), lambda r, t: (r, t, 0)),
            constant_spec(gains.shape),
            constant_spec((width, 3 * width)),
        ],
        out_specs=pl.BlockSpec((1, tile, 3 * width), lambda r, t: (r, t, 0)),
        out_shape=jax.ShapeDtypeStruct((rows, length, 3 * width), BF16),
        compiler_params=pltpu.CompilerParams(vmem_limit_bytes=40 << 20),
        cost_estimate=pl.CostEstimate(
            flops=rows * length * width * width * 6, bytes_accessed=rows * length * width * 8, transcendentals=0
        ),
        name="join",
    )(tokens, gains, packed)


def mixed_kernel(attended_ref, tokens_ref, gains_ref, weight_ref, router_ref, hidden_ref, mixed_ref, logits_ref):
    hidden = tokens_ref[0].astype(F32) + dot(attended_ref[0], weight_ref[...])
    hidden_ref[0] = hidden
    hat, _ = normalise(hidden)
    mixed = (hat * gains_ref[2:3] + gains_ref[3:4]).astype(BF16)
    mixed_ref[0] = mixed
    logits_ref[0] = dot_nt(router_ref[...], mixed)


def mix_tokens(attended, tokens, gains, packed, router, offset, tile=1024):
    rows, span, width = attended.shape
    block = pl.BlockSpec((1, tile, width), lambda r, t: (r, t, 0))
    return pl.pallas_call(
        mixed_kernel,
        grid=(rows, span // tile),
        in_specs=[
            block,
            pl.BlockSpec((1, tile, width), lambda r, t: (r, t + offset // tile, 0)),
            constant_spec(gains.shape),
            constant_spec((width, width), 0, 3),
            constant_spec(router.shape),
        ],
        out_specs=[block, block, pl.BlockSpec((1, router.shape[0], tile), lambda r, t: (r, 0, t))],
        out_shape=[
            jax.ShapeDtypeStruct((rows, span, width), F32),
            jax.ShapeDtypeStruct((rows, span, width), BF16),
            jax.ShapeDtypeStruct((rows, router.shape[0], span), F32),
        ],
        compiler_params=pltpu.CompilerParams(vmem_limit_bytes=40 << 20),
        cost_estimate=pl.CostEstimate(
            flops=rows * span * width * width * 2, bytes_accessed=rows * span * width * 10, transcendentals=0
        ),
        name="mix",
    )(attended, tokens, gains, packed, router)


def pool_kernel(experts, scale, slots_ref, gates_ref, values_ref, out_ref):
    rows, places = values_ref.shape[0], values_ref.shape[1]
    sub = 16

    def step(s, _):
        here = pl.ds(pl.multiple_of(s * sub, sub), sub)
        gates = gates_ref[here, :].astype(BF16).astype(F32)
        values = [values_ref[r, here, :].astype(F32) for r in range(rows)]
        for e in range(experts):
            total = sum(gates[:, r * experts + e: r * experts + e + 1] * values[r] for r in range(rows))
            out_ref[0, e, here, :] = (scale * total).astype(BF16)
        return 0

    lax.fori_loop(0, places // sub, step, 0, unroll=8)


def pool_tokens(slots, gates, values, experts, scale):
    rows, span, width = values.shape
    owners = slots.shape[0]
    places = span // owners
    return pl.pallas_call(
        functools.partial(pool_kernel, experts, scale),
        grid_spec=pltpu.PrefetchScalarGridSpec(
            num_scalar_prefetch=1,
            grid=(owners,),
            in_specs=[
                pl.BlockSpec((places, gates.shape[1]), lambda i, slots: (slots[i], 0)),
                pl.BlockSpec((rows, places, width), lambda i, slots: (0, slots[i], 0)),
            ],
            out_specs=pl.BlockSpec((1, experts, places, width), lambda i, slots: (i, 0, 0, 0)),
        ),
        out_shape=jax.ShapeDtypeStruct((owners, experts, places, width), BF16),
        compiler_params=pltpu.CompilerParams(vmem_limit_bytes=40 << 20),
        cost_estimate=pl.CostEstimate(
            flops=rows * span * width * 1000, bytes_accessed=rows * span * width * 8, transcendentals=0
        ),
        name="pool",
    )(slots, gates, values)


CUBIC = 0.044715
SLOPE = math.sqrt(2.0 / math.pi)


def expert_kernel(steps, pooled_ref, weights_ref, result_ref, act_ref, slope_ref, total_ref):
    step = pl.program_id(0)
    blocks, places, width = pooled_ref.shape
    pooled = pooled_ref[...].reshape(blocks * places, width)
    pre = dot(pooled, weights_ref[0, 0])
    square = pre * pre
    bent = jnp.tanh(SLOPE * pre * (1.0 + CUBIC * square))
    half = 0.5 * (1.0 + bent)
    act = (pre * half).astype(BF16)
    act_ref[0] = act
    slope_ref[0] = half + 0.5 * pre * (1.0 - bent * bent) * (SLOPE * (1.0 + 3.0 * CUBIC * square))
    result = dot_nt(act, weights_ref[0, 1])

    @pl.when(step == 0)
    def _():
        total_ref[...] = result

    @pl.when(step > 0)
    def _():
        total_ref[...] += result

    @pl.when(step == steps - 1)
    def _():
        result_ref[...] = total_ref[...].astype(BF16).reshape(blocks, places, width)


def run_experts(pooled, weights):
    blocks, places, width = pooled.shape
    steps, _, _, tile = weights.shape
    count = blocks * places
    return pl.pallas_call(
        functools.partial(expert_kernel, steps),
        grid=(steps,),
        in_specs=[constant_spec(pooled.shape), pl.BlockSpec((1, 2, width, tile), lambda i: (i, 0, 0, 0))],
        out_specs=[
            constant_spec(pooled.shape),
            pl.BlockSpec((1, count, tile), lambda i: (i, 0, 0)),
            pl.BlockSpec((1, count, tile), lambda i: (i, 0, 0)),
        ],
        out_shape=[
            jax.ShapeDtypeStruct(pooled.shape, BF16),
            jax.ShapeDtypeStruct((steps, count, tile), BF16),
            jax.ShapeDtypeStruct((steps, count, tile), F32),
        ],
        scratch_shapes=[pltpu.VMEM((count, width), F32)],
        compiler_params=pltpu.CompilerParams(vmem_limit_bytes=40 << 20),
        cost_estimate=pl.CostEstimate(
            flops=count * width * tile * steps * 8, bytes_accessed=width * tile * steps * 8, transcendentals=0
        ),
        name="experts",
    )(pooled, weights)


def expert_back_kernel(steps, slots_ref, pooled_ref, grads_ref, result_ref, act_ref, slope_ref, weights_ref, back_ref, grad_ref, total_ref):
    step = pl.program_id(0)
    blocks, places, width = pooled_ref.shape
    count = blocks * places
    pooled = pooled_ref[...].reshape(count, width)
    grads = grads_ref[...].reshape(count, width)
    act = act_ref[0]
    grad_pre = (dot(grads, weights_ref[0, 1]) * slope_ref[0]).astype(BF16)
    grad_ref[0, 0] = dot_tn(pooled, grad_pre).astype(BF16)
    grad_ref[0, 1] = dot_tn(grads, act).astype(BF16)
    part = dot_nt(grad_pre, weights_ref[0, 0])

    @pl.when(step == 0)
    def _():
        total_ref[...] = part

    @pl.when(step > 0)
    def _():
        total_ref[...] += part

    @pl.when(step == steps - 1)
    def _():
        grad_pooled = total_ref[...].astype(BF16)
        back_ref[:, :places] = grad_pooled.reshape(blocks, places, width)
        result = result_ref[...].reshape(count, width)
        product = result.astype(F32) * grads.astype(F32) + grad_pooled.astype(F32) * pooled.astype(F32)
        high = product.astype(BF16)
        rest = (product - high.astype(F32)).astype(BF16)
        ones = jnp.ones((16, width), BF16)
        sums = dot_nt(ones, high) + dot_nt(ones, rest)
        top = sums.astype(BF16)
        low = (sums - top.astype(F32)).astype(BF16)
        for b in range(blocks):
            here = slice(b * places, b * places + places)
            fill = jnp.zeros((16, width - 2 * places), BF16)
            back_ref[b, places:] = jnp.concatenate([top[:, here], low[:, here], fill], axis=1)


def pull_experts(slots, pooled, grads, result, act, slope, weights):
    blocks, places, width = pooled.shape
    steps, _, _, tile = weights.shape
    count = blocks * places
    return pl.pallas_call(
        functools.partial(expert_back_kernel, steps),
        grid_spec=pltpu.PrefetchScalarGridSpec(
            num_scalar_prefetch=1,
            grid=(steps,),
            in_specs=[constant_spec(pooled.shape)] * 3
            + [pl.BlockSpec((1, count, tile), lambda i, slots: (i, 0, 0))] * 2
            + [pl.BlockSpec((1, 2, width, tile), lambda i, slots: (i, 0, 0, 0))],
            out_specs=[
                constant_spec((blocks, places + 16, width)),
                pl.BlockSpec((1, 2, width, tile), lambda i, slots: (slots[i], 0, 0, 0)),
            ],
            scratch_shapes=[pltpu.VMEM((count, width), F32)],
        ),
        out_shape=[
            jax.ShapeDtypeStruct((blocks, places + 16, width), BF16),
            jax.ShapeDtypeStruct(weights.shape, BF16),
        ],
        compiler_params=pltpu.CompilerParams(vmem_limit_bytes=40 << 20),
        cost_estimate=pl.CostEstimate(
            flops=count * width * tile * steps * 12, bytes_accessed=width * tile * steps * 8, transcendentals=0
        ),
        name="pull_experts",
    )(slots, pooled, grads, result, act, slope, weights)


def spread_kernel(group, count, slots_ref, gates_ref, grads_ref, hidden_ref, *rest):
    parts, (out_ref, change_ref, result_ref) = rest[:count], rest[-3:]
    for k in range(count):
        @pl.when(pl.program_id(0) == k)
        def _():
            result_ref[...] = parts[k][...]

    rows, places = grads_ref.shape[0], grads_ref.shape[1]
    experts = result_ref.shape[0]
    sub = 16
    columns = gates_ref.shape[1]

    def step(s, _):
        here = pl.ds(pl.multiple_of(s * sub, sub), sub)
        results = [result_ref[e, here, :].astype(F32) * group for e in range(experts)]
        gates = gates_ref[here, :].astype(BF16).astype(F32)
        lane = iota((sub, columns), 1)
        changes = jnp.zeros((sub, columns), F32)
        for r in range(rows):
            grads = grads_ref[r, here, :].astype(F32)
            for e in range(experts):
                both = jnp.sum(grads * results[e], axis=1, keepdims=True)
                changes = jnp.where(lane == r * experts + e, both, changes)
            total = sum(gates[:, r * experts + e: r * experts + e + 1] * results[e] for e in range(experts))
            out_ref[r, here, :] = (hidden_ref[r, here, :] + total.astype(BF16).astype(F32)).astype(BF16)
        change_ref[0, here, :] = changes
        return 0

    lax.fori_loop(0, places // sub, step, 0, unroll=8)


def slot_of(found):
    found = list(found)
    step = found[-1] - found[0]
    return lambda i, slots: slots[found[0] + i * step]


def spread_tokens(found, slots, gates, cotangent, hidden, group, held):
    rows, span, width = hidden.shape
    parts = list(found.values())
    experts, places, _ = parts[0].shape
    at = slot_of(found)
    block = pl.BlockSpec((rows, places, width), lambda i, slots: (0, at(i, slots), 0))
    columns = gates.shape[1]
    aliased = [] if held is None else [held]
    return pl.pallas_call(
        functools.partial(spread_kernel, group, len(parts)),
        grid_spec=pltpu.PrefetchScalarGridSpec(
            num_scalar_prefetch=1,
            grid=(len(parts),),
            in_specs=[pl.BlockSpec((places, columns), lambda i, slots: (at(i, slots), 0)), block, block]
            + [constant_spec(part.shape) for part in parts]
            + [pl.BlockSpec(memory_space=pltpu.HBM) for _ in aliased],
            out_specs=[block, pl.BlockSpec((1, places, columns), lambda i, slots: (i, 0, 0))],
            scratch_shapes=[pltpu.VMEM(parts[0].shape, BF16)],
        ),
        out_shape=[
            jax.ShapeDtypeStruct((rows, span, width), BF16),
            jax.ShapeDtypeStruct((len(parts), places, columns), F32),
        ],
        input_output_aliases={4 + len(parts): 0} if aliased else {},
        compiler_params=pltpu.CompilerParams(vmem_limit_bytes=58 << 20),
        cost_estimate=pl.CostEstimate(
            flops=len(parts) * rows * places * width * 5000, bytes_accessed=rows * places * width * 10, transcendentals=0
        ),
        name="spread",
    )(slots, gates, cotangent, hidden, *parts, *aliased)


def pull_kernel(first, count, slots_ref, gates_ref, change_ref, mixed_ref, hidden_ref, cotangent_ref, attended_ref, router_ref, gains_ref, weight_ref, *rest):
    parts, rest = rest[:count], rest[count:]
    out_ref, low_ref, router_grad_ref, project_ref, sums_ref, pooled_ref, logits_ref, grad_ref = rest[-8:]

    @pl.when(pl.program_id(0) == 0)
    def _():
        if first:
            router_grad_ref[...] = jnp.zeros_like(router_grad_ref)
            project_ref[...] = jnp.zeros_like(project_ref)
            sums_ref[...] = jnp.zeros_like(sums_ref)
        else:
            router_grad_ref[...] = rest[2][...]
            project_ref[...] = rest[3][...]
            sums_ref[...] = rest[4][...]

    for k in range(count):
        @pl.when(pl.program_id(0) == k)
        def _():
            pooled_ref[...] = parts[k][...]

    rows, places, width = mixed_ref.shape
    experts = pooled_ref.shape[0]
    sub = 16
    columns = gates_ref.shape[1]
    inner = jnp.zeros((places, columns), F32)
    for e in range(experts):
        pick = (iota((16, columns), 0) == 0) & (iota((16, columns), 1) % experts == e)
        pick = jnp.where(pick, 1.0, 0.0).astype(BF16)
        inner += dot_tn(pooled_ref[e, places:, :places], pick) + dot_tn(pooled_ref[e, places:, places: 2 * places], pick)

    def change(s, _):
        here = pl.ds(pl.multiple_of(s * sub, sub), sub)
        pooled = [pooled_ref[e, here, :].astype(F32) for e in range(experts)]
        lane = iota((sub, columns), 1)
        changes = jnp.zeros((sub, columns), F32)
        for r in range(rows):
            mixed = mixed_ref[r, here, :].astype(F32)
            for e in range(experts):
                both = jnp.sum(pooled[e] * mixed, axis=1, keepdims=True)
                changes = jnp.where(lane == r * experts + e, both, changes)
        logits_ref[here, :] = changes
        return 0

    lax.fori_loop(0, places // sub, change, 0, unroll=8)
    changes = (logits_ref[...] + change_ref[0]).astype(BF16).astype(F32)
    low = (gates_ref[...] * (changes - inner)).astype(BF16)
    for r in range(rows):
        grad_ref[r] = dot(low, router_ref[r])
        router_grad_ref[...] += dot_tn(low, mixed_ref[r])[r * experts: r * experts + experts]

    def spread(s, _):
        here = pl.ds(pl.multiple_of(s * sub, sub), sub)
        pooled = [pooled_ref[e, here, :].astype(F32) for e in range(experts)]
        gates = gates_ref[here, :].astype(BF16).astype(F32)
        for r in range(rows):
            grad_ref[r, here, :] = sum(
                (gates[:, r * experts + e: r * experts + e + 1] * pooled[e] for e in range(experts)),
                grad_ref[r, here, :],
            )
        return 0

    lax.fori_loop(0, places // sub, spread, 0, unroll=8)

    for r in range(rows):
        grads = grad_ref[r].astype(BF16).astype(F32)
        hat, inverse = normalise(hidden_ref[r])
        sums_ref[0:1] += jnp.sum(grads * hat, axis=0, keepdims=True)
        sums_ref[1:2] += jnp.sum(grads, axis=0, keepdims=True)
        total = cotangent_ref[r].astype(F32) + pull_norm(grads * gains_ref[2:3], hat, inverse)
        out_ref[r] = total
        total = total.astype(BF16)
        project_ref[...] += dot_tn(attended_ref[r], total)
        low_ref[r] = dot_nt(total, weight_ref[...]).astype(BF16)


def pull_slots(found, slots, gates, change, mixed, hidden, cotangent, attended, router, gains, packed, held, weight=20):
    rows, span, width = mixed.shape
    parts = list(found.values())
    experts, depth, _ = parts[0].shape
    places = span // slots.shape[0]
    at = slot_of(found)
    block = pl.BlockSpec((rows, places, width), lambda i, slots: (0, at(i, slots), 0))
    columns = gates.shape[1]
    sums = [(experts, width), (width, width), (8, width)]
    ins = [
        pl.BlockSpec((places, columns), lambda i, slots: (at(i, slots), 0)),
        pl.BlockSpec((1, places, columns), lambda i, slots: (i, 0, 0)),
        block,
        block,
        block,
        block,
        constant_spec(router.shape),
        constant_spec(gains.shape),
        constant_spec((width, width), 0, 3),
    ] + [constant_spec(part.shape) for part in parts]
    aliases = {}
    if held is not None:
        aliases = {len(ins) + 1: 0, len(ins) + 2: 1}
        ins += [pl.BlockSpec(memory_space=pltpu.HBM)] * 2 + [constant_spec(shape) for shape in sums]
    return pl.pallas_call(
        functools.partial(pull_kernel, held is None, len(parts)),
        grid_spec=pltpu.PrefetchScalarGridSpec(
            num_scalar_prefetch=1,
            grid=(len(parts),),
            in_specs=ins,
            out_specs=[block, block] + [constant_spec(shape) for shape in sums],
            scratch_shapes=[
                pltpu.VMEM(parts[0].shape, BF16),
                pltpu.VMEM((places, columns), F32),
                pltpu.VMEM((rows, places, width), F32),
            ],
        ),
        out_shape=[jax.ShapeDtypeStruct((rows, span, width), F32), jax.ShapeDtypeStruct((rows, span, width), BF16)]
        + [jax.ShapeDtypeStruct(shape, F32) for shape in sums],
        input_output_aliases=aliases,
        compiler_params=pltpu.CompilerParams(vmem_limit_bytes=58 << 20),
        cost_estimate=pl.CostEstimate(
            flops=len(parts) * rows * places * width * width * weight,
            bytes_accessed=rows * places * weight,
            transcendentals=0,
        ),
        name="pull_slots",
    )(slots, gates, change, mixed, hidden, cotangent, attended, router, gains, packed, *parts, *(held or ()))


def project_kernel(experts, grads_ref, tokens_ref, gains_ref, weight_ref, project_ref, late_ref, out_ref, product_ref, sums_ref):
    width, wide = product_ref.shape
    steps = pl.num_programs(0) * pl.num_programs(1)
    step = pl.program_id(0) * pl.num_programs(1) + pl.program_id(1)

    @pl.when(step == 0)
    def _():
        product_ref[...] = jnp.zeros_like(product_ref)
        sums_ref[...] = jnp.zeros_like(sums_ref)

    hat = normalise(tokens_ref[0].astype(F32))[0].astype(BF16)
    ones = jnp.ones((hat.shape[0], 8), BF16)
    product_ref[...] += dot_tn(hat, grads_ref[0])
    sums_ref[...] += dot_tn(ones, grads_ref[0])

    @pl.when(step == steps - 1)
    def _():
        sums = sums_ref[0:1, :]
        for at in range(0, width, 64):
            here = slice(at, at + 64)
            product = product_ref[here, :]
            weights = weight_ref[here, :].astype(F32)
            out_ref[here, :wide] = (gains_ref[here, 0:1] * product + gains_ref[here, 1:2] * sums).astype(BF16)
            out_ref[here, wide: wide + width] = project_ref[here, :].astype(BF16)
            late = late_ref[here, :]
            lane = iota(late.shape, 1)
            late = jnp.where(lane == experts, jnp.sum(weights * product, axis=1, keepdims=True), late)
            late = jnp.where(lane == experts + 1, jnp.sum(weights * sums, axis=1, keepdims=True), late)
            out_ref[here, wide + width:] = late.astype(BF16)


def project_grads(grads, tokens, gains, packed, project, late, experts, tile=1024):
    rows, length, width = tokens.shape
    wide = 3 * width
    return pl.pallas_call(
        functools.partial(project_kernel, experts),
        grid=(rows, length // tile),
        in_specs=[
            pl.BlockSpec((1, tile, wide), lambda r, t: (r, t, 0)),
            pl.BlockSpec((1, tile, width), lambda r, t: (r, t, 0)),
            constant_spec(gains.shape),
            constant_spec((width, wide)),
            constant_spec(project.shape),
            constant_spec(late.shape),
        ],
        out_specs=constant_spec(packed.shape),
        out_shape=jax.ShapeDtypeStruct(packed.shape, BF16),
        scratch_shapes=[pltpu.VMEM((width, wide), F32), pltpu.VMEM((8, wide), F32)],
        compiler_params=pltpu.CompilerParams(vmem_limit_bytes=48 << 20),
        cost_estimate=pl.CostEstimate(flops=rows, bytes_accessed=rows, transcendentals=0),
        name="project_grads",
    )(grads, tokens, gains, packed, project, late)


def tokens_kernel(grads_ref, tokens_ref, hidden_ref, gains_ref, weight_ref, *rest):
    out_ref = rest[-1]
    for at in pieces(tokens_ref.shape[1]):
        hat, inverse = normalise(tokens_ref[0, at].astype(F32))
        grads = dot_nt(grads_ref[0, at], weight_ref[...])
        out_ref[0, at] = hidden_ref[0, at] + pull_norm(grads * gains_ref[0:1], hat, inverse)


def pull_tokens(grads, tokens, hidden, gains, packed, row_from, row_to, held=None, tile=1024):
    rows, length, width = tokens.shape
    block = pl.BlockSpec((1, tile, width), lambda r, t: (r + row_from, t, 0))
    aliased = [] if held is None else [held]
    return pl.pallas_call(
        tokens_kernel,
        grid=(row_to - row_from, length // tile),
        in_specs=[
            pl.BlockSpec((1, tile, 3 * width), lambda r, t: (r + row_from, t, 0)),
            block,
            block,
            constant_spec(gains.shape),
            constant_spec((width, 3 * width)),
        ]
        + [pl.BlockSpec(memory_space=pltpu.HBM) for _ in aliased],
        out_specs=block,
        out_shape=jax.ShapeDtypeStruct((rows, length, width), F32),
        input_output_aliases={5: 0} if aliased else {},
        compiler_params=pltpu.CompilerParams(vmem_limit_bytes=58 << 20),
        cost_estimate=pl.CostEstimate(
            flops=(row_to - row_from) * length * width * width * 20,
            bytes_accessed=(row_to - row_from) * length * width * 16,
            transcendentals=0,
        ),
        name="pull_tokens",
    )(grads, tokens, hidden, gains, packed, *aliased)


def ring_order(size):
    inner = 2 if size % 2 == 0 and size > 2 else 1
    outer = size // inner
    up = [z * inner for z in range(outer)]
    if inner == 1:
        return up
    return up + [z * inner + 1 for z in reversed(range(outer))]


def shift(value, order, step):
    count = len(order)
    return lax.ppermute(value, "dp", [(order[i], order[(i + step) % count]) for i in range(count)])


def flip(value, bit, axis="fsdp"):
    count = lax.axis_size(axis)
    return lax.ppermute(value, axis, [(i, i ^ bit) for i in range(count)])


def turn(value, step, axis="dp"):
    count = lax.axis_size(axis)
    return lax.ppermute(value, axis, [(i, (i + step) % count) for i in range(count)])


def take(values, index):
    starts = (index,) + (jnp.uint32(0),) * (values.ndim - 1)
    return lax.dynamic_slice(values, starts, (1,) + values.shape[1:])[0]


def put(values, value, index):
    return lax.dynamic_update_slice(values, value[None], (index,) + (jnp.uint32(0),) * value.ndim)


def add(a, b):
    return (a.astype(F32) + b.astype(F32)).astype(BF16)


def together(*values):
    return lax.optimization_barrier(values)


class Ring:
    def __init__(self, value, order):
        self.order, self.done = order, 0
        self.ahead = self.behind = value

    def left(self):
        return self.done < len(self.order) // 2

    def after(self, *values):
        self.ahead, self.behind, *_ = together(self.ahead, self.behind, *values)

    def step(self, *beside):
        count = len(self.order)
        self.done += 1
        slot = count - self.done
        ahead, behind = self.ahead, self.behind
        middle = 2 * self.done == count and ahead.shape[0] % 2 == 0
        if middle:
            half = ahead.shape[0] // 2
            ahead, behind = ahead[:half], behind[half:]
        ahead = shift(ahead, self.order, 1)
        if 2 * self.done < count or middle:
            behind = shift(behind, self.order, -1)
        ahead, behind, *beside = together(ahead, behind, *beside)
        self.ahead, self.behind = ahead, behind
        if middle:
            return {slot: jnp.concatenate([ahead, behind], axis=0)}, beside
        return {slot: ahead, self.done: behind} if 2 * self.done < count else {slot: ahead}, beside


def gather_all(value, steps, *beside):
    pair = pair_of(lax.axis_size("dp"))
    lines = lax.axis_size("dp") // pair
    size = lax.axis_size("fsdp")
    here = lax.axis_index("fsdp")

    def both(value, bit, axis, index):
        other = flip(value, bit, axis)
        upper = (index & bit) != 0
        return jnp.stack([jnp.where(upper, other, value), jnp.where(upper, value, other)])

    whole = put(jnp.zeros((lines,) + value.shape, value.dtype), value, steps[0])
    for k in range(1, lines):
        whole = put(whole, turn(value, -k * pair), steps[k])
    if beside:
        whole, *beside = together(whole, *beside)
    whole = both(whole, 1, "dp", lax.axis_index("dp")) if pair == 2 else whole[None]
    whole = jnp.moveaxis(whole, 0, 1)
    whole = whole.reshape((lines * pair, 1) + value.shape)
    bit = size // 2
    while bit:
        whole = both(whole, bit, "fsdp", here)
        whole = jnp.moveaxis(whole, 0, 2)
        whole = whole.reshape((lines * pair, -1) + value.shape)
        bit //= 2
    return whole, beside


def scatter_all(values, steps, work):
    owners, size = lax.axis_size("dp"), lax.axis_size("fsdp")
    bits = size.bit_length() - 1
    here = lax.axis_index("fsdp")
    width = values.shape[1]
    pair = pair_of(owners)
    work = list(work)

    def half(held, axis, upper, bit, name):
        low, high = (lax.index_in_dim(held, i, axis, keepdims=False) for i in (0, 1))
        came = flip(jnp.where(upper, low, high), bit, name)
        if work:
            came, = work.pop(0)(came)
        return add(jnp.where(upper, high, low), came)

    held = values.reshape((owners // pair, pair) + (2,) * bits + (-1, width))
    for level in range(bits):
        held = half(held, bits + 1 - level, ((here >> level) & 1) != 0, 1 << level, "fsdp")
    held = half(held, 1, (lax.axis_index("dp") & 1) != 0, 1, "dp") if pair == 2 else held[:, 0]
    came = [turn(take(held, steps[k]), k * pair) for k in range(1, owners // pair)]
    while work:
        came = work.pop(0)(*came)
    return sum((value.astype(F32) for value in came), take(held, steps[0]).astype(F32))


def pair_of(owners):
    return 2 if owners % 2 == 0 else 1


def exchange(values):
    return jnp.stack([values[0]] + [flip(values[k], k) for k in range(1, values.shape[0])])


def per_device(
    tokens,
    segment_ids,
    pad_tokens,
    cotangent,
    project_in,
    project_out,
    router_weight,
    expert_in,
    expert_out,
    first_gain,
    first_bias,
    second_gain,
    second_bias,
):
    blocks_here, rows, length, width = tokens.shape
    tokens = tokens.reshape(rows, length, width)
    cotangent = cotangent.reshape(rows, length, width)
    segments = segment_ids.reshape(rows, length)
    group = pad_tokens.shape[1]
    owners = lax.axis_size("dp")
    experts = router_weight.shape[1]
    order = ring_order(owners)
    data_index = lax.axis_index("dp")
    expert_index = lax.axis_index("fsdp")
    places = length // owners

    pair = pair_of(owners)
    lines = owners // pair
    ring = np.array([[order[(order.index(d) + k) % owners] for k in range(owners)] for d in range(owners)], np.int32)
    place = np.array(
        [[(o % pair ^ d % pair) * lines + (o // pair - d // pair) % lines for o in ring[d]] for d in range(owners)],
        np.int32,
    )
    line = np.array([[(d // pair + k) % lines for k in range(lines)] for d in range(owners)], np.int32)
    tables = np.concatenate([ring, place, line], axis=1)
    tables = lax.dynamic_slice(
        jnp.asarray(tables), (data_index.astype(jnp.uint32), jnp.uint32(0)), (1, tables.shape[1])
    )[0]
    slots, shares = tables[:owners], tables[owners: 2 * owners]
    spots = [tables[k].astype(jnp.uint32) for k in range(owners)]
    steps = [tables[2 * owners + k].astype(jnp.uint32) for k in range(lines)]

    vectors = jnp.stack([first_gain, first_bias, second_gain, second_bias], axis=1)
    small = jnp.concatenate([router_weight, vectors], axis=1)
    small = jnp.pad(small, ((0, 0), (0, 128 - small.shape[1])))
    packed = jnp.concatenate([project_in, project_out, small], axis=1)
    packed, (expert_in, expert_out) = gather_all(packed, steps, expert_in, expert_out)
    weights = jnp.stack([expert_in[0], expert_out[0].T])
    packed = packed.reshape(width, packed.shape[-1])
    packed, weights = together(packed, weights)
    kept = {0: weights}
    weights = Ring(weights, order)
    small = packed[:, 4 * width:].T
    mine = (jnp.arange(experts)[:, None] ^ jnp.arange(experts)[None, :]) == expert_index
    router = jnp.sum(jnp.where(mine[:, :, None], small[None, :experts], 0), axis=1).astype(BF16)
    spread_router = jnp.stack(
        [jnp.pad(router, ((r * experts, (rows - 1 - r) * experts), (0, 0))) for r in range(rows)]
    )
    gains = jnp.pad(small[experts: experts + 4].astype(F32), ((0, 4), (0, 0)))

    own_pads = lax.dynamic_slice_in_dim(pad_tokens[0], data_index * rows, rows, 0)
    vlens = (length - own_pads).astype(jnp.int32)
    starts = jnp.zeros_like(segments)
    for doc in range(1, 4):
        before = jnp.sum((segments < doc).astype(jnp.int32), axis=1, keepdims=True)
        starts = jnp.where(segments == doc, before, starts)
    starts = starts.reshape(rows, length // QB, QB)
    lows = starts[:, :, 0] // QB

    def meanwhile(value):
        if not weights.left():
            return value
        found, (value,) = weights.step(value)
        kept.update(found)
        return value

    joined = meanwhile(join_tokens(tokens, gains, packed))
    attended, logs = attn_fwd(joined, starts, lows, vlens, 1)
    attended = meanwhile(attended)
    hidden, mixed, logits = mix_tokens(
        attended, tokens, gains, packed, jnp.pad(router, ((0, 16 - experts), (0, 0))), 0
    )
    logits = meanwhile(logits)[:, :experts]
    valid = (jnp.arange(length)[None, :] < vlens[:, None])[:, None, :]
    highest = jnp.max(jnp.where(valid, logits, NEGATIVE), axis=0)
    total = jnp.sum(jnp.where(valid, jnp.exp(logits - highest), 0.0), axis=0)
    stats = jnp.stack([highest, total])[None]
    if pair == 2:
        stats = jnp.concatenate([stats, flip(stats, 1, "dp")])
    stats = jnp.concatenate([stats] + [turn(stats, k * pair) for k in range(1, lines)])
    tops = jnp.max(stats[:, 0], axis=0)
    total = jnp.sum(stats[:, 1] * jnp.exp(stats[:, 0] - tops), axis=0)
    gates = jnp.where(valid, jnp.exp(jnp.where(valid, logits - tops, NEGATIVE)) / total, 0.0)
    gates = gates.reshape(rows * experts, length).T
    pooled = meanwhile(pool_tokens(slots, gates, mixed, experts, 1.0))
    while weights.left():
        kept.update(weights.step()[0])
    weights = jnp.stack([kept[k] for k in range(owners)])
    grads = pool_tokens(slots, gates, cotangent, experts, float(group))

    half = experts // 2
    first = [(pooled[:, :half], 1), (pooled[:, half:], -1)]
    second = [(grads[:, :half], 1), (grads[:, half:], -1)]
    held = [part[-way % owners] for part, way in first]
    later = [part[-way % owners] for part, way in second]
    for step in range(owners - 1):
        came = [shift(value, order, way) for value, (_, way) in zip(held, first)]
        if step == 0:
            *came, one, two = together(*came, *later)
            later = [one, two]
        held = [add(value, part[-way * (2 + step) % owners]) for value, (part, way) in zip(came, first)]
        came = [shift(value, order, way) for value, (_, way) in zip(later, second)]
        later = [add(value, part[-way * (2 + step) % owners]) for value, (part, way) in zip(came, second)]
    pooled = exchange(jnp.concatenate(held, axis=0))
    result, act, slope = run_experts(pooled, weights)
    grads = exchange(jnp.concatenate(later, axis=0))
    grad_pooled, grad_weights = pull_experts(shares, pooled, grads, result, act, slope, weights)

    result = exchange(result)
    back = exchange(grad_pooled)

    def pull(found, change, out, *weight):
        return pull_slots(
            found, slots, gates, change, mixed, hidden, cotangent, attended, spread_router, gains, packed, out, *weight
        )

    def spread(found, out):
        return spread_tokens(found, slots, gates, cotangent, hidden, group, out)

    turns = owners // 2
    first, second = Ring(result, order), Ring(back, order)
    found, (grad_weights,) = first.step(grad_weights)
    groups, arrived = [{0: result}, found], [{0: back}]
    out, pulled, changes = None, None, []
    for step in range(turns + 1):
        work = []
        for k in [step] if step < turns - 1 else [turns - 1, turns] if step == turns - 1 else []:
            out, change = spread(groups[k], out)
            changes.append(change)
            work = [out]
        if 0 < step < turns - 1 or step == turns:
            k = step - 1 if step < turns else turns - 2
            pulled = pull(arrived[k], changes[k], pulled)
            work += pulled
        if step > 0:
            if step == 1:
                second.after(*groups[2].values())
        if first.left():
            found, _ = first.step()
            groups.append(found)
        if second.left() and step > 0:
            found, work = second.step(*work)
            arrived.append(found)
        if step < turns:
            out, *work = work
        pulled = work or pulled
    pulled = pull(arrived[turns - 1], changes[turns - 1], pulled)
    layer_out = out
    grad_weights, *_ = together(grad_weights, *arrived[turns].values())
    if pair == 2:
        came = flip(grad_weights[lines:], 1, "dp")
    pulled = pull(arrived[turns], changes[turns], pulled, 0)
    grad_hidden, grad_attended, router_grad, grad_proj_out, sums_two = pulled
    split = rows - max(1, rows // 2)
    grads = attn_bwd(joined, grad_attended, attended, logs, starts, lows, vlens, 0, split)
    grad_weights = grad_weights[:lines]
    if pair == 2:
        came, grads = together(came, grads)
        grad_weights = add(grad_weights, came)
    grad_parts = [turn(grad_weights[k], k * pair) for k in range(1, lines)]
    grads = attn_bwd(joined, grad_attended, attended, logs, starts, lows, vlens, split, rows, grads)
    router_grad = jnp.sum(jnp.where(mine[:, :, None], router_grad[None], 0.0), axis=1)
    late = jnp.concatenate([router_grad, jnp.zeros((2, width), F32), sums_two[:2]], axis=0).T
    late = jnp.pad(late, ((0, 0), (0, 128 - late.shape[1])))
    reduced = project_grads(grads, tokens, gains.T, packed, grad_proj_out, late, experts)
    reduced, *grad_parts = together(reduced, *grad_parts)
    made = []

    def tokens_beside(*came):
        *came, grad = together(*came, pull_tokens(grads, tokens, grad_hidden, gains, packed, 0, rows))
        made.append(grad)
        return came

    def weights_beside(*came):
        value, *parts = together(*came, *grad_parts)
        made.append(sum((part.astype(F32) for part in parts), grad_weights[0].astype(F32)))
        return [value]

    reduced = scatter_all(reduced, steps, [lambda *came: came, tokens_beside, weights_beside])
    tokens_grad, grad_weights = made
    late = reduced[:, 4 * width:]
    return (
        layer_out[None],
        tokens_grad[None],
        reduced[:, : 3 * width],
        reduced[:, 3 * width: 4 * width],
        late[:, :experts],
        grad_weights[0][None],
        grad_weights[1].T[None],
        late[:, experts],
        late[:, experts + 1],
        late[:, experts + 2],
        late[:, experts + 3],
    )


def solution(mesh):
    in_specs = (
        P("fsdp", "dp", None, None),
        P("fsdp", "dp", None),
        P("fsdp", None),
        P("fsdp", "dp", None, None),
        P(("dp", "fsdp"), None),
        P(("dp", "fsdp"), None),
        P(("dp", "fsdp"), None),
        P("fsdp", None, "dp"),
        P("fsdp", "dp", None),
        P(("dp", "fsdp")),
        P(("dp", "fsdp")),
        P(("dp", "fsdp")),
        P(("dp", "fsdp")),
    )
    out_specs = (
        P("fsdp", "dp", None, None),
        P("fsdp", "dp", None, None),
        P(("dp", "fsdp"), None),
        P(("dp", "fsdp"), None),
        P(("dp", "fsdp"), None),
        P("fsdp", None, "dp"),
        P("fsdp", "dp", None),
        P(("dp", "fsdp")),
        P(("dp", "fsdp")),
        P(("dp", "fsdp")),
        P(("dp", "fsdp")),
    )
    return jax.shard_map(
        per_device, mesh=mesh, in_specs=in_specs, out_specs=out_specs, check_vma=False
    )
```
